32 devices in a mesh: dp: 4 (over z), mp: 8 (over y, x, core).
Axes of the slice: x: 2, y: 2, z: 4, core: 2. Of those that a mesh axis runs over, the one named last changes fastest.
Arguments:
- tokens: bfloat16 [4096, 8, 768], P('mp', 'dp'), may hold values from -6 to 6
- upstream: bfloat16 [4096, 8, 768], P('mp', 'dp'), may hold values from -6 to 6
- pieces: int32 [8], P('dp'), may hold values from 1 to 4, as said below
- layer_index: int32 [1], replicated, may hold values from 1 to 11
- mix_gain: float32 [768], replicated, may hold values from 0.5 to 1.5
- w_input: bfloat16 [768, 2, 384], P(None, None, 'mp'), may hold values from -0.21875 to 0.21875
- w_forget: bfloat16 [768, 384], P(None, 'mp'), may hold values from -0.21875 to 0.21875
- w_outgate: bfloat16 [768, 2, 384], P(None, None, 'mp'), may hold values from -0.21875 to 0.21875
- phase_angle: float32 [384], P('mp'), may hold values from -3.140625 to 3.140625
- lower_logits: float32 [12, 384], P(None, 'mp'), may hold values from -6 to 6
- out_gain: float32 [2, 384], P(None, 'mp'), may hold values from 0.5 to 1.5
- w_output: bfloat16 [2, 384, 768], P(None, 'mp'), may hold values from -0.21875 to 0.21875
- ffn_gain: float32 [768], replicated, may hold values from 0.5 to 1.5
- w_gate: bfloat16 [768, 1536], P(None, 'mp'), may hold values from -0.21875 to 0.21875
- w_up: bfloat16 [768, 1536], P(None, 'mp'), may hold values from -0.21875 to 0.21875
- w_down: bfloat16 [1536, 768], P('mp'), may hold values from -0.15625 to 0.15625
Outputs:
- result: bfloat16 [4096, 8, 768], P('mp', 'dp')
- grad_tokens: bfloat16 [4096, 8, 768], P('mp', 'dp')
- grad_mix_gain: float32 [768], replicated
- grad_w_input: float32 [768, 2, 384], P(None, None, 'mp')
- grad_w_forget: float32 [768, 384], P(None, 'mp')
- grad_w_outgate: float32 [768, 2, 384], P(None, None, 'mp')
- grad_phase: float32 [384], P('mp')
- grad_lower: float32 [12, 384], P(None, 'mp')
- grad_out_gain: float32 [2, 384], P(None, 'mp')
- grad_w_output: float32 [2, 384, 768], P(None, 'mp')
- grad_ffn_gain: float32 [768], replicated
- grad_w_gate: float32 [768, 1536], P(None, 'mp')
- grad_w_up: float32 [768, 1536], P(None, 'mp')
- grad_w_down: float32 [1536, 768], P('mp')
The draws below stay inside these ranges and needn't reach their ends.
Inputs may be any that keep to these rules, and one draw needn't show every extreme that they name: `pieces`: each group of 4096 positions is one sequence (value 1) or four sequences of 1024 positions (value 4); the 2 groups of each dp index hold a group of value 1, and some group has value 4.
All inputs are finite; a program needn't handle non-finite values.
Results may differ from the reference program's by a relative error of at most 0.014.
Values may be sent and summed in bfloat16 or wider, within the bound.
No kernel may reach another device: no remote copies, remote signals or barrier semaphores. Data moves between devices by JAX's collectives and lax.ppermute only.
A program may use at most 320 MiB of HBM per device.

```python
import jax
import jax.numpy as jnp
from jax import lax

D = 768
C = 384
F = 1536
LAYERS = 12
SLEN = 4096
STREAMS_DP = 2
STREAMS = 8


def draw_pieces(key, part):
    key = jax.random.fold_in(key, 11)
    key_kind, key_one, key_four = jax.random.split(key, 3)
    blocks = STREAMS // STREAMS_DP
    kind_bits = jax.random.randint(key_kind, (STREAMS,), 0, 2)
    values = jnp.where(kind_bits == 0, 1, 4).astype(jnp.int32)
    four_at = jax.random.randint(key_four, (), 0, STREAMS)
    values = values.at[four_at].set(4)
    offsets = jax.random.randint(key_one, (blocks,), 0, STREAMS_DP - 1)
    one_at = jnp.arange(blocks, dtype=jnp.int32) * STREAMS_DP + (four_at % STREAMS_DP + 1 + offsets) % STREAMS_DP
    values = values.at[one_at].set(1)
    return values


def steps_of(stream_key, extent, cuts, low, largest):
    level, own = 1.0, jax.random.fold_in(stream_key, 6)
    for position, blocks in cuts:
        draws = jnp.exp(jax.random.uniform(jax.random.fold_in(own, position), (blocks,), jnp.float32, low / len(cuts), largest / len(cuts)))
        level = level * jnp.repeat(draws, extent[position] // blocks).reshape([-1 if axis == position else 1 for axis in range(len(extent))])
    return level


def gaussian(rng, extent, deviation, bound, shards=(), held_as=jnp.bfloat16):
    drawn = jax.random.normal(rng, extent, jnp.float32) * deviation
    if len(shards) > 0:
        drawn = steps_of(rng, extent, shards, -0.22, 0.18) * drawn
    return jnp.clip(drawn, min=-bound, max=bound).astype(held_as)


def setup_inputs(seed: int = 0) -> dict:
    splits = jax.random.split(jax.random.key(seed), 17)
    return {
        "tokens": gaussian(splits[0], (SLEN, STREAMS, D), 1.0, 6.0, ((0, 8), (1, 4))),
        "upstream": gaussian(splits[1], (SLEN, STREAMS, D), 1.0, 6.0, ((0, 8), (1, 4))),
        "pieces": draw_pieces(jax.random.fold_in(splits[16], 71), 0),
        "layer_index": jax.random.randint(splits[3], (1,), 1, LAYERS).astype(jnp.int32),
        "mix_gain": jnp.clip(1.0 + 0.1 * jax.random.normal(splits[4], (D,), jnp.float32), 0.5, 1.5),
        "w_input": gaussian(splits[5], (D, 2, C), D ** -0.5, 0.21875, ((2, 8),)),
        "w_forget": gaussian(splits[6], (D, C), D ** -0.5, 0.21875, ((1, 8),)),
        "w_outgate": gaussian(splits[7], (D, 2, C), D ** -0.5, 0.21875, ((2, 8),)),
        "phase_angle": jnp.clip(jax.random.uniform(splits[8], (C,), jnp.float32, -3.140625, 3.140625), -3.140625, 3.140625),
        "lower_logits": gaussian(splits[9], (LAYERS, C), 1.5, 6.0, ((1, 8),), jnp.float32),
        "out_gain": jnp.clip(1.0 + 0.1 * jax.random.normal(splits[10], (2, C), jnp.float32), 0.5, 1.5),
        "w_output": gaussian(splits[11], (2, C, D), (2 * C) ** -0.5, 0.21875, ((1, 8),)),
        "ffn_gain": jnp.clip(1.0 + 0.1 * jax.random.normal(splits[12], (D,), jnp.float32), 0.5, 1.5),
        "w_gate": gaussian(splits[13], (D, F), D ** -0.5, 0.21875, ((1, 8),)),
        "w_up": gaussian(splits[14], (D, F), D ** -0.5, 0.21875, ((1, 8),)),
        "w_down": gaussian(splits[15], (F, D), F ** -0.5, 0.15625, ((0, 8),)),
    }


EPSILON = 1e-06

@jax.custom_vjp
def low(v):
    return lax.optimization_barrier(v.astype(jnp.bfloat16)).astype(jnp.float32)

@jax.custom_vjp
def low_back(v):
    return v

def low_keep(v):
    return (low(v), None)

def low_pass(kept, grad):
    return (grad,)

def back_keep(v):
    return (v, None)

def back_low(kept, grad):
    return (low(grad),)
low.defvjp(low_keep, low_pass)
low_back.defvjp(back_keep, back_low)

def rms_scale(values, gain):
    return values * lax.rsqrt(lax.optimization_barrier(jnp.mean(values * values, axis=-1, keepdims=True)) + EPSILON) * gain

def combine(first_pair, second_pair):
    ar_one, ai_one, br_one, bi_one = first_pair
    ar_two, ai_two, br_two, bi_two = second_pair
    return (ar_two * ar_one - ai_two * ai_one, ar_two * ai_one + ai_two * ar_one, ar_two * br_one - ai_two * bi_one + br_two, ar_two * bi_one + ai_two * br_one + bi_two)

def recurrence(in_pre, forget_pre, lower_bound, phase_rows, keep_mask):
    decay = lower_bound + (1.0 - lower_bound) * jax.nn.sigmoid(forget_pre)
    activated = jax.nn.silu(in_pre)
    kept_decay = keep_mask[:, None] * decay
    scanned = lax.associative_scan(combine, (kept_decay * jnp.cos(phase_rows), kept_decay * jnp.sin(phase_rows), (1.0 - decay) * activated[:, 0], (1.0 - decay) * activated[:, 1]), axis=0)
    return jnp.stack([scanned[2], scanned[3]], axis=1)

def layer_block(tokens, mix_gain, w_input, w_forget, w_outgate, phase_angle, lower_logits, out_gain, w_output, ffn_gain, w_gate, w_up, w_down, keep_mask, layer_mask):
    highest = lax.Precision.HIGHEST
    normed = low(rms_scale(tokens, mix_gain))
    in_pre = low_back(jnp.einsum('td,dkc->tkc', normed, w_input, precision=highest))
    forget_pre = low_back(jnp.dot(normed, w_forget, precision=highest, preferred_element_type=jnp.float32))
    outgate_pre = low_back(jnp.einsum('td,dkc->tkc', normed, w_outgate, precision=highest))
    lower_bound = lax.optimization_barrier(jnp.sum(jax.nn.softmax(lower_logits, axis=0) * layer_mask[:, None], axis=0))
    states = recurrence(in_pre, forget_pre, lower_bound, phase_angle, keep_mask)
    mean_square = low_back(lax.optimization_barrier(jnp.mean(states * states, axis=(1, 2))))
    gated = low(states * out_gain * jax.nn.silu(outgate_pre))
    mix_out = low_back(jnp.einsum('tkc,kcd->td', gated, w_output, precision=highest))
    mid_stream = tokens + lax.rsqrt(mean_square + EPSILON)[:, None] * mix_out
    ffn_normed = low(rms_scale(mid_stream, ffn_gain))
    gate_pre = low_back(jnp.dot(ffn_normed, w_gate, precision=highest, preferred_element_type=jnp.float32))
    up_pre = low_back(jnp.dot(ffn_normed, w_up, precision=highest, preferred_element_type=jnp.float32))
    hidden = low(jax.nn.silu(gate_pre) * up_pre)
    return mid_stream + jnp.dot(hidden, w_down, precision=highest, preferred_element_type=jnp.float32)

def reference(tokens, upstream, pieces, layer_index, mix_gain, w_input, w_forget, w_outgate, phase_angle, lower_logits, out_gain, w_output, ffn_gain, w_gate, w_up, w_down):
    layer_mask = (jnp.arange(LAYERS, dtype=jnp.int32) < layer_index[0]).astype(jnp.float32)
    weights = (mix_gain.astype(jnp.float32), w_input.astype(jnp.float32), w_forget.astype(jnp.float32), w_outgate.astype(jnp.float32), phase_angle.astype(jnp.float32), lower_logits.astype(jnp.float32), out_gain.astype(jnp.float32), w_output.astype(jnp.float32), ffn_gain.astype(jnp.float32), w_gate.astype(jnp.float32), w_up.astype(jnp.float32), w_down.astype(jnp.float32))
    positions = jnp.arange(SLEN, dtype=jnp.int32)

    def per_group(totals, group_item):
        group_tokens, group_upstream, group_pieces = group_item
        seq_span = SLEN // group_pieces
        keep_mask = (positions % seq_span != 0).astype(jnp.float32)

        def forward(inputs, *params):
            return layer_block(inputs, *params, keep_mask, layer_mask)
        outputs, pull_back = jax.vjp(forward, group_tokens.astype(jnp.float32), *weights)
        gradients = pull_back(group_upstream.astype(jnp.float32))
        totals = tuple((total + grad for total, grad in zip(totals, gradients[1:])))
        return (totals, (outputs.astype(jnp.bfloat16), gradients[0].astype(jnp.bfloat16)))
    zeros_init = tuple((jnp.zeros_like(weight) for weight in weights))
    sums, (outputs, grad_inputs) = lax.scan(per_group, zeros_init, (jnp.swapaxes(tokens, 0, 1), jnp.swapaxes(upstream, 0, 1), pieces))
    return (jnp.swapaxes(outputs, 0, 1), jnp.swapaxes(grad_inputs, 0, 1), sums[0], sums[1], sums[2], sums[3], sums[4], sums[5], sums[6], sums[7], sums[8], sums[9], sums[10], sums[11])
```

```python
import functools

import jax
import jax.numpy as jnp
from jax import lax
from jax.experimental import pallas as pl
from jax.experimental.pallas import tpu as pltpu
from jax.sharding import PartitionSpec as P

EPSILON = 1e-06
CHUNKS = 8
VMEM_BYTES = 48 * 1024 * 1024
F32 = jnp.float32
BF16 = jnp.bfloat16


def kernel_call(body, grid, in_specs, out_specs, out_shape, scratch=()):
    return pl.pallas_call(
        body,
        grid=grid,
        in_specs=in_specs,
        out_specs=out_specs,
        out_shape=out_shape,
        scratch_shapes=scratch,
        compiler_params=pltpu.CompilerParams(vmem_limit_bytes=VMEM_BYTES),
    )


def whole(shape):
    zeros = (0,) * len(shape)
    return pl.BlockSpec(shape, lambda *_: zeros)


def per_group(shape):
    zeros = (0,) * (len(shape) - 1)
    return pl.BlockSpec(shape, lambda g: (g,) + zeros)


SMEM_SPEC = pl.BlockSpec(memory_space=pltpu.SMEM)


def turn(cos, sin, re, im):
    return cos * re - sin * im, sin * re + cos * im


def back_turn(cos, sin, re, im):
    return cos * re + sin * im, cos * im - sin * re


def scan_local_body(steps, chans, pre, bound, angles, local, prods, decays, prefix, totals):
    low = bound[0:1, :]
    cos_one, sin_one = angles[0:1, :], angles[1:2, :]
    cos_chunk, sin_chunk = angles[2:3, :], angles[3:4, :]

    def step(j, carry):
        state_re, state_im, prod = carry
        rows = pl.ds(pl.multiple_of(j * CHUNKS, CHUNKS), CHUNKS)
        in_re = pre[rows, 0:chans]
        in_im = pre[rows, chans : 2 * chans]
        decay = low + (1.0 - low) * jax.nn.sigmoid(pre[rows, 2 * chans : 3 * chans])
        turned_re, turned_im = turn(cos_one, sin_one, state_re, state_im)
        state_re = decay * turned_re + (1.0 - decay) * (in_re * jax.nn.sigmoid(in_re))
        state_im = decay * turned_im + (1.0 - decay) * (in_im * jax.nn.sigmoid(in_im))
        prod = prod * decay
        local[rows, 0:chans] = state_re
        local[rows, chans : 2 * chans] = state_im
        prods[rows, :] = prod
        decays[rows, :] = decay
        return state_re, state_im, prod

    zeros = jnp.zeros((CHUNKS, chans), F32)
    end_re, end_im, prod = lax.fori_loop(0, steps, step, (zeros, zeros, zeros + 1.0), unroll=4)
    run, run_re, run_im = zeros[0:1] + 1.0, zeros[0:1], zeros[0:1]
    for s in range(CHUNKS):
        prefix[0, 0, s : s + 1, :] = run
        prefix[0, 1, s : s + 1, :] = run_re
        prefix[0, 2, s : s + 1, :] = run_im
        turned_re, turned_im = turn(cos_chunk, sin_chunk, run_re, run_im)
        run_re = prod[s : s + 1] * turned_re + end_re[s : s + 1]
        run_im = prod[s : s + 1] * turned_im + end_im[s : s + 1]
        run = run * prod[s : s + 1]
    totals[0] = zeros
    totals[0, 0:1, :] = run
    totals[0, 1:2, :] = run_re
    totals[0, 2:3, :] = run_im


def scan_local(pre, bound, angles, groups, chans):
    rows = pre.shape[0]
    per = rows // groups
    return kernel_call(
        functools.partial(scan_local_body, per // CHUNKS, chans),
        (groups,),
        [
            pl.BlockSpec((per, 3 * chans), lambda g: (g, 0)),
            whole((1, chans)),
            whole(angles.shape),
        ],
        [
            per_group((per, 2 * chans)),
            per_group((per, chans)),
            per_group((per, chans)),
            per_group((1, 3, CHUNKS, chans)),
            per_group((1, CHUNKS, chans)),
        ],
        [
            jax.ShapeDtypeStruct((rows, 2 * chans), F32),
            jax.ShapeDtypeStruct((rows, chans), F32),
            jax.ShapeDtypeStruct((rows, chans), F32),
            jax.ShapeDtypeStruct((groups, 3, CHUNKS, chans), F32),
            jax.ShapeDtypeStruct((groups, CHUNKS, chans), F32),
        ],
    )(pre, bound, angles)


def scan_finish_body(
    steps, chans, blocks, me, keep, gathered, local, prods, prefix, angles, table, states, entering
):
    g = pl.program_id(0)
    cos_dev, sin_dev = angles[4:5, :], angles[5:6, :]
    state_re = jnp.zeros((1, chans), F32)
    state_im = jnp.zeros((1, chans), F32)
    for d in range(blocks):
        kept = keep[g, d]
        turned_re, turned_im = turn(cos_dev, sin_dev, kept * state_re, kept * state_im)
        decay = gathered[d, 0, 0:1, :]
        earlier = d < me[0]
        state_re = jnp.where(earlier, decay * turned_re + gathered[d, 0, 1:2, :], state_re)
        state_im = jnp.where(earlier, decay * turned_im + gathered[d, 0, 2:3, :], state_im)
    kept = keep[g, me[0]]
    state_re, state_im = kept * state_re, kept * state_im
    cos_chunk, sin_chunk = angles[2:3, :], angles[3:4, :]
    for s in range(CHUNKS):
        run = prefix[0, 0, s : s + 1, :]
        entering[0, 0, s : s + 1, :] = run * state_re + prefix[0, 1, s : s + 1, :]
        entering[0, 1, s : s + 1, :] = run * state_im + prefix[0, 2, s : s + 1, :]
        state_re, state_im = turn(cos_chunk, sin_chunk, state_re, state_im)
    enter_re, enter_im = entering[0, 0], entering[0, 1]

    def step(j, carry):
        rows = pl.ds(pl.multiple_of(j * CHUNKS, CHUNKS), CHUNKS)
        prod = prods[rows, :]
        turned_re, turned_im = turn(
            table[pl.ds(j, 1), 0:chans], table[pl.ds(j, 1), chans : 2 * chans], enter_re, enter_im
        )
        states[rows, 0:chans] = local[rows, 0:chans] + prod * turned_re
        states[rows, chans : 2 * chans] = local[rows, chans : 2 * chans] + prod * turned_im
        return carry

    lax.fori_loop(0, steps, step, 0, unroll=4)


def scan_finish(me, keep, gathered, local, prods, prefix, angles, table, groups, chans):
    rows = prods.shape[0]
    per = rows // groups
    blocks = gathered.shape[0]
    return kernel_call(
        functools.partial(scan_finish_body, per // CHUNKS, chans, blocks),
        (groups,),
        [
            SMEM_SPEC,
            SMEM_SPEC,
            pl.BlockSpec((blocks, 1, CHUNKS, chans), lambda g: (0, g, 0, 0)),
            per_group((per, 2 * chans)),
            per_group((per, chans)),
            per_group((1, 3, CHUNKS, chans)),
            whole(angles.shape),
            whole(table.shape),
        ],
        [per_group((per, 2 * chans)), per_group((1, 2, CHUNKS, chans))],
        [
            jax.ShapeDtypeStruct((rows, 2 * chans), F32),
            jax.ShapeDtypeStruct((groups, 2, CHUNKS, chans), F32),
        ],
    )(me, keep, gathered, local, prods, prefix, angles, table)


def adjoint_local_body(steps, chans, d_states, decays, angles, local, prods, suffix, totals):
    cos_one, sin_one = angles[0:1, :], angles[1:2, :]
    cos_chunk, sin_chunk = angles[2:3, :], angles[3:4, :]

    def step(i, carry):
        flow_re, flow_im, prod = carry
        j = steps - 1 - i
        rows = pl.ds(pl.multiple_of(j * CHUNKS, CHUNKS), CHUNKS)
        grad_re = d_states[rows, 0:chans] + flow_re
        grad_im = d_states[rows, chans : 2 * chans] + flow_im
        local[rows, 0:chans] = grad_re
        local[rows, chans : 2 * chans] = grad_im
        prods[rows, :] = prod
        decay = decays[rows, :]
        turned_re, turned_im = back_turn(cos_one, sin_one, grad_re, grad_im)
        return decay * turned_re, decay * turned_im, prod * decay

    zeros = jnp.zeros((CHUNKS, chans), F32)
    end_re, end_im, prod = lax.fori_loop(0, steps, step, (zeros, zeros, zeros + 1.0), unroll=4)
    run, run_re, run_im = zeros[0:1] + 1.0, zeros[0:1], zeros[0:1]
    for s in reversed(range(CHUNKS)):
        suffix[0, 0, s : s + 1, :] = run
        suffix[0, 1, s : s + 1, :] = run_re
        suffix[0, 2, s : s + 1, :] = run_im
        turned_re, turned_im = back_turn(cos_chunk, sin_chunk, run_re, run_im)
        run_re = prod[s : s + 1] * turned_re + end_re[s : s + 1]
        run_im = prod[s : s + 1] * turned_im + end_im[s : s + 1]
        run = run * prod[s : s + 1]
    totals[0] = zeros
    totals[0, 0:1, :] = run
    totals[0, 1:2, :] = run_re
    totals[0, 2:3, :] = run_im


def adjoint_local(d_states, decays, angles, groups, chans):
    rows = decays.shape[0]
    per = rows // groups
    return kernel_call(
        functools.partial(adjoint_local_body, per // CHUNKS, chans),
        (groups,),
        [per_group((per, 2 * chans)), per_group((per, chans)), whole(angles.shape)],
        [
            per_group((per, 2 * chans)),
            per_group((per, chans)),
            per_group((1, 3, CHUNKS, chans)),
            per_group((1, CHUNKS, chans)),
        ],
        [
            jax.ShapeDtypeStruct((rows, 2 * chans), F32),
            jax.ShapeDtypeStruct((rows, chans), F32),
            jax.ShapeDtypeStruct((groups, 3, CHUNKS, chans), F32),
            jax.ShapeDtypeStruct((groups, CHUNKS, chans), F32),
        ],
    )(d_states, decays, angles)


def silu_slope(values, sigma):
    return sigma * (1.0 + values * (1.0 - sigma))


def adjoint_finish_body(
    steps,
    chans,
    blocks,
    me,
    keep,
    gathered,
    local,
    prods,
    suffix,
    pre,
    states,
    entering,
    bound,
    angles,
    table,
    d_pre,
    sums,
    leaving,
):
    g = pl.program_id(0)
    low = bound[0:1, :]
    cos_one, sin_one = angles[0:1, :], angles[1:2, :]
    cos_chunk, sin_chunk = angles[2:3, :], angles[3:4, :]
    cos_dev, sin_dev = angles[4:5, :], angles[5:6, :]
    flow_re = jnp.zeros((1, chans), F32)
    flow_im = jnp.zeros((1, chans), F32)
    for d in reversed(range(blocks)):
        kept = keep[g, d]
        turned_re, turned_im = back_turn(cos_dev, sin_dev, flow_re, flow_im)
        decay = gathered[d, 0, 0:1, :]
        later = d > me[0]
        flow_re = jnp.where(
            later, kept * (decay * turned_re + gathered[d, 0, 1:2, :]), flow_re
        )
        flow_im = jnp.where(
            later, kept * (decay * turned_im + gathered[d, 0, 2:3, :]), flow_im
        )
    for s in reversed(range(CHUNKS)):
        run = suffix[0, 0, s : s + 1, :]
        leaving[0, s : s + 1, :] = run * flow_re + suffix[0, 1, s : s + 1, :]
        leaving[1, s : s + 1, :] = run * flow_im + suffix[0, 2, s : s + 1, :]
        flow_re, flow_im = back_turn(cos_chunk, sin_chunk, flow_re, flow_im)
    leave_re, leave_im = leaving[0], leaving[1]

    def one(j, carry):
        last_re, last_im, phase_sum, bound_sum = carry
        rows = pl.ds(pl.multiple_of(j * CHUNKS, CHUNKS), CHUNKS)
        left = pl.ds(steps - 1 - j, 1)
        prod = prods[rows, :]
        turned_re, turned_im = back_turn(
            table[left, 0:chans], table[left, chans : 2 * chans], leave_re, leave_im
        )
        grad_re = local[rows, 0:chans] + prod * turned_re
        grad_im = local[rows, chans : 2 * chans] + prod * turned_im
        in_re = pre[rows, 0:chans]
        in_im = pre[rows, chans : 2 * chans]
        sigma_re = jax.nn.sigmoid(in_re)
        sigma_im = jax.nn.sigmoid(in_im)
        sigma = jax.nn.sigmoid(pre[rows, 2 * chans : 3 * chans])
        decay = low + (1.0 - low) * sigma
        cross_re = grad_re * last_re + grad_im * last_im
        cross_im = grad_im * last_re - grad_re * last_im
        along, across = back_turn(cos_one, sin_one, cross_re, cross_im)
        d_decay = along - (grad_re * in_re * sigma_re + grad_im * in_im * sigma_im)
        rest = 1.0 - decay
        d_re = grad_re * rest * silu_slope(in_re, sigma_re)
        d_im = grad_im * rest * silu_slope(in_im, sigma_im)
        d_low = d_decay * (1.0 - sigma)
        d_forget = d_low * (1.0 - low) * sigma
        carry = (
            states[rows, 0:chans],
            states[rows, chans : 2 * chans],
            phase_sum + decay * across,
            bound_sum + d_low,
        )
        return carry, (d_re, d_im, d_forget)

    def pair(i, carry):
        carry, first = one(2 * i, carry)
        carry, second = one(2 * i + 1, carry)
        rows = pl.ds(pl.multiple_of(i * 2 * CHUNKS, 2 * CHUNKS), 2 * CHUNKS)
        for k in range(3):
            d_pre[rows, k * chans : (k + 1) * chans] = jnp.concatenate(
                [first[k], second[k]], axis=0
            ).astype(BF16)
        return carry

    zeros = jnp.zeros((CHUNKS, chans), F32)
    _, _, phase_sum, bound_sum = lax.fori_loop(
        0, steps // 2, pair, (entering[0, 0], entering[0, 1], zeros, zeros), unroll=2
    )
    sums[0, 0] = phase_sum
    sums[0, 1] = bound_sum


def adjoint_finish(
    me, keep, gathered, local, prods, suffix, pre, states, entering, bound, angles, table, groups, chans
):
    rows = prods.shape[0]
    per = rows // groups
    blocks = gathered.shape[0]
    return kernel_call(
        functools.partial(adjoint_finish_body, per // CHUNKS, chans, blocks),
        (groups,),
        [
            SMEM_SPEC,
            SMEM_SPEC,
            pl.BlockSpec((blocks, 1, CHUNKS, chans), lambda g: (0, g, 0, 0)),
            per_group((per, 2 * chans)),
            per_group((per, chans)),
            per_group((1, 3, CHUNKS, chans)),
            pl.BlockSpec((per, 3 * chans), lambda g: (g, 0)),
            per_group((per, 2 * chans)),
            per_group((1, 2, CHUNKS, chans)),
            whole((1, chans)),
            whole(angles.shape),
            whole(table.shape),
        ],
        [per_group((per, 3 * chans)), per_group((1, 2, CHUNKS, chans))],
        [
            jax.ShapeDtypeStruct((rows, 3 * chans), BF16),
            jax.ShapeDtypeStruct((groups, 2, CHUNKS, chans), F32),
        ],
        [pltpu.VMEM((2, CHUNKS, chans), F32)],
    )(me, keep, gathered, local, prods, suffix, pre, states, entering, bound, angles, table)


def rms_rows(values):
    return lax.rsqrt(jnp.mean(values * values, axis=-1, keepdims=True) + EPSILON)


def rms_pull(values, inv, gain, d_out):
    scaled = d_out * gain
    dot = jnp.mean(scaled * values, axis=-1, keepdims=True)
    return inv * scaled - values * (inv * inv * inv * dot)


def nt(left, right):
    return lax.dot_general(left, right, (((1,), (1,)), ((), ())), preferred_element_type=F32)


def nn(left, right):
    return lax.dot_general(left, right, (((1,), (0,)), ((), ())), preferred_element_type=F32)


def tn(left, right):
    return lax.dot_general(left, right, (((0,), (0,)), ((), ())), preferred_element_type=F32)


def shards(
    tokens,
    upstream,
    pieces,
    layer_index,
    mix_gain,
    w_input,
    w_forget,
    w_outgate,
    phase_angle,
    lower_logits,
    out_gain,
    w_output,
    ffn_gain,
    w_gate,
    w_up,
    w_down,
):
    rows_dev, groups, width = tokens.shape
    blocks = lax.axis_size("mp")
    me = lax.axis_index("mp")
    seq_len = rows_dev * blocks
    chans_dev = w_input.shape[2]
    chans = chans_dev * blocks
    units_dev = w_gate.shape[1]
    units = units_dev * blocks
    steps = rows_dev // CHUNKS
    rows = rows_dev * groups

    def to_rows(values):
        return jnp.transpose(
            values.reshape(CHUNKS, steps, groups, width), (2, 1, 0, 3)
        ).reshape(rows, width)

    def from_rows(values):
        return jnp.transpose(
            values.reshape(groups, steps, CHUNKS, width), (2, 1, 0, 3)
        ).reshape(rows_dev, groups, width)

    mix_shard = jnp.concatenate(
        [
            jnp.transpose(w_input, (1, 2, 0)),
            jnp.transpose(w_forget)[None],
            jnp.transpose(w_outgate, (1, 2, 0)),
        ],
        axis=0,
    )
    w_mix = jnp.transpose(lax.all_gather(mix_shard, "mp", axis=0), (1, 0, 2, 3)).reshape(
        5 * chans, width
    )
    out_all = jnp.transpose(lax.all_gather(w_output, "mp", axis=0), (1, 0, 2, 3)).reshape(
        2 * chans, width
    )
    gate_all = lax.all_gather(jnp.transpose(w_gate), "mp", axis=0, tiled=True)
    up_all = lax.all_gather(jnp.transpose(w_up), "mp", axis=0, tiled=True)
    down_all = lax.all_gather(w_down, "mp", axis=0, tiled=True)
    layer_mask = (jnp.arange(lower_logits.shape[0], dtype=jnp.int32) < layer_index[0]).astype(F32)
    soft = jax.nn.softmax(lower_logits, axis=0)
    bound_own = jnp.sum(soft * layer_mask[:, None], axis=0)
    small = lax.all_gather(
        jnp.concatenate([bound_own[None], phase_angle[None], out_gain], axis=0), "mp", axis=0
    )
    small = jnp.transpose(small, (1, 0, 2)).reshape(4, chans)
    bound = small[0:1]
    phase = small[1:2]
    gain_row = small[2:4].reshape(1, 2 * chans)
    spans = phase * jnp.array([[1.0], [steps], [rows_dev]], F32)
    angles = jnp.stack([jnp.cos(spans), jnp.sin(spans)], axis=1).reshape(6, chans)
    lags = phase * jnp.arange(steps + 1, dtype=F32)[:, None]
    table = jnp.concatenate([jnp.cos(lags), jnp.sin(lags)], axis=1)
    table_one = table[1:]
    starts = jnp.arange(blocks, dtype=jnp.int32) * rows_dev
    keep = (starts[None, :] % (seq_len // pieces)[:, None] != 0).astype(F32)
    me_one = me[None].astype(jnp.int32)

    tok = to_rows(tokens).astype(F32)
    up_rows = to_rows(upstream)
    mix_row = mix_gain[None]
    inv_tok = rms_rows(tok)
    normed = (tok * inv_tok * mix_row).astype(BF16)
    pre = nt(normed, w_mix)
    local, prods, decays, prefix, totals = scan_local(pre, bound, angles, groups, chans)
    ends = lax.all_gather(totals, "mp", axis=0)
    states, entering = scan_finish(
        me_one, keep, ends, local, prods, prefix, angles, table_one, groups, chans
    )
    mean_square = jnp.mean(states * states, axis=-1, keepdims=True)
    inv_rms = lax.rsqrt(mean_square + EPSILON)
    gate_pre_out = pre[:, 3 * chans :]
    sigma_out = jax.nn.sigmoid(gate_pre_out)
    gated = (states * gain_row * gate_pre_out * sigma_out).astype(BF16)
    mix_out = nn(gated, out_all)
    mid = tok + inv_rms * mix_out
    inv_mid = rms_rows(mid)
    ffn_row = ffn_gain[None]
    ffn_normed = (mid * inv_mid * ffn_row).astype(BF16)

    gate_pre = nt(ffn_normed, gate_all)
    up_pre = nt(ffn_normed, up_all)
    sigma = jax.nn.sigmoid(gate_pre)
    hidden = (gate_pre * sigma * up_pre).astype(BF16)
    result = (mid + nn(hidden, down_all)).astype(BF16)
    d_hidden = nt(up_rows, down_all)
    d_gate = (d_hidden * up_pre * silu_slope(gate_pre, sigma)).astype(BF16)
    d_up = (d_hidden * gate_pre * sigma).astype(BF16)
    grad_down = tn(hidden, up_rows)
    grad_gate = tn(d_gate, ffn_normed)
    grad_up = tn(d_up, ffn_normed)
    d_ffn = nn(d_gate, gate_all) + nn(d_up, up_all)
    grad_ffn = jnp.stack(
        [part.astype(BF16).reshape(blocks, units_dev, width) for part in (grad_gate, grad_up, grad_down)],
        axis=1,
    )
    grad_ffn = lax.psum_scatter(grad_ffn, "mp", scatter_dimension=0, tiled=False)
    grad_ffn = lax.psum(grad_ffn, "dp").astype(F32)

    grad_ffn_gain = jnp.sum(d_ffn * mid * inv_mid, axis=0)
    d_mid = up_rows.astype(F32) + rms_pull(mid, inv_mid, ffn_row, d_ffn)
    d_mix = (inv_rms * d_mid).astype(BF16)
    d_square = -0.5 * inv_rms * inv_rms * inv_rms * jnp.sum(d_mid * mix_out, axis=-1, keepdims=True)
    d_gated = nt(d_mix, out_all)
    grad_out = tn(gated, d_mix).astype(BF16)
    silu_out = gate_pre_out * sigma_out
    d_states = d_gated * gain_row * silu_out + d_square * states / chans
    d_outgate = (d_gated * states * gain_row * silu_slope(gate_pre_out, sigma_out)).astype(BF16)
    grad_out_gain = jnp.sum(d_gated * states * silu_out, axis=0)
    back_local, back_prods, suffix, back_totals = adjoint_local(
        d_states, decays, angles, groups, chans
    )
    back_ends = lax.all_gather(back_totals, "mp", axis=0)
    d_scan, sums = adjoint_finish(
        me_one,
        keep,
        back_ends,
        back_local,
        back_prods,
        suffix,
        pre,
        states,
        entering,
        bound,
        angles,
        table[:-1],
        groups,
        chans,
    )
    d_project = jnp.concatenate([d_scan, d_outgate], axis=1)
    d_normed = nn(d_project, w_mix)
    grad_mix = tn(d_project, normed).astype(BF16)
    grad_tokens = d_mid + rms_pull(tok, inv_tok, mix_row, d_normed)
    grad_mix_gain = jnp.sum(d_normed * tok * inv_tok, axis=0)

    grad_rows = jnp.concatenate(
        [
            grad_mix.reshape(5, blocks, chans_dev, width),
            grad_out.reshape(2, blocks, chans_dev, width),
        ],
        axis=0,
    )
    grad_rows = jnp.transpose(grad_rows, (1, 0, 2, 3))
    grad_rows = lax.psum_scatter(grad_rows, "mp", scatter_dimension=0, tiled=False)
    grad_rows = lax.psum(grad_rows, "dp").astype(F32)
    sums = jnp.sum(sums, axis=(0, 2))
    flat = jnp.concatenate(
        [grad_mix_gain, grad_ffn_gain, grad_out_gain, sums[0], sums[1]], axis=0
    )
    flat = lax.psum(flat, ("dp", "mp"))
    own = me * chans_dev

    def own_part(offset):
        return lax.dynamic_slice(flat, (2 * width + offset * chans + own,), (chans_dev,))

    grad_gain = jnp.stack([own_part(0), own_part(1)], axis=0)
    d_bound = own_part(3)
    grad_lower = soft * (layer_mask[:, None] - bound_own[None]) * d_bound[None]
    return (
        from_rows(result),
        from_rows(grad_tokens.astype(BF16)),
        flat[0:width],
        jnp.transpose(grad_rows[0:2], (2, 0, 1)),
        jnp.transpose(grad_rows[2]),
        jnp.transpose(grad_rows[3:5], (2, 0, 1)),
        own_part(2),
        grad_lower,
        grad_gain,
        grad_rows[5:7],
        flat[width : 2 * width],
        jnp.transpose(grad_ffn[0]),
        jnp.transpose(grad_ffn[1]),
        grad_ffn[2],
    )


def solution(mesh):
    in_specs = (
        P("mp", "dp", None),
        P("mp", "dp", None),
        P("dp"),
        P(),
        P(),
        P(None, None, "mp"),
        P(None, "mp"),
        P(None, None, "mp"),
        P("mp"),
        P(None, "mp"),
        P(None, "mp"),
        P(None, "mp", None),
        P(),
        P(None, "mp"),
        P(None, "mp"),
        P("mp", None),
    )
    out_specs = (
        P("mp", "dp", None),
        P("mp", "dp", None),
        P(),
        P(None, None, "mp"),
        P(None, "mp"),
        P(None, None, "mp"),
        P("mp"),
        P(None, "mp"),
        P(None, "mp"),
        P(None, "mp", None),
        P(),
        P(None, "mp"),
        P(None, "mp"),
        P("mp", None),
    )
    return jax.shard_map(shards, mesh=mesh, in_specs=in_specs, out_specs=out_specs, check_vma=False)
```

```python
import functools

import jax
import jax.numpy as jnp
from jax import lax
from jax.experimental import pallas as pl
from jax.experimental.pallas import tpu as pltpu
from jax.sharding import PartitionSpec as P

EPSILON = 1e-06
CHUNKS = 8
VMEM_BYTES = 48 * 1024 * 1024
F32 = jnp.float32
BF16 = jnp.bfloat16


def kernel_call(body, grid, in_specs, out_specs, out_shape, scratch=()):
    return pl.pallas_call(
        body,
        grid=grid,
        in_specs=in_specs,
        out_specs=out_specs,
        out_shape=out_shape,
        scratch_shapes=scratch,
        compiler_params=pltpu.CompilerParams(vmem_limit_bytes=VMEM_BYTES),
    )


def whole(shape):
    zeros = (0,) * len(shape)
    return pl.BlockSpec(shape, lambda *_: zeros)


def per_group(shape):
    zeros = (0,) * (len(shape) - 1)
    return pl.BlockSpec(shape, lambda g: (g,) + zeros)


SMEM_SPEC = pl.BlockSpec(memory_space=pltpu.SMEM)


def turn(cos, sin, re, im):
    return cos * re - sin * im, sin * re + cos * im


def back_turn(cos, sin, re, im):
    return cos * re + sin * im, cos * im - sin * re


def scan_local_body(steps, chans, pre, bound, angles, local, prods, decays, prefix, totals):
    low = bound[0:1, :]
    cos_one, sin_one = angles[0:1, :], angles[1:2, :]
    cos_chunk, sin_chunk = angles[2:3, :], angles[3:4, :]

    def step(j, carry):
        state_re, state_im, prod = carry
        rows = pl.ds(pl.multiple_of(j * CHUNKS, CHUNKS), CHUNKS)
        in_re = pre[rows, 0:chans]
        in_im = pre[rows, chans : 2 * chans]
        decay = low + (1.0 - low) * jax.nn.sigmoid(pre[rows, 2 * chans : 3 * chans])
        turned_re, turned_im = turn(cos_one, sin_one, state_re, state_im)
        state_re = decay * turned_re + (1.0 - decay) * (in_re * jax.nn.sigmoid(in_re))
        state_im = decay * turned_im + (1.0 - decay) * (in_im * jax.nn.sigmoid(in_im))
        prod = prod * decay
        local[rows, 0:chans] = state_re
        local[rows, chans : 2 * chans] = state_im
        prods[rows, :] = prod
        decays[rows, :] = decay
        return state_re, state_im, prod

    zeros = jnp.zeros((CHUNKS, chans), F32)
    end_re, end_im, prod = lax.fori_loop(0, steps, step, (zeros, zeros, zeros + 1.0), unroll=4)
    run, run_re, run_im = zeros[0:1] + 1.0, zeros[0:1], zeros[0:1]
    for s in range(CHUNKS):
        prefix[0, 0, s : s + 1, :] = run
        prefix[0, 1, s : s + 1, :] = run_re
        prefix[0, 2, s : s + 1, :] = run_im
        turned_re, turned_im = turn(cos_chunk, sin_chunk, run_re, run_im)
        run_re = prod[s : s + 1] * turned_re + end_re[s : s + 1]
        run_im = prod[s : s + 1] * turned_im + end_im[s : s + 1]
        run = run * prod[s : s + 1]
    totals[0] = zeros
    totals[0, 0:1, :] = run
    totals[0, 1:2, :] = run_re
    totals[0, 2:3, :] = run_im


def scan_local(pre, bound, angles, groups, chans):
    rows = pre.shape[0]
    per = rows // groups
    return kernel_call(
        functools.partial(scan_local_body, per // CHUNKS, chans),
        (groups,),
        [
            pl.BlockSpec((per, 3 * chans), lambda g: (g, 0)),
            whole((1, chans)),
            whole(angles.shape),
        ],
        [
            per_group((per, 2 * chans)),
            per_group((per, chans)),
            per_group((per, chans)),
            per_group((1, 3, CHUNKS, chans)),
            per_group((1, CHUNKS, chans)),
        ],
        [
            jax.ShapeDtypeStruct((rows, 2 * chans), F32),
            jax.ShapeDtypeStruct((rows, chans), F32),
            jax.ShapeDtypeStruct((rows, chans), F32),
            jax.ShapeDtypeStruct((groups, 3, CHUNKS, chans), F32),
            jax.ShapeDtypeStruct((groups, CHUNKS, chans), F32),
        ],
    )(pre, bound, angles)


def scan_finish_body(
    steps, chans, blocks, me, keep, gathered, local, prods, prefix, angles, table, states, entering
):
    g = pl.program_id(0)
    cos_dev, sin_dev = angles[4:5, :], angles[5:6, :]
    state_re = jnp.zeros((1, chans), F32)
    state_im = jnp.zeros((1, chans), F32)
    for d in range(blocks):
        kept = keep[g, d]
        turned_re, turned_im = turn(cos_dev, sin_dev, kept * state_re, kept * state_im)
        decay = gathered[d, 0, 0:1, :]
        earlier = d < me[0]
        state_re = jnp.where(earlier, decay * turned_re + gathered[d, 0, 1:2, :], state_re)
        state_im = jnp.where(earlier, decay * turned_im + gathered[d, 0, 2:3, :], state_im)
    kept = keep[g, me[0]]
    state_re, state_im = kept * state_re, kept * state_im
    cos_chunk, sin_chunk = angles[2:3, :], angles[3:4, :]
    for s in range(CHUNKS):
        run = prefix[0, 0, s : s + 1, :]
        entering[0, 0, s : s + 1, :] = run * state_re + prefix[0, 1, s : s + 1, :]
        entering[0, 1, s : s + 1, :] = run * state_im + prefix[0, 2, s : s + 1, :]
        state_re, state_im = turn(cos_chunk, sin_chunk, state_re, state_im)
    enter_re, enter_im = entering[0, 0], entering[0, 1]

    def step(j, carry):
        rows = pl.ds(pl.multiple_of(j * CHUNKS, CHUNKS), CHUNKS)
        prod = prods[rows, :]
        turned_re, turned_im = turn(
            table[pl.ds(j, 1), 0:chans], table[pl.ds(j, 1), chans : 2 * chans], enter_re, enter_im
        )
        states[rows, 0:chans] = local[rows, 0:chans] + prod * turned_re
        states[rows, chans : 2 * chans] = local[rows, chans : 2 * chans] + prod * turned_im
        return carry

    lax.fori_loop(0, steps, step, 0, unroll=4)


def scan_finish(me, keep, gathered, local, prods, prefix, angles, table, groups, chans):
    rows = prods.shape[0]
    per = rows // groups
    blocks = gathered.shape[0]
    return kernel_call(
        functools.partial(scan_finish_body, per // CHUNKS, chans, blocks),
        (groups,),
        [
            SMEM_SPEC,
            SMEM_SPEC,
            pl.BlockSpec((blocks, 1, CHUNKS, chans), lambda g: (0, g, 0, 0)),
            per_group((per, 2 * chans)),
            per_group((per, chans)),
            per_group((1, 3, CHUNKS, chans)),
            whole(angles.shape),
            whole(table.shape),
        ],
        [per_group((per, 2 * chans)), per_group((1, 2, CHUNKS, chans))],
        [
            jax.ShapeDtypeStruct((rows, 2 * chans), F32),
            jax.ShapeDtypeStruct((groups, 2, CHUNKS, chans), F32),
        ],
    )(me, keep, gathered, local, prods, prefix, angles, table)


def adjoint_local_body(steps, chans, d_states, decays, angles, local, prods, suffix, totals):
    cos_one, sin_one = angles[0:1, :], angles[1:2, :]
    cos_chunk, sin_chunk = angles[2:3, :], angles[3:4, :]

    def step(i, carry):
        flow_re, flow_im, prod = carry
        j = steps - 1 - i
        rows = pl.ds(pl.multiple_of(j * CHUNKS, CHUNKS), CHUNKS)
        grad_re = d_states[rows, 0:chans] + flow_re
        grad_im = d_states[rows, chans : 2 * chans] + flow_im
        local[rows, 0:chans] = grad_re
        local[rows, chans : 2 * chans] = grad_im
        prods[rows, :] = prod
        decay = decays[rows, :]
        turned_re, turned_im = back_turn(cos_one, sin_one, grad_re, grad_im)
        return decay * turned_re, decay * turned_im, prod * decay

    zeros = jnp.zeros((CHUNKS, chans), F32)
    end_re, end_im, prod = lax.fori_loop(0, steps, step, (zeros, zeros, zeros + 1.0), unroll=4)
    run, run_re, run_im = zeros[0:1] + 1.0, zeros[0:1], zeros[0:1]
    for s in reversed(range(CHUNKS)):
        suffix[0, 0, s : s + 1, :] = run
        suffix[0, 1, s : s + 1, :] = run_re
        suffix[0, 2, s : s + 1, :] = run_im
        turned_re, turned_im = back_turn(cos_chunk, sin_chunk, run_re, run_im)
        run_re = prod[s : s + 1] * turned_re + end_re[s : s + 1]
        run_im = prod[s : s + 1] * turned_im + end_im[s : s + 1]
        run = run * prod[s : s + 1]
    totals[0] = zeros
    totals[0, 0:1, :] = run
    totals[0, 1:2, :] = run_re
    totals[0, 2:3, :] = run_im


def adjoint_local(d_states, decays, angles, groups, chans):
    rows = decays.shape[0]
    per = rows // groups
    return kernel_call(
        functools.partial(adjoint_local_body, per // CHUNKS, chans),
        (groups,),
        [per_group((per, 2 * chans)), per_group((per, chans)), whole(angles.shape)],
        [
            per_group((per, 2 * chans)),
            per_group((per, chans)),
            per_group((1, 3, CHUNKS, chans)),
            per_group((1, CHUNKS, chans)),
        ],
        [
            jax.ShapeDtypeStruct((rows, 2 * chans), F32),
            jax.ShapeDtypeStruct((rows, chans), F32),
            jax.ShapeDtypeStruct((groups, 3, CHUNKS, chans), F32),
            jax.ShapeDtypeStruct((groups, CHUNKS, chans), F32),
        ],
    )(d_states, decays, angles)


def silu_slope(values, sigma):
    return sigma * (1.0 + values * (1.0 - sigma))


def adjoint_finish_body(
    steps,
    chans,
    blocks,
    me,
    keep,
    gathered,
    local,
    prods,
    suffix,
    pre,
    states,
    entering,
    bound,
    angles,
    table,
    d_pre,
    sums,
    leaving,
):
    g = pl.program_id(0)
    low = bound[0:1, :]
    cos_one, sin_one = angles[0:1, :], angles[1:2, :]
    cos_chunk, sin_chunk = angles[2:3, :], angles[3:4, :]
    cos_dev, sin_dev = angles[4:5, :], angles[5:6, :]
    flow_re = jnp.zeros((1, chans), F32)
    flow_im = jnp.zeros((1, chans), F32)
    for d in reversed(range(blocks)):
        kept = keep[g, d]
        turned_re, turned_im = back_turn(cos_dev, sin_dev, flow_re, flow_im)
        decay = gathered[d, 0, 0:1, :]
        later = d > me[0]
        flow_re = jnp.where(
            later, kept * (decay * turned_re + gathered[d, 0, 1:2, :]), flow_re
        )
        flow_im = jnp.where(
            later, kept * (decay * turned_im + gathered[d, 0, 2:3, :]), flow_im
        )
    for s in reversed(range(CHUNKS)):
        run = suffix[0, 0, s : s + 1, :]
        leaving[0, s : s + 1, :] = run * flow_re + suffix[0, 1, s : s + 1, :]
        leaving[1, s : s + 1, :] = run * flow_im + suffix[0, 2, s : s + 1, :]
        flow_re, flow_im = back_turn(cos_chunk, sin_chunk, flow_re, flow_im)
    leave_re, leave_im = leaving[0], leaving[1]

    def one(j, carry):
        last_re, last_im, phase_sum, bound_sum = carry
        rows = pl.ds(pl.multiple_of(j * CHUNKS, CHUNKS), CHUNKS)
        left = pl.ds(steps - 1 - j, 1)
        prod = prods[rows, :]
        turned_re, turned_im = back_turn(
            table[left, 0:chans], table[left, chans : 2 * chans], leave_re, leave_im
        )
        grad_re = local[rows, 0:chans] + prod * turned_re
        grad_im = local[rows, chans : 2 * chans] + prod * turned_im
        in_re = pre[rows, 0:chans]
        in_im = pre[rows, chans : 2 * chans]
        sigma_re = jax.nn.sigmoid(in_re)
        sigma_im = jax.nn.sigmoid(in_im)
        sigma = jax.nn.sigmoid(pre[rows, 2 * chans : 3 * chans])
        decay = low + (1.0 - low) * sigma
        cross_re = grad_re * last_re + grad_im * last_im
        cross_im = grad_im * last_re - grad_re * last_im
        along, across = back_turn(cos_one, sin_one, cross_re, cross_im)
        d_decay = along - (grad_re * in_re * sigma_re + grad_im * in_im * sigma_im)
        rest = 1.0 - decay
        d_re = grad_re * rest * silu_slope(in_re, sigma_re)
        d_im = grad_im * rest * silu_slope(in_im, sigma_im)
        d_low = d_decay * (1.0 - sigma)
        d_forget = d_low * (1.0 - low) * sigma
        carry = (
            states[rows, 0:chans],
            states[rows, chans : 2 * chans],
            phase_sum + decay * across,
            bound_sum + d_low,
        )
        return carry, (d_re, d_im, d_forget)

    def pair(i, carry):
        carry, first = one(2 * i, carry)
        carry, second = one(2 * i + 1, carry)
        rows = pl.ds(pl.multiple_of(i * 2 * CHUNKS, 2 * CHUNKS), 2 * CHUNKS)
        for k in range(3):
            d_pre[rows, k * chans : (k + 1) * chans] = jnp.concatenate(
                [first[k], second[k]], axis=0
            ).astype(BF16)
        return carry

    zeros = jnp.zeros((CHUNKS, chans), F32)
    _, _, phase_sum, bound_sum = lax.fori_loop(
        0, steps // 2, pair, (entering[0, 0], entering[0, 1], zeros, zeros), unroll=2
    )
    sums[0, 0] = phase_sum
    sums[0, 1] = bound_sum


def adjoint_finish(
    me, keep, gathered, local, prods, suffix, pre, states, entering, bound, angles, table, groups, chans
):
    rows = prods.shape[0]
    per = rows // groups
    blocks = gathered.shape[0]
    return kernel_call(
        functools.partial(adjoint_finish_body, per // CHUNKS, chans, blocks),
        (groups,),
        [
            SMEM_SPEC,
            SMEM_SPEC,
            pl.BlockSpec((blocks, 1, CHUNKS, chans), lambda g: (0, g, 0, 0)),
            per_group((per, 2 * chans)),
            per_group((per, chans)),
            per_group((1, 3, CHUNKS, chans)),
            pl.BlockSpec((per, 3 * chans), lambda g: (g, 0)),
            per_group((per, 2 * chans)),
            per_group((1, 2, CHUNKS, chans)),
            whole((1, chans)),
            whole(angles.shape),
            whole(table.shape),
        ],
        [per_group((per, 3 * chans)), per_group((1, 2, CHUNKS, chans))],
        [
            jax.ShapeDtypeStruct((rows, 3 * chans), BF16),
            jax.ShapeDtypeStruct((groups, 2, CHUNKS, chans), F32),
        ],
        [pltpu.VMEM((2, CHUNKS, chans), F32)],
    )(me, keep, gathered, local, prods, suffix, pre, states, entering, bound, angles, table)


def swap(values, axis, bit, size):
    return lax.ppermute(values, axis, [(i, i ^ bit) for i in range(size)])


def joined(*parts):
    return sum(part.astype(F32) for part in parts)


def pick(values, index, axis):
    return lax.dynamic_index_in_dim(values, index, axis, keepdims=False)


def gather_pieces(shard, size):
    half = shard.shape[0] // 2
    near_x = swap(shard, "mp", 2, size)
    near_y = swap(shard, "mp", 4, size)
    core = swap(shard, "mp", 1, size)
    far_one = swap(near_x[:half], "mp", 4, size)
    far_two = swap(near_y[half:], "mp", 2, size)
    core_x = swap(near_x, "mp", 1, size)
    core_y = swap(near_y, "mp", 1, size)
    far = jnp.concatenate([far_one, far_two], axis=0)
    core_far = swap(far, "mp", 1, size)
    return shard, core, near_x, core_x, near_y, core_y, far, core_far


def reduce_mp(grads, me, size):
    n, _, r, width = grads.shape
    if size != 8:
        grads = jnp.moveaxis(grads, 1, 0)
        return lax.psum_scatter(grads, "mp", scatter_dimension=0, tiled=False).reshape(n * r, width)
    core, chip = me & 1, me >> 1
    cores = grads.reshape(n, 4, 2, r, width)
    other = swap(pick(cores, 1 - core, 2), "mp", 1, size)
    chips = joined(pick(cores, core, 2), other).astype(BF16)

    def piece(b):
        return pick(chips, chip ^ b, 1).reshape(n * r, width)

    half = n * r // 32 * 16
    far = piece(3)
    far_x = swap(far[:half], "mp", 2, size)
    far_y = swap(far[half:], "mp", 4, size)
    send_x, send_y = piece(1), piece(2)
    send_x = jnp.concatenate([send_x[:half], joined(send_x[half:], far_y).astype(BF16)], axis=0)
    send_y = jnp.concatenate([joined(send_y[:half], far_x).astype(BF16), send_y[half:]], axis=0)
    near_x = swap(send_x, "mp", 2, size)
    near_y = swap(send_y, "mp", 4, size)
    return joined(piece(0), near_x, near_y).astype(BF16)


def reduce_dp(share, z, size):
    rows = share.shape[0]
    if size != 4 or rows % 64:
        return lax.psum(share, "dp").astype(F32)
    one, two = z & 1, z >> 1
    halves = share.reshape(2, rows // 2, share.shape[1])
    got = swap(pick(halves, 1 - one, 0), "dp", 1, size)
    half = joined(pick(halves, one, 0), got).astype(BF16)
    quarters = half.reshape(2, rows // 4, share.shape[1])
    got = swap(pick(quarters, 1 - two, 0), "dp", 2, size)
    own = joined(pick(quarters, two, 0), got).astype(BF16)
    got = swap(own, "dp", 2, size)
    first = two == 0
    half = jnp.concatenate([jnp.where(first, own, got), jnp.where(first, got, own)], axis=0)
    got = swap(half, "dp", 1, size)
    first = one == 0
    whole_sum = jnp.concatenate([jnp.where(first, half, got), jnp.where(first, got, half)], axis=0)
    return whole_sum.astype(F32)


def reduce_dp_short(share, size):
    if size != 4:
        return lax.psum(share, "dp").astype(F32)
    share = joined(share, swap(share, "dp", 1, size)).astype(share.dtype)
    return joined(share, swap(share, "dp", 2, size))


def reduce_all(values, mp_size, dp_size):
    for axis, size in (("mp", mp_size), ("dp", dp_size)):
        bit = 1
        while bit < size:
            values = values + swap(values, axis, bit, size)
            bit *= 2
    return values


def assemble_body(me, *refs):
    out = refs[-1]
    for b, ref in enumerate(refs[:-1]):
        out[:, me[0] ^ b] = ref[...]


def assemble(me, pieces):
    n, r, width = pieces[0].shape
    vmem = pl.BlockSpec(memory_space=pltpu.VMEM)
    return pl.pallas_call(
        assemble_body,
        in_specs=[SMEM_SPEC] + [vmem] * len(pieces),
        out_specs=vmem,
        out_shape=jax.ShapeDtypeStruct((n, len(pieces), r, width), BF16),
        compiler_params=pltpu.CompilerParams(vmem_limit_bytes=VMEM_BYTES),
    )(me, *pieces)


def rms_rows(values):
    return lax.rsqrt(jnp.mean(values * values, axis=-1, keepdims=True) + EPSILON)


def rms_pull(values, inv, gain, d_out):
    scaled = d_out * gain
    dot = jnp.mean(scaled * values, axis=-1, keepdims=True)
    return inv * scaled - values * (inv * inv * inv * dot)


def nt(left, right):
    return lax.dot_general(left, right, (((1,), (1,)), ((), ())), preferred_element_type=F32)


def nn(left, right):
    return lax.dot_general(left, right, (((1,), (0,)), ((), ())), preferred_element_type=F32)


def tn(left, right):
    return lax.dot_general(left, right, (((0,), (0,)), ((), ())), preferred_element_type=F32)


def shards(
    tokens,
    upstream,
    pieces,
    layer_index,
    mix_gain,
    w_input,
    w_forget,
    w_outgate,
    phase_angle,
    lower_logits,
    out_gain,
    w_output,
    ffn_gain,
    w_gate,
    w_up,
    w_down,
):
    rows_dev, groups, width = tokens.shape
    blocks = lax.axis_size("mp")
    me = lax.axis_index("mp")
    layers_z = lax.axis_size("dp")
    at_z = lax.axis_index("dp")
    seq_len = rows_dev * blocks
    chans_dev = w_input.shape[2]
    chans = chans_dev * blocks
    units_dev = w_gate.shape[1]
    units = units_dev * blocks
    steps = rows_dev // CHUNKS
    rows = rows_dev * groups

    def to_rows(values):
        return jnp.transpose(
            values.reshape(CHUNKS, steps, groups, width), (2, 1, 0, 3)
        ).reshape(rows, width)

    def from_rows(values):
        return jnp.transpose(
            values.reshape(groups, steps, CHUNKS, width), (2, 1, 0, 3)
        ).reshape(rows_dev, groups, width)

    mix_shard = jnp.concatenate(
        [
            jnp.transpose(w_input, (1, 2, 0)),
            jnp.transpose(w_forget)[None],
            jnp.transpose(w_outgate, (1, 2, 0)),
        ],
        axis=0,
    )
    me_one = me[None].astype(jnp.int32)
    if blocks == 8:
        w_mix = assemble(me_one, gather_pieces(mix_shard, blocks))
    else:
        w_mix = jnp.transpose(lax.all_gather(mix_shard, "mp", axis=0), (1, 0, 2, 3))
    w_mix = w_mix.reshape(5 * chans, width)
    rest = jnp.concatenate(
        [jnp.transpose(w_gate), jnp.transpose(w_up), w_down, w_output.reshape(-1, width)], axis=0
    )
    rest = lax.all_gather(rest, "mp", axis=0)
    gate_all = rest[:, :units_dev].reshape(units, width)
    up_all = rest[:, units_dev : 2 * units_dev].reshape(units, width)
    down_all = rest[:, 2 * units_dev : 3 * units_dev].reshape(units, width)
    out_all = jnp.transpose(
        rest[:, 3 * units_dev :].reshape(blocks, 2, chans_dev, width), (1, 0, 2, 3)
    ).reshape(2 * chans, width)
    layer_mask = (jnp.arange(lower_logits.shape[0], dtype=jnp.int32) < layer_index[0]).astype(F32)
    soft = jax.nn.softmax(lower_logits, axis=0)
    bound_own = jnp.sum(soft * layer_mask[:, None], axis=0)
    small = lax.all_gather(
        jnp.concatenate([bound_own[None], phase_angle[None], out_gain], axis=0), "mp", axis=0
    )
    small = jnp.transpose(small, (1, 0, 2)).reshape(4, chans)
    bound = small[0:1]
    phase = small[1:2]
    gain_row = small[2:4].reshape(1, 2 * chans)
    spans = phase * jnp.array([[1.0], [steps], [rows_dev]], F32)
    angles = jnp.stack([jnp.cos(spans), jnp.sin(spans)], axis=1).reshape(6, chans)
    lags = phase * jnp.arange(steps + 1, dtype=F32)[:, None]
    table = jnp.concatenate([jnp.cos(lags), jnp.sin(lags)], axis=1)
    table_one = table[1:]
    starts = jnp.arange(blocks, dtype=jnp.int32) * rows_dev
    keep = (starts[None, :] % (seq_len // pieces)[:, None] != 0).astype(F32)

    tok = to_rows(tokens).astype(F32)
    up_rows = to_rows(upstream)
    mix_row = mix_gain[None]
    inv_tok = rms_rows(tok)
    normed = (tok * inv_tok * mix_row).astype(BF16)
    pre = nt(normed, w_mix)
    local, prods, decays, prefix, totals = scan_local(pre, bound, angles, groups, chans)
    ends = lax.all_gather(totals, "mp", axis=0)
    states, entering = scan_finish(
        me_one, keep, ends, local, prods, prefix, angles, table_one, groups, chans
    )
    mean_square = jnp.mean(states * states, axis=-1, keepdims=True)
    inv_rms = lax.rsqrt(mean_square + EPSILON)
    gate_pre_out = pre[:, 3 * chans :]
    sigma_out = jax.nn.sigmoid(gate_pre_out)
    gated = (states * gain_row * gate_pre_out * sigma_out).astype(BF16)
    mix_out = nn(gated, out_all)
    mid = tok + inv_rms * mix_out
    inv_mid = rms_rows(mid)
    ffn_row = ffn_gain[None]
    ffn_normed = (mid * inv_mid * ffn_row).astype(BF16)

    gate_pre = nt(ffn_normed, gate_all)
    up_pre = nt(ffn_normed, up_all)
    sigma = jax.nn.sigmoid(gate_pre)
    hidden = (gate_pre * sigma * up_pre).astype(BF16)
    result = (mid + nn(hidden, down_all)).astype(BF16)
    d_hidden = nt(up_rows, down_all)
    d_gate = (d_hidden * up_pre * silu_slope(gate_pre, sigma)).astype(BF16)
    d_up = (d_hidden * gate_pre * sigma).astype(BF16)
    grad_down = tn(hidden, up_rows)
    grad_gate = tn(d_gate, ffn_normed)
    grad_up = tn(d_up, ffn_normed)
    d_ffn = nn(d_gate, gate_all) + nn(d_up, up_all)
    grad_ffn = jnp.stack(
        [part.astype(BF16).reshape(blocks, units_dev, width) for part in (grad_gate, grad_up, grad_down)],
        axis=0,
    )
    grad_ffn = reduce_dp(reduce_mp(grad_ffn, me, blocks), at_z, layers_z)
    grad_ffn = grad_ffn.reshape(3, units_dev, width)

    grad_ffn_gain = jnp.sum(d_ffn * mid * inv_mid, axis=0)
    d_mid = up_rows.astype(F32) + rms_pull(mid, inv_mid, ffn_row, d_ffn)
    d_mix = (inv_rms * d_mid).astype(BF16)
    d_square = -0.5 * inv_rms * inv_rms * inv_rms * jnp.sum(d_mid * mix_out, axis=-1, keepdims=True)
    d_gated = nt(d_mix, out_all)
    grad_out = tn(gated, d_mix).astype(BF16)
    silu_out = gate_pre_out * sigma_out
    d_states = d_gated * gain_row * silu_out + d_square * states / chans
    d_outgate = (d_gated * states * gain_row * silu_slope(gate_pre_out, sigma_out)).astype(BF16)
    grad_out_gain = jnp.sum(d_gated * states * silu_out, axis=0)
    back_local, back_prods, suffix, back_totals = adjoint_local(
        d_states, decays, angles, groups, chans
    )
    back_ends = lax.all_gather(back_totals, "mp", axis=0)
    d_scan, sums = adjoint_finish(
        me_one,
        keep,
        back_ends,
        back_local,
        back_prods,
        suffix,
        pre,
        states,
        entering,
        bound,
        angles,
        table[:-1],
        groups,
        chans,
    )
    d_project = jnp.concatenate([d_scan, d_outgate], axis=1)
    d_normed = nn(d_project, w_mix)
    grad_mix = tn(d_scan, normed).astype(BF16)
    grad_outgate = tn(d_outgate, normed).astype(BF16)
    grad_tokens = d_mid + rms_pull(tok, inv_tok, mix_row, d_normed)
    grad_mix_gain = jnp.sum(d_normed * tok * inv_tok, axis=0)

    early = jnp.concatenate([grad_out.reshape(2, blocks, chans_dev, width), grad_outgate.reshape(2, blocks, chans_dev, width)], axis=0)
    early = reduce_dp_short(reduce_mp(early, me, blocks), layers_z).reshape(4, chans_dev, width)
    late = reduce_mp(grad_mix.reshape(3, blocks, chans_dev, width), me, blocks)
    late = reduce_dp_short(late, layers_z).reshape(3, chans_dev, width)
    sums = jnp.sum(sums, axis=(0, 2))
    flat = jnp.concatenate(
        [grad_mix_gain, grad_ffn_gain, grad_out_gain, sums[0], sums[1]], axis=0
    )
    flat = reduce_all(flat.reshape(8, -1), blocks, layers_z).reshape(-1)
    own = me * chans_dev

    def own_part(offset):
        return lax.dynamic_slice(flat, (2 * width + offset * chans + own,), (chans_dev,))

    grad_gain = jnp.stack([own_part(0), own_part(1)], axis=0)
    d_bound = own_part(3)
    grad_lower = soft * (layer_mask[:, None] - bound_own[None]) * d_bound[None]
    return (
        from_rows(result),
        from_rows(grad_tokens.astype(BF16)),
        flat[0:width],
        jnp.transpose(late[0:2], (2, 0, 1)),
        jnp.transpose(late[2]),
        jnp.transpose(early[2:4], (2, 0, 1)),
        own_part(2),
        grad_lower,
        grad_gain,
        early[0:2],
        flat[width : 2 * width],
        jnp.transpose(grad_ffn[0]),
        jnp.transpose(grad_ffn[1]),
        grad_ffn[2],
    )


def solution(mesh):
    in_specs = (
        P("mp", "dp", None),
        P("mp", "dp", None),
        P("dp"),
        P(),
        P(),
        P(None, None, "mp"),
        P(None, "mp"),
        P(None, None, "mp"),
        P("mp"),
        P(None, "mp"),
        P(None, "mp"),
        P(None, "mp", None),
        P(),
        P(None, "mp"),
        P(None, "mp"),
        P("mp", None),
    )
    out_specs = (
        P("mp", "dp", None),
        P("mp", "dp", None),
        P(),
        P(None, None, "mp"),
        P(None, "mp"),
        P(None, None, "mp"),
        P("mp"),
        P(None, "mp"),
        P(None, "mp"),
        P(None, "mp", None),
        P(),
        P(None, "mp"),
        P(None, "mp"),
        P("mp", None),
    )
    return jax.shard_map(shards, mesh=mesh, in_specs=in_specs, out_specs=out_specs, check_vma=False)
```

```python
import functools

import jax
import jax.numpy as jnp
from jax import lax
from jax.experimental import pallas as pl
from jax.experimental.pallas import tpu as pltpu
from jax.sharding import PartitionSpec as P

EPSILON = 1e-06
CHUNKS = 8
TILE = 256
MIB = 1024 * 1024
F32 = jnp.float32
BF16 = jnp.bfloat16


class Near:
    def __init__(self, value):
        self.value = value


def kernel_call(body, grid, in_specs, out_specs, out_shape, scratch=(), vmem=32):
    def space(shape):
        if isinstance(shape, Near):
            return pltpu.VMEM(shape.value.shape, shape.value.dtype)
        return pltpu.HBM(shape.shape, shape.dtype) if shape.size >= 65536 else shape

    def placed(value):
        if isinstance(value, Near):
            return pltpu.with_memory_space_constraint(value.value, pltpu.VMEM)
        if value.size < 65536:
            return value
        return pltpu.with_memory_space_constraint(value, pltpu.HBM)

    single = not isinstance(out_shape, (list, tuple))
    call = pl.pallas_call(
        body,
        grid=grid,
        in_specs=in_specs,
        out_specs=out_specs,
        out_shape=space(out_shape) if single else [space(shape) for shape in out_shape],
        scratch_shapes=scratch,
        cost_estimate=pl.CostEstimate(flops=1, bytes_accessed=1, transcendentals=0),
        compiler_params=pltpu.CompilerParams(vmem_limit_bytes=vmem * MIB),
    )
    return lambda *args: call(*map(placed, args))


def shaped(shape, dtype=F32):
    return jax.ShapeDtypeStruct(shape, dtype)


def whole(shape, start=None):
    start = start or (0,) * len(shape)
    return pl.BlockSpec(shape, lambda *_: start, pipeline_mode=pl.Buffered(1))


def kept(shape):
    zeros = (0,) * len(shape)
    return pl.BlockSpec(shape, lambda *_: zeros)


def per_group(shape):
    zeros = (0,) * (len(shape) - 1)
    return pl.BlockSpec(shape, lambda g, t: (g,) + zeros)


def ahead(tiles, rows, width):
    return pl.BlockSpec((rows, width), lambda g, t: (g * tiles + t, 0))


def behind(tiles, rows, width):
    return pl.BlockSpec((rows, width), lambda g, t: (g * tiles + tiles - 1 - t, 0))


SMEM_SPEC = pl.BlockSpec(memory_space=pltpu.SMEM)
VMEM_SPEC = pl.BlockSpec(memory_space=pltpu.VMEM)


def turn(cos, sin, re, im):
    return cos * re - sin * im, sin * re + cos * im


def back_turn(cos, sin, re, im):
    return cos * re + sin * im, cos * im - sin * re


def sigmoid(values):
    return 0.5 * jnp.tanh(0.5 * values) + 0.5


def nt(left, right):
    return lax.dot_general(left, right, (((1,), (1,)), ((), ())), preferred_element_type=F32)


def nn(left, right):
    return lax.dot_general(left, right, (((1,), (0,)), ((), ())), preferred_element_type=F32)


def tn(left, right):
    return lax.dot_general(left, right, (((0,), (0,)), ((), ())), preferred_element_type=F32)


def rms_rows(values):
    return lax.rsqrt(jnp.mean(values * values, axis=-1, keepdims=True) + EPSILON)


def rms_pull(unit, inv, gain, d_out):
    scaled = d_out * gain
    return inv * (scaled - unit * jnp.mean(scaled * unit, axis=-1, keepdims=True))


def step_rows(j):
    return pl.ds(pl.multiple_of(j * CHUNKS, CHUNKS), CHUNKS)


def chain_chunks(order, turning, angles, prod, end_re, end_im, chain, totals):
    cos_chunk, sin_chunk = angles[2:3, :], angles[3:4, :]
    zero = jnp.zeros_like(prod[0:1])
    run, run_re, run_im = zero + 1.0, zero, zero
    for s in order:
        chain[0, 0, s : s + 1, :] = run
        chain[0, 1, s : s + 1, :] = run_re
        chain[0, 2, s : s + 1, :] = run_im
        turned_re, turned_im = turning(cos_chunk, sin_chunk, run_re, run_im)
        run_re = prod[s : s + 1] * turned_re + end_re[s : s + 1]
        run_im = prod[s : s + 1] * turned_im + end_im[s : s + 1]
        run = run * prod[s : s + 1]
    totals[0] = jnp.zeros_like(prod)
    totals[0, 0:1, :] = run
    totals[0, 1:2, :] = run_re
    totals[0, 2:3, :] = run_im


def project_body(
    steps, chans, tokens, gain, w, bound, angles, normed, pre, pre_out, local, decays, prefix, totals, carry
):
    t = pl.program_id(1)

    @pl.when(t == 0)
    def _():
        carry[0:2] = jnp.zeros((2,) + carry.shape[1:], F32)
        carry[2] = jnp.ones(carry.shape[1:], F32)

    values = tokens[...].astype(F32)
    unit = (values * rms_rows(values) * gain[...]).astype(BF16)
    normed[...] = unit
    low = bound[0:1, :]
    scan = nt(unit, w[4 * chans : 7 * chans, :])
    pre[...] = scan
    decay = low + (1.0 - low) * sigmoid(scan[:, 2 * chans :])
    decays[...] = decay
    in_re, in_im = scan[:, 0:chans], scan[:, chans : 2 * chans]
    local[:, 0:chans] = (1.0 - decay) * (in_re * sigmoid(in_re))
    local[:, chans:] = (1.0 - decay) * (in_im * sigmoid(in_im))
    pre_out[...] = nt(unit, w[2 * chans : 4 * chans, :])
    cos_one, sin_one = angles[0:1, :], angles[1:2, :]

    def step(j, state):
        state_re, state_im, prod = state
        rows = step_rows(j)
        decay = decays[rows, :]
        turned_re, turned_im = turn(cos_one, sin_one, state_re, state_im)
        state_re = decay * turned_re + local[rows, 0:chans]
        state_im = decay * turned_im + local[rows, chans:]
        local[rows, 0:chans] = state_re
        local[rows, chans:] = state_im
        return state_re, state_im, prod * decay

    end_re, end_im, prod = lax.fori_loop(
        0, steps, step, (carry[0], carry[1], carry[2]), unroll=8
    )
    carry[0], carry[1], carry[2] = end_re, end_im, prod

    @pl.when(t == pl.num_programs(1) - 1)
    def _():
        chain_chunks(range(CHUNKS), turn, angles, prod, end_re, end_im, prefix, totals)


def project(tokens, gain, w, bound, angles, groups, chans):
    rows, width = tokens.shape
    per = rows // groups
    tile = min(TILE, per)
    tiles = per // tile
    rowed = functools.partial(ahead, tiles, tile)
    return kernel_call(
        functools.partial(project_body, tile // CHUNKS, chans),
        (groups, tiles),
        [rowed(width), whole((1, width)), whole(w.shape), whole((1, chans)), whole(angles.shape)],
        [
            rowed(width),
            rowed(3 * chans),
            rowed(2 * chans),
            rowed(2 * chans),
            rowed(chans),
            per_group((1, 3, CHUNKS, chans)),
            per_group((1, CHUNKS, chans)),
        ],
        [
            shaped((rows, width), BF16),
            shaped((rows, 3 * chans)),
            shaped((rows, 2 * chans)),
            Near(shaped((rows, 2 * chans))),
            shaped((rows, chans)),
            shaped((groups, 3, CHUNKS, chans)),
            shaped((groups, CHUNKS, chans)),
        ],
        [pltpu.VMEM((3, CHUNKS, chans), F32)],
    )(tokens, gain, w, bound, angles)


def mix_body(
    steps,
    chans,
    blocks,
    me,
    keep,
    gathered,
    local,
    decays,
    prefix,
    angles,
    table,
    pre_out,
    tokens,
    w_out,
    out_gain,
    ffn_gain,
    states,
    entering,
    gated,
    mix_out,
    mid,
    ffn_normed,
    carry,
):
    g, t = pl.program_id(0), pl.program_id(1)

    @pl.when(t == 0)
    def _():
        cos_dev, sin_dev = angles[4:5, :], angles[5:6, :]
        state_re = jnp.zeros((1, chans), F32)
        state_im = jnp.zeros((1, chans), F32)
        for d in range(blocks):
            kept_one = keep[g, d]
            turned_re, turned_im = turn(cos_dev, sin_dev, kept_one * state_re, kept_one * state_im)
            decay = gathered[d, 0, 0:1, :]
            earlier = d < me[0]
            state_re = jnp.where(earlier, decay * turned_re + gathered[d, 0, 1:2, :], state_re)
            state_im = jnp.where(earlier, decay * turned_im + gathered[d, 0, 2:3, :], state_im)
        kept_one = keep[g, me[0]]
        state_re, state_im = kept_one * state_re, kept_one * state_im
        cos_chunk, sin_chunk = angles[2:3, :], angles[3:4, :]
        for s in range(CHUNKS):
            run = prefix[0, 0, s : s + 1, :]
            entering[0, 0, s : s + 1, :] = run * state_re + prefix[0, 1, s : s + 1, :]
            entering[0, 1, s : s + 1, :] = run * state_im + prefix[0, 2, s : s + 1, :]
            state_re, state_im = turn(cos_chunk, sin_chunk, state_re, state_im)
        carry[...] = jnp.ones_like(carry)

    enter_re, enter_im = entering[0, 0], entering[0, 1]

    def step(j, prod):
        rows = step_rows(j)
        prod = prod * decays[rows, :]
        lag = pl.ds(t * steps + j, 1)
        turned_re, turned_im = turn(table[lag, 0:chans], table[lag, chans:], enter_re, enter_im)
        states[rows, 0:chans] = local[rows, 0:chans] + prod * turned_re
        states[rows, chans:] = local[rows, chans:] + prod * turned_im
        return prod

    carry[...] = lax.fori_loop(0, steps, step, carry[...], unroll=8)
    state = states[...]
    inv_rms = rms_rows(state)
    gate = pre_out[...]
    gate_in = (state * out_gain[...] * (gate * sigmoid(gate))).astype(BF16)
    gated[...] = gate_in
    mixed = nn(gate_in, w_out[...])
    mix_out[...] = mixed
    stream = tokens[...].astype(F32) + inv_rms * mixed
    mid[...] = stream
    ffn_normed[...] = (stream * rms_rows(stream) * ffn_gain[...]).astype(BF16)


def mix(
    me, keep, gathered, local, decays, prefix, angles, table, pre_out, tokens, w, out_gain, ffn_gain, groups, chans
):
    rows, width = tokens.shape
    per = rows // groups
    tile = min(TILE, per)
    tiles = per // tile
    blocks = gathered.shape[0]
    rowed = functools.partial(ahead, tiles, tile)
    return kernel_call(
        functools.partial(mix_body, tile // CHUNKS, chans, blocks),
        (groups, tiles),
        [
            SMEM_SPEC,
            SMEM_SPEC,
            pl.BlockSpec((blocks, 1, CHUNKS, chans), lambda g, t: (0, g, 0, 0)),
            rowed(2 * chans),
            rowed(chans),
            per_group((1, 3, CHUNKS, chans)),
            whole(angles.shape),
            whole(table.shape),
            rowed(2 * chans),
            rowed(width),
            whole((2 * chans, width)),
            whole((1, 2 * chans)),
            whole((1, width)),
        ],
        [
            rowed(2 * chans),
            per_group((1, 2, CHUNKS, chans)),
            rowed(2 * chans),
            rowed(width),
            rowed(width),
            rowed(width),
        ],
        [
            shaped((rows, 2 * chans)),
            shaped((groups, 2, CHUNKS, chans)),
            shaped((rows, 2 * chans), BF16),
            shaped((rows, width)),
            shaped((rows, width)),
            Near(shaped((rows, width), BF16)),
        ],
        [pltpu.VMEM((CHUNKS, chans), F32)],
    )(me, keep, gathered, Near(local), decays, prefix, angles, table, pre_out, tokens, w, out_gain, ffn_gain)


def split_by_core(first, grads, span, unit, same, other):
    for chip in range(span // (2 * unit)):
        for k, part in enumerate(grads):
            even = part[2 * chip * unit : (2 * chip + 1) * unit]
            odd = part[(2 * chip + 1) * unit : (2 * chip + 2) * unit]
            rows = slice(k * unit, (k + 1) * unit)
            same[chip, rows, :] = jnp.where(first, even, odd)
            other[chip, rows, :] = jnp.where(first, odd, even)


def swiglu_body(unit, tile, x, up, w, act, d_pre, grads):
    devices = w.shape[0]

    def every(part):
        return jnp.concatenate([w[dev, part] for dev in range(devices)], axis=0)

    span = devices * unit
    w_pre = jnp.concatenate([every(0), every(1)], axis=0)
    w_down = every(2)
    for start in range(0, x.shape[0], tile):
        rows = slice(start, start + tile)
        pre = nt(x[rows, :], w_pre)
        d_hidden = nt(up[rows, :], w_down)
        gate, lift = pre[:, :span], pre[:, span:]
        sigma = sigmoid(gate)
        silu = gate * sigma
        act[rows, :] = (silu * lift).astype(BF16)
        d_pre[rows, :span] = (d_hidden * lift * (sigma + silu * (1.0 - sigma))).astype(BF16)
        d_pre[rows, span:] = (d_hidden * silu).astype(BF16)
    g_pre = tn(d_pre[...], x[...]).astype(BF16)
    g_down = tn(act[...], up[...]).astype(BF16)
    for dev in range(devices):
        own = slice(dev * unit, (dev + 1) * unit)
        grads[dev, 0:unit, :] = g_pre[own]
        grads[dev, unit : 2 * unit, :] = g_pre[span + dev * unit : span + (dev + 1) * unit]
        grads[dev, 2 * unit : 3 * unit, :] = g_down[own]


def units_at_once(blocks, unit):
    devices = 2
    while devices < blocks and (devices * unit % 128 or devices * unit < 384):
        devices *= 2
    return devices


def swiglu(x, up, w):
    rows, width = x.shape
    blocks, _, unit, _ = w.shape
    devices = units_at_once(blocks, unit)
    span = devices * unit
    return kernel_call(
        functools.partial(swiglu_body, unit, min(rows, 512)),
        (blocks // devices,),
        [
            whole((rows, width)),
            whole((rows, width)),
            pl.BlockSpec((devices, 3, unit, width), lambda q: (q, 0, 0, 0)),
        ],
        [
            pl.BlockSpec((rows, span), lambda q: (0, q)),
            pl.BlockSpec((rows, 2 * span), lambda q: (0, q)),
            pl.BlockSpec((devices, 3 * unit, width), lambda q: (q, 0, 0)),
        ],
        [
            shaped((rows, blocks * unit), BF16),
            Near(shaped((rows, 2 * blocks * unit), BF16)),
            shaped((blocks, 3 * unit, width), BF16),
        ],
    )(Near(x), up, w)


def finish_grads(core, acc, kinds, chans, unit, same, other):
    if unit % 16:
        same[...] = acc[...].astype(BF16)
        other[...] = jnp.zeros_like(other)
        return
    grads = [acc[k * chans : (k + 1) * chans, :].astype(BF16) for k in range(kinds)]
    split_by_core(core[0] == 0, grads, chans, unit, same, other)


def grads_shapes(kinds, chans, unit, width):
    if unit % 16:
        return [(kinds * chans, width), (16, width)]
    return [(chans // (2 * unit), kinds * unit, width)] * 2


def first_step():
    return jnp.logical_and(pl.program_id(0) == 0, pl.program_id(1) == 0)


def last_step():
    return jnp.logical_and(
        pl.program_id(0) == pl.num_programs(0) - 1, pl.program_id(1) == pl.num_programs(1) - 1
    )


def mix_back_body(steps, chans, unit_chans, parts, core, *refs):
    d_pres, refs = refs[:parts], refs[parts:]
    (
        w_ffn,
        mid,
        upstream,
        mix_out,
        states,
        pre_out,
        gated,
        normed,
        decays,
        w_out,
        out_gain,
        ffn_gain,
        angles,
        d_mid,
        d_outgate,
        local,
        suffix,
        totals,
        same,
        other,
        sums,
        acc,
        w_pre,
        carry,
    ) = refs
    blocks, _, units, _ = w_ffn.shape
    unit = units // parts
    devices = units_at_once(blocks, unit)

    @pl.when(first_step())
    def _():
        acc[...] = jnp.zeros_like(acc)
        sums[...] = jnp.zeros_like(sums)
        at = 0
        for part in range(parts):
            for q in range(0, blocks, devices):
                for kind in (0, 1):
                    for dev in range(q, q + devices):
                        w_pre[at : at + unit, :] = w_ffn[dev, kind, part * unit : (part + 1) * unit, :]
                        at += unit

    @pl.when(pl.program_id(1) == 0)
    def _():
        carry[0:2] = jnp.zeros((2,) + carry.shape[1:], F32)
        carry[2] = jnp.ones(carry.shape[1:], F32)

    span = 2 * units * blocks // parts
    d_norm = nn(d_pres[0][...], w_pre[0:span, :])
    for part in range(1, parts):
        d_norm += nn(d_pres[part][...], w_pre[part * span : (part + 1) * span, :])
    stream = mid[...]
    inv_mid = rms_rows(stream)
    unit_mid = stream * inv_mid
    sums[0:1, :] += jnp.sum(d_norm * unit_mid, axis=0, keepdims=True)
    d_stream = upstream[...].astype(F32) + rms_pull(unit_mid, inv_mid, ffn_gain[...], d_norm)
    d_mid[...] = d_stream
    state = states[...]
    inv_rms = rms_rows(state)
    d_mix = (inv_rms * d_stream).astype(BF16)
    d_rms = jnp.sum(d_stream * mix_out[...], axis=-1, keepdims=True)
    d_square = (-0.5 / chans) * inv_rms * inv_rms * inv_rms * d_rms
    d_gated = nt(d_mix, w_out[...])
    gate = pre_out[...]
    sigma = sigmoid(gate)
    silu = gate * sigma
    gain = out_gain[...]
    local[...] = d_gated * gain * silu + d_square * state
    d_state_gate = d_gated * state
    sums[1:2, :] += jnp.sum(d_state_gate * silu, axis=0, keepdims=True)
    d_gate = (d_state_gate * gain * (sigma + silu * (1.0 - sigma))).astype(BF16)
    d_outgate[...] = d_gate
    acc[0 : 2 * chans, :] += tn(gated[...], d_mix)
    acc[2 * chans : 4 * chans, :] += tn(d_gate, normed[...])
    cos_one, sin_one = angles[0:1, :], angles[1:2, :]

    def step(i, flow):
        flow_re, flow_im, prod = flow
        rows = step_rows(steps - 1 - i)
        grad_re = local[rows, 0:chans] + flow_re
        grad_im = local[rows, chans:] + flow_im
        local[rows, 0:chans] = grad_re
        local[rows, chans:] = grad_im
        decay = decays[rows, :]
        turned_re, turned_im = back_turn(cos_one, sin_one, grad_re, grad_im)
        return decay * turned_re, decay * turned_im, prod * decay

    end_re, end_im, prod = lax.fori_loop(
        0, steps, step, (carry[0], carry[1], carry[2]), unroll=8
    )
    carry[0], carry[1], carry[2] = end_re, end_im, prod

    @pl.when(pl.program_id(1) == pl.num_programs(1) - 1)
    def _():
        chain_chunks(reversed(range(CHUNKS)), back_turn, angles, prod, end_re, end_im, suffix, totals)

    @pl.when(last_step())
    def _():
        finish_grads(core, acc, 4, chans, unit_chans, same, other)


def mix_back(
    core,
    unit_chans,
    d_pres,
    w_ffn,
    mid,
    upstream,
    mix_out,
    states,
    pre_out,
    gated,
    normed,
    decays,
    w,
    out_gain,
    ffn_gain,
    angles,
    groups,
    chans,
):
    rows, width = mid.shape
    per = rows // groups
    tile = min(TILE, per)
    tiles = per // tile
    blocks, _, units, _ = w_ffn.shape
    parts = len(d_pres)
    rowed = functools.partial(behind, tiles, tile)
    return kernel_call(
        functools.partial(mix_back_body, tile // CHUNKS, chans, unit_chans, parts),
        (groups, tiles),
        [SMEM_SPEC]
        + [rowed(part.shape[1]) for part in d_pres]
        + [
            whole((blocks, 2, units, width)),
            rowed(width),
            rowed(width),
            rowed(width),
            rowed(2 * chans),
            rowed(2 * chans),
            rowed(2 * chans),
            rowed(width),
            rowed(chans),
            whole((2 * chans, width)),
            whole((1, 2 * chans)),
            whole((1, width)),
            whole(angles.shape),
        ],
        [
            rowed(width),
            rowed(2 * chans),
            rowed(2 * chans),
            per_group((1, 3, CHUNKS, chans)),
            per_group((1, CHUNKS, chans)),
            *map(kept, grads_shapes(4, chans, unit_chans, width)),
            kept((8, width)),
        ],
        [
            shaped((rows, width)),
            shaped((rows, 2 * chans), BF16),
            Near(shaped((rows, 2 * chans))),
            shaped((groups, 3, CHUNKS, chans)),
            shaped((groups, CHUNKS, chans)),
            *(shaped(shape, BF16) for shape in grads_shapes(4, chans, unit_chans, width)),
            shaped((8, width)),
        ],
        [
            pltpu.VMEM((4 * chans, width), F32),
            pltpu.VMEM((2 * blocks * units, width), BF16),
            pltpu.VMEM((3, CHUNKS, chans), F32),
        ],
        vmem=46,
    )(
        core,
        *map(Near, d_pres),
        w_ffn,
        mid,
        upstream,
        mix_out,
        states,
        pre_out,
        gated,
        normed,
        decays,
        w,
        out_gain,
        ffn_gain,
        angles,
    )


def silu_slope(values, sigma):
    return sigma * (1.0 + values * (1.0 - sigma))


def adjoint_finish_body(
    steps,
    chans,
    blocks,
    unit_chans,
    me,
    core,
    keep,
    gathered,
    local,
    decays,
    suffix,
    pre,
    states,
    before,
    entering,
    bound,
    angles,
    table,
    normed,
    d_pre,
    sums,
    same,
    other,
    leaving,
    full,
    acc,
    carry,
):
    g, t = pl.program_id(0), pl.program_id(1)
    tiles = pl.num_programs(1)

    @pl.when(first_step())
    def _():
        acc[...] = jnp.zeros_like(acc)

    @pl.when(t == 0)
    def _():
        cos_chunk, sin_chunk = angles[2:3, :], angles[3:4, :]
        cos_dev, sin_dev = angles[4:5, :], angles[5:6, :]
        flow_re = jnp.zeros((1, chans), F32)
        flow_im = jnp.zeros((1, chans), F32)
        for d in reversed(range(blocks)):
            kept_one = keep[g, d]
            turned_re, turned_im = back_turn(cos_dev, sin_dev, flow_re, flow_im)
            decay = gathered[d, 0, 0:1, :]
            later = d > me[0]
            flow_re = jnp.where(
                later, kept_one * (decay * turned_re + gathered[d, 0, 1:2, :]), flow_re
            )
            flow_im = jnp.where(
                later, kept_one * (decay * turned_im + gathered[d, 0, 2:3, :]), flow_im
            )
        for s in reversed(range(CHUNKS)):
            run = suffix[0, 0, s : s + 1, :]
            leaving[0, s : s + 1, :] = run * flow_re + suffix[0, 1, s : s + 1, :]
            leaving[1, s : s + 1, :] = run * flow_im + suffix[0, 2, s : s + 1, :]
            flow_re, flow_im = back_turn(cos_chunk, sin_chunk, flow_re, flow_im)
        carry[...] = jnp.ones_like(carry)
        sums[...] = jnp.zeros_like(sums)

    low = bound[0:1, :]
    cos_one, sin_one = angles[0:1, :], angles[1:2, :]
    leave_re, leave_im = leaving[0], leaving[1]

    def step(i, prod):
        rows = step_rows(steps - 1 - i)
        lag = pl.ds(t * steps + i, 1)
        turned_re, turned_im = back_turn(table[lag, 0:chans], table[lag, chans:], leave_re, leave_im)
        full[rows, 0:chans] = local[rows, 0:chans] + prod * turned_re
        full[rows, chans:] = local[rows, chans:] + prod * turned_im
        return prod * decays[rows, :]

    carry[...] = lax.fori_loop(0, steps, step, carry[...], unroll=8)
    first_tile = t == tiles - 1
    last_re = jnp.where(first_tile, entering[0, 0], before[:, 0:chans])
    last_im = jnp.where(first_tile, entering[0, 1], before[:, chans:])
    if steps > 1:
        rows = slice(0, (steps - 1) * CHUNKS)
        last_re = jnp.concatenate([last_re, states[rows, 0:chans]], axis=0)
        last_im = jnp.concatenate([last_im, states[rows, chans:]], axis=0)
    grad_re, grad_im = full[:, 0:chans], full[:, chans:]
    in_re, in_im = pre[:, 0:chans], pre[:, chans : 2 * chans]
    sigma_re, sigma_im = sigmoid(in_re), sigmoid(in_im)
    sigma = sigmoid(pre[:, 2 * chans :])
    decay = decays[...]
    cross_re = grad_re * last_re + grad_im * last_im
    cross_im = grad_im * last_re - grad_re * last_im
    along, across = back_turn(cos_one, sin_one, cross_re, cross_im)
    d_decay = along - (grad_re * in_re * sigma_re + grad_im * in_im * sigma_im)
    rest = 1.0 - decay
    d_low = d_decay * (1.0 - sigma)
    d_re = (grad_re * rest * silu_slope(in_re, sigma_re)).astype(BF16)
    d_im = (grad_im * rest * silu_slope(in_im, sigma_im)).astype(BF16)
    d_forget = (d_low * (1.0 - low) * sigma).astype(BF16)
    d_pre[:, 0:chans] = d_re
    d_pre[:, chans : 2 * chans] = d_im
    d_pre[:, 2 * chans :] = d_forget
    sums[0, 0] += jnp.sum((decay * across).reshape(steps, CHUNKS, chans), axis=0)
    sums[0, 1] += jnp.sum(d_low.reshape(steps, CHUNKS, chans), axis=0)
    acc[...] += tn(d_pre[...], normed[...])

    @pl.when(last_step())
    def _():
        finish_grads(core, acc, 3, chans, unit_chans, same, other)


def adjoint_finish(
    unit_chans,
    me,
    core,
    keep,
    gathered,
    local,
    decays,
    suffix,
    pre,
    states,
    entering,
    bound,
    angles,
    table,
    normed,
    groups,
    chans,
):
    rows, width = normed.shape
    per = rows // groups
    tile = min(TILE, per)
    tiles = per // tile
    steps = tile // CHUNKS
    blocks = gathered.shape[0]
    rowed = functools.partial(behind, tiles, tile)

    def one_before(g, t):
        return (jnp.maximum((g * tiles + tiles - 1 - t) * steps - 1, 0), 0)

    return kernel_call(
        functools.partial(adjoint_finish_body, steps, chans, blocks, unit_chans),
        (groups, tiles),
        [
            SMEM_SPEC,
            SMEM_SPEC,
            SMEM_SPEC,
            pl.BlockSpec((blocks, 1, CHUNKS, chans), lambda g, t: (0, g, 0, 0)),
            rowed(2 * chans),
            rowed(chans),
            per_group((1, 3, CHUNKS, chans)),
            rowed(3 * chans),
            rowed(2 * chans),
            pl.BlockSpec((CHUNKS, 2 * chans), one_before),
            per_group((1, 2, CHUNKS, chans)),
            whole((1, chans)),
            whole(angles.shape),
            whole(table.shape),
            rowed(width),
        ],
        [
            rowed(3 * chans),
            per_group((1, 2, CHUNKS, chans)),
            *map(kept, grads_shapes(3, chans, unit_chans, width)),
        ],
        [
            Near(shaped((rows, 3 * chans), BF16)),
            shaped((groups, 2, CHUNKS, chans)),
            *(shaped(shape, BF16) for shape in grads_shapes(3, chans, unit_chans, width)),
        ],
        [
            pltpu.VMEM((2, CHUNKS, chans), F32),
            pltpu.VMEM((tile, 2 * chans), F32),
            pltpu.VMEM((3 * chans, width), F32),
            pltpu.VMEM((CHUNKS, chans), F32),
        ],
    )(
        me,
        core,
        keep,
        gathered,
        Near(local),
        decays,
        suffix,
        pre,
        states,
        states,
        entering,
        bound,
        angles,
        table,
        normed,
    )


def tokens_back_body(chans, d_scan, d_outgate, w, tokens, d_mid, gain, early, scan, grad_tokens, sums):
    @pl.when(first_step())
    def _():
        sums[...] = jnp.zeros_like(sums)
        sums[1:3, :] = early[0:2, :]
        sums[3:4, 0:chans] = jnp.sum(scan[:, 0], axis=(0, 1))[None]
        sums[3:4, chans : 2 * chans] = jnp.sum(scan[:, 1], axis=(0, 1))[None]

    d_normed = nn(d_scan[...], w[4 * chans : 7 * chans, :])
    d_normed += nn(d_outgate[...], w[2 * chans : 4 * chans, :])
    values = tokens[...].astype(F32)
    inv = rms_rows(values)
    unit = values * inv
    sums[0:1, :] += jnp.sum(d_normed * unit, axis=0, keepdims=True)
    grad_tokens[...] = (d_mid[...] + rms_pull(unit, inv, gain[...], d_normed)).astype(BF16)


def tokens_back(d_scan, d_outgate, w, tokens, d_mid, gain, early, scan, groups, chans):
    rows, width = tokens.shape
    per = rows // groups
    tile = min(TILE, per)
    tiles = per // tile
    rowed = functools.partial(ahead, tiles, tile)
    return kernel_call(
        functools.partial(tokens_back_body, chans),
        (groups, tiles),
        [
            rowed(3 * chans),
            rowed(2 * chans),
            whole(w.shape),
            rowed(width),
            rowed(width),
            whole((1, width)),
            whole(early.shape),
            whole(scan.shape),
        ],
        [rowed(width), kept((8, width))],
        [Near(shaped((rows, width), BF16)), shaped((8, width))],
        vmem=20,
    )(Near(d_scan), d_outgate, w, tokens, d_mid, gain, early, scan)


def result_body(parts, *refs):
    acts, (w_down, mid, result) = refs[:parts], refs[parts:]
    blocks, _, units, _ = w_down.shape
    unit = units // parts
    total = mid[...]
    for part, act in enumerate(acts):
        rows = slice(part * unit, (part + 1) * unit)
        total += nn(
            act[...], jnp.concatenate([w_down[dev, 0, rows, :] for dev in range(blocks)], axis=0)
        )
    result[...] = total.astype(BF16)


def block_result(acts, w_ffn, mid):
    rows, width = mid.shape
    blocks, _, units, _ = w_ffn.shape
    tile = min(TILE, rows)

    def rowed(wide):
        return pl.BlockSpec((tile, wide), lambda i: (i, 0))

    return kernel_call(
        functools.partial(result_body, len(acts)),
        (rows // tile,),
        [rowed(act.shape[1]) for act in acts]
        + [whole((blocks, 1, units, width), (0, 2, 0, 0)), rowed(width)],
        rowed(width),
        Near(shaped((rows, width), BF16)),
        vmem=20,
    )(*acts, w_ffn, mid)


def swap(values, axis, bit, size):
    return lax.ppermute(values, axis, [(i, i ^ bit) for i in range(size)])


def joined(*parts):
    return sum(part.astype(F32) for part in parts)


def pick(values, index, axis):
    return lax.dynamic_index_in_dim(values, index, axis, keepdims=False)


def gather_pieces(shard, size):
    half = shard.shape[0] // 2
    near_x = swap(shard, "mp", 2, size)
    near_y = swap(shard, "mp", 4, size)
    core = swap(shard, "mp", 1, size)
    far_one = swap(near_x[:half], "mp", 4, size)
    far_two = swap(near_y[half:], "mp", 2, size)
    core_x = swap(near_x, "mp", 1, size)
    core_y = swap(near_y, "mp", 1, size)
    far = jnp.concatenate([far_one, far_two], axis=0)
    core_far = swap(far, "mp", 1, size)
    return shard, core, near_x, core_x, near_y, core_y, far, core_far


def reduce_mp(grads):
    return lax.psum_scatter(grads, "mp", scatter_dimension=0, tiled=False)


def sends_body(chip, same, got, out_x, out_y, out_far):
    for b, out in ((1, out_x), (2, out_y), (3, out_far)):
        at = chip[0] ^ b
        out[...] = (same[at].astype(F32) + got[at].astype(F32)).astype(BF16)


def sends(chip, same, got):
    return pl.pallas_call(
        sends_body,
        in_specs=[SMEM_SPEC, VMEM_SPEC, VMEM_SPEC],
        out_specs=[VMEM_SPEC] * 3,
        out_shape=[jax.ShapeDtypeStruct(same.shape[1:], BF16)] * 3,
        cost_estimate=pl.CostEstimate(flops=1, bytes_accessed=1, transcendentals=0),
        compiler_params=pltpu.CompilerParams(vmem_limit_bytes=16 * MIB),
    )(chip, same, got)


class Reduction:
    def __init__(self, same, other, chip, size, layers):
        self.same, self.chip, self.size, self.layers = same, chip, size, layers
        self.flying = [swap(other, "mp", 1, size)]

    def arrived(self, *others):
        count = len(self.flying)
        both = tied(*self.flying, *others)
        self.flying = both[:count]
        return both[count:] if len(others) > 1 else both[-1]

    def to_chips(self, other):
        self.got = self.flying[0]
        *parts, other = tied(*sends(self.chip, self.same, self.got), other)
        self.flying = [swap(part, "mp", 2 * b, self.size) for b, part in zip((1, 2, 3), parts)]
        return other

    def share_here(self):
        at = self.chip[0]
        mine = pick(self.same, at, 0), pick(self.got, at, 0)
        return joined(*mine, *self.flying).astype(BF16)

    def to_layer(self, number, other):
        if number == 1:
            self.share = self.share_here()
        else:
            self.share = joined(self.share, *self.flying).astype(BF16)
        self.share, other = tied(self.share, other)
        self.flying = [swap(self.share, "dp", number, self.layers)]
        return other

    def total(self):
        return joined(self.share, *self.flying).astype(BF16).astype(F32)


def assemble_body(kinds, size, me, *refs):
    out, extra = refs[-2:]
    for b, ref in enumerate(refs[:-2]):
        d = me[0] ^ b
        for k in range(kinds):
            out[k, d] = ref[k * size : (k + 1) * size, :]
        extra[d] = ref[kinds * size :, :]


def assemble(me, pieces, kinds, size):
    rows, width = pieces[0].shape
    vmem = VMEM_SPEC
    return pl.pallas_call(
        functools.partial(assemble_body, kinds, size),
        in_specs=[SMEM_SPEC] + [vmem] * len(pieces),
        out_specs=[vmem, vmem],
        out_shape=[
            jax.ShapeDtypeStruct((kinds, len(pieces), size, width), BF16),
            jax.ShapeDtypeStruct((len(pieces), rows - kinds * size, width), BF16),
        ],
        cost_estimate=pl.CostEstimate(flops=1, bytes_accessed=1, transcendentals=0),
        compiler_params=pltpu.CompilerParams(vmem_limit_bytes=16 * MIB),
    )(me, *pieces)


def split_three(values):
    one = lax.reduce_precision(values, 8, 7)
    two = lax.reduce_precision(values - one, 8, 7)
    three = values - one - two
    return jnp.stack([one, two, three], axis=0).astype(BF16)


def tied(*values):
    return lax.optimization_barrier(values)


def shards(
    tokens,
    upstream,
    pieces,
    layer_index,
    mix_gain,
    w_input,
    w_forget,
    w_outgate,
    phase_angle,
    lower_logits,
    out_gain,
    w_output,
    ffn_gain,
    w_gate,
    w_up,
    w_down,
):
    rows_dev, groups, width = tokens.shape
    blocks = lax.axis_size("mp")
    me = lax.axis_index("mp")
    layers_z = lax.axis_size("dp")
    seq_len = rows_dev * blocks
    chans_dev = w_input.shape[2]
    chans = chans_dev * blocks
    units_dev = w_gate.shape[1]
    units = units_dev * blocks
    steps = rows_dev // CHUNKS
    rows = rows_dev * groups

    def to_rows(values):
        return jnp.transpose(
            values.reshape(CHUNKS, steps, groups, width), (2, 1, 0, 3)
        ).reshape(rows, width)

    def from_rows(values):
        return jnp.transpose(
            values.reshape(groups, steps, CHUNKS, width), (2, 1, 0, 3)
        ).reshape(rows_dev, groups, width)

    me_one = me[None].astype(jnp.int32)
    layer_mask = (jnp.arange(lower_logits.shape[0], dtype=jnp.int32) < layer_index[0]).astype(F32)
    soft = jax.nn.softmax(lower_logits, axis=0)
    bound_own = jnp.sum(soft * layer_mask[:, None], axis=0)
    small = jnp.concatenate([bound_own[None], phase_angle[None], out_gain], axis=0)
    mix_shard = jnp.concatenate(
        [
            w_output,
            jnp.transpose(w_outgate, (1, 2, 0)),
            jnp.transpose(w_input, (1, 2, 0)),
            jnp.transpose(w_forget)[None],
        ],
        axis=0,
    ).reshape(7 * chans_dev, width)
    if blocks == 8 and 4 * chans_dev <= width:
        terms = split_three(small.reshape(1, -1)).reshape(3, 4 * chans_dev)
        terms = jnp.pad(terms, ((0, 13), (0, width - 4 * chans_dev)))
        pieces_w = gather_pieces(jnp.concatenate([mix_shard, terms], axis=0), blocks)
        w_mix, extra = assemble(me_one, pieces_w, 7, chans_dev)
        small = jnp.sum(extra[:, 0:3, 0 : 4 * chans_dev].astype(F32), axis=1)
        small = small.reshape(blocks, 4, chans_dev)
    else:
        w_mix = lax.all_gather(mix_shard.reshape(7, chans_dev, width), "mp", axis=0)
        w_mix = jnp.transpose(w_mix, (1, 0, 2, 3))
        small = lax.all_gather(small, "mp", axis=0)
    w_mix = w_mix.reshape(7 * chans, width)
    ffn_shard = jnp.concatenate([jnp.transpose(w_gate), jnp.transpose(w_up), w_down], axis=0)
    w_ffn = lax.all_gather(ffn_shard, "mp", axis=0)

    small = jnp.transpose(small, (1, 0, 2)).reshape(4, chans)
    bound = small[0:1]
    phase = small[1:2]
    gain_row = small[2:4].reshape(1, 2 * chans)
    spans = phase * jnp.array([[1.0], [steps], [rows_dev]], F32)
    angles = jnp.stack([jnp.cos(spans), jnp.sin(spans)], axis=1).reshape(6, chans)
    lags = phase * jnp.arange(steps + 1, dtype=F32)[:, None]
    table = jnp.concatenate([jnp.cos(lags), jnp.sin(lags)], axis=1)
    starts = jnp.arange(blocks, dtype=jnp.int32) * rows_dev
    keep = (starts[None, :] % (seq_len // pieces)[:, None] != 0).astype(F32)

    tok = to_rows(tokens)
    up_rows = to_rows(upstream)
    mix_row, ffn_row = mix_gain[None], ffn_gain[None]
    normed, pre, pre_out, local, decays, prefix, totals = project(
        tok, mix_row, w_mix, bound, angles, groups, chans
    )
    ends = lax.all_gather(totals, "mp", axis=0)
    states, entering, gated, mix_out, mid, ffn_normed = mix(
        me_one,
        keep,
        ends,
        local,
        decays,
        prefix,
        angles,
        table[1:],
        pre_out,
        tok,
        w_mix,
        gain_row,
        ffn_row,
        groups,
        chans,
    )
    by_hand = blocks == 8 and layers_z == 4
    core = (me & 1) if by_hand else jnp.zeros_like(me)
    core_one = core[None].astype(jnp.int32)
    chip_one = (me >> 1)[None].astype(jnp.int32)
    w_ffn = w_ffn.reshape(blocks, 3, units_dev, width)

    def reduction(same, other):
        return Reduction(same, other, chip_one, blocks, layers_z)

    act, d_pre, grad_ffn = swiglu(ffn_normed, up_rows, w_ffn)
    grad_ffn = lax.psum(reduce_mp(grad_ffn), "dp")
    acts, d_pres = [act], [d_pre]
    d_mid, d_outgate, back_local, suffix, back_totals, same, other, early_sums = mix_back(
        core_one,
        chans_dev,
        d_pres,
        w_ffn,
        mid,
        up_rows,
        mix_out,
        states,
        pre_out,
        gated,
        normed,
        decays,
        w_mix,
        gain_row,
        ffn_row,
        angles,
        groups,
        chans,
    )
    if by_hand:
        early = reduction(same, other)
    else:
        early = jnp.moveaxis(same.reshape(4, blocks, chans_dev, width), 1, 0)
    back_ends = lax.all_gather(back_totals, "mp", axis=0)
    if by_hand:
        back_ends = early.to_chips(early.arrived(back_ends))
    d_scan, sums, same, other = adjoint_finish(
        chans_dev,
        me_one,
        core_one,
        keep,
        back_ends,
        back_local,
        decays,
        suffix,
        pre,
        states,
        entering,
        bound,
        angles,
        table[:-1],
        normed,
        groups,
        chans,
    )
    if by_hand:
        other, d_scan = early.arrived(other, d_scan)
        late = reduction(same, other)
        d_scan = early.to_layer(1, d_scan)
        mid, d_scan = tied(mid, d_scan)
        result = block_result(acts, w_ffn, mid)
        d_scan = late.to_chips(late.arrived(d_scan, result)[0])
    else:
        late = jnp.moveaxis(same.reshape(3, blocks, chans_dev, width), 1, 0)
    grad_tokens, flat = tokens_back(
        d_scan, d_outgate, w_mix, tok, d_mid, mix_row, early_sums, sums, groups, chans
    )
    if by_hand:
        flat = early.to_layer(2, early.arrived(flat))
    else:
        early = lax.psum(reduce_mp(early.reshape(blocks, -1, width)), "dp").astype(F32)
        late = lax.psum(reduce_mp(late.reshape(blocks, -1, width)), "dp").astype(F32)
    if by_hand:
        flat = flat + swap(flat, "mp", 1, blocks)
        out_tokens, out_result = from_rows(grad_tokens), from_rows(result)
        flat, out_tokens, out_result = late.arrived(flat, out_tokens, out_result)
        flat = late.to_layer(1, flat)
        flat = flat + swap(flat, "mp", 2, blocks)
        flat = flat + swap(flat, "mp", 4, blocks)
        flat = late.to_layer(2, late.arrived(flat))
        flat = flat + swap(flat, "dp", 1, layers_z)
        flat = flat + swap(flat, "dp", 2, layers_z)
        early, late = early.total(), late.total()
    else:
        flat = lax.psum(flat, ("dp", "mp"))
        out_tokens, out_result = from_rows(grad_tokens), from_rows(block_result(acts, w_ffn, mid))
    grad_ffn = grad_ffn.astype(F32).reshape(3, units_dev, width)
    early = early.reshape(4, chans_dev, width)
    late = late.reshape(3, chans_dev, width)
    own = me * chans_dev

    def own_part(row, offset):
        return lax.dynamic_slice(flat, (row, offset * chans + own), (1, chans_dev))[0]

    grad_gain = jnp.stack([own_part(2, 0), own_part(2, 1)], axis=0)
    d_bound = own_part(3, 1)
    grad_lower = soft * (layer_mask[:, None] - bound_own[None]) * d_bound[None]
    return (
        out_result,
        out_tokens,
        flat[0],
        jnp.transpose(late[0:2], (2, 0, 1)),
        jnp.transpose(late[2]),
        jnp.transpose(early[2:4], (2, 0, 1)),
        own_part(3, 0),
        grad_lower,
        grad_gain,
        early[0:2],
        flat[1],
        jnp.transpose(grad_ffn[0]),
        jnp.transpose(grad_ffn[1]),
        grad_ffn[2],
    )


def solution(mesh):
    in_specs = (
        P("mp", "dp", None),
        P("mp", "dp", None),
        P("dp"),
        P(),
        P(),
        P(None, None, "mp"),
        P(None, "mp"),
        P(None, None, "mp"),
        P("mp"),
        P(None, "mp"),
        P(None, "mp"),
        P(None, "mp", None),
        P(),
        P(None, "mp"),
        P(None, "mp"),
        P("mp", None),
    )
    out_specs = (
        P("mp", "dp", None),
        P("mp", "dp", None),
        P(),
        P(None, None, "mp"),
        P(None, "mp"),
        P(None, None, "mp"),
        P("mp"),
        P(None, "mp"),
        P(None, "mp"),
        P(None, "mp", None),
        P(),
        P(None, "mp"),
        P(None, "mp"),
        P("mp", None),
    )
    return jax.shard_map(shards, mesh=mesh, in_specs=in_specs, out_specs=out_specs, check_vma=False)
```

```python
import functools

import jax
import jax.numpy as jnp
from jax import lax
from jax.experimental import pallas as pl
from jax.experimental.pallas import tpu as pltpu
from jax.sharding import PartitionSpec as P

EPSILON = 1e-06
CHUNKS = 8
TILE = 256
MIB = 1024 * 1024
F32 = jnp.float32
BF16 = jnp.bfloat16


class Near:
    def __init__(self, value):
        self.value = value


def kernel_call(body, grid, in_specs, out_specs, out_shape, scratch=(), vmem=32, free=()):
    def space(shape):
        if isinstance(shape, Near):
            return pltpu.VMEM(shape.value.shape, shape.value.dtype)
        return pltpu.HBM(shape.shape, shape.dtype) if shape.size >= 65536 else shape

    def placed(value):
        if isinstance(value, Near):
            return pltpu.with_memory_space_constraint(value.value, pltpu.VMEM)
        if value.size < 65536:
            return value
        return pltpu.with_memory_space_constraint(value, pltpu.HBM)

    single = not isinstance(out_shape, (list, tuple))
    call = pl.pallas_call(
        body,
        grid=grid,
        in_specs=in_specs,
        out_specs=out_specs,
        out_shape=space(out_shape) if single else [space(shape) for shape in out_shape],
        scratch_shapes=scratch,
        cost_estimate=pl.CostEstimate(flops=1, bytes_accessed=1, transcendentals=0),
        compiler_params=pltpu.CompilerParams(vmem_limit_bytes=vmem * MIB),
    )
    return lambda *args: call(
        *(arg if at in free else placed(arg) for at, arg in enumerate(args))
    )


def shaped(shape, dtype=F32):
    return jax.ShapeDtypeStruct(shape, dtype)


def whole(shape, start=None):
    start = start or (0,) * len(shape)
    return pl.BlockSpec(shape, lambda *_: start, pipeline_mode=pl.Buffered(1))


def kept(shape):
    zeros = (0,) * len(shape)
    return pl.BlockSpec(shape, lambda *_: zeros)


def per_group(shape):
    zeros = (0,) * (len(shape) - 1)
    return pl.BlockSpec(shape, lambda g, t: (g,) + zeros)


def ahead(tiles, rows, width):
    return pl.BlockSpec((rows, width), lambda g, t: (g * tiles + t, 0))


def behind(tiles, rows, width):
    return pl.BlockSpec((rows, width), lambda g, t: (g * tiles + tiles - 1 - t, 0))


SMEM_SPEC = pl.BlockSpec(memory_space=pltpu.SMEM)
VMEM_SPEC = pl.BlockSpec(memory_space=pltpu.VMEM)


def turn(cos, sin, re, im):
    return cos * re - sin * im, sin * re + cos * im


def back_turn(cos, sin, re, im):
    return cos * re + sin * im, cos * im - sin * re


def sigmoid(values):
    return 0.5 * jnp.tanh(0.5 * values) + 0.5


def nt(left, right):
    return lax.dot_general(left, right, (((1,), (1,)), ((), ())), preferred_element_type=F32)


def nn(left, right):
    return lax.dot_general(left, right, (((1,), (0,)), ((), ())), preferred_element_type=F32)


def tn(left, right):
    return lax.dot_general(left, right, (((0,), (0,)), ((), ())), preferred_element_type=F32)


def rms_rows(values):
    return lax.rsqrt(jnp.mean(values * values, axis=-1, keepdims=True) + EPSILON)


def rms_pull(unit, inv, gain, d_out):
    scaled = d_out * gain
    return inv * (scaled - unit * jnp.mean(scaled * unit, axis=-1, keepdims=True))


def step_rows(j):
    return pl.ds(pl.multiple_of(j * CHUNKS, CHUNKS), CHUNKS)


def chain_chunks(order, turning, angles, prod, end_re, end_im, chain, totals):
    cos_chunk, sin_chunk = angles[CHUNK : CHUNK + 1, :], angles[CHUNK + 1 : CHUNK + 2, :]
    zero = jnp.zeros_like(prod[0:1])
    run, run_re, run_im = zero + 1.0, zero, zero
    for s in order:
        chain[0, 0, s : s + 1, :] = run
        chain[0, 1, s : s + 1, :] = run_re
        chain[0, 2, s : s + 1, :] = run_im
        turned_re, turned_im = turning(cos_chunk, sin_chunk, run_re, run_im)
        run_re = prod[s : s + 1] * turned_re + end_re[s : s + 1]
        run_im = prod[s : s + 1] * turned_im + end_im[s : s + 1]
        run = run * prod[s : s + 1]
    totals[0] = jnp.zeros_like(prod)
    totals[0, 0:1, :] = run
    totals[0, 1:2, :] = run_re
    totals[0, 2:3, :] = run_im


BOUND, PHASE, ONE, CHUNK, DEVICE, GAIN = 0, 1, 2, 4, 6, 8


def channel_rows(logits, phase, out_gain):
    return jnp.concatenate([logits, phase[None], out_gain], axis=0)


def make_tables(rows, layer, steps, rows_dev, tables, lags):
    layers = rows.shape[0] - 3
    logits = rows[:layers]
    phase = rows[layers : layers + 1]
    grown = jnp.exp(logits - jnp.max(logits, axis=0, keepdims=True))
    below = lax.broadcasted_iota(jnp.int32, grown.shape, 0) < layer
    bound = jnp.sum(jnp.where(below, grown, 0.0), axis=0, keepdims=True)
    tables[BOUND : BOUND + 1, :] = bound / jnp.sum(grown, axis=0, keepdims=True)
    tables[PHASE : PHASE + 1, :] = phase
    for at, span in ((ONE, 1), (CHUNK, steps), (DEVICE, rows_dev)):
        tables[at : at + 1, :] = jnp.cos(phase * span)
        tables[at + 1 : at + 2, :] = jnp.sin(phase * span)
    tables[GAIN : GAIN + 2, :] = rows[layers + 1 :]
    count, chans = lags.shape[0], phase.shape[1]
    turns = phase * lax.broadcasted_iota(jnp.int32, (count, chans), 0).astype(F32)
    lags[:, 0:chans] = jnp.cos(turns)
    lags[:, chans:] = jnp.sin(turns)


def gathered_weights(chans, kinds, me, pieces, proj, w_out):
    size = chans // len(pieces)
    spare = pieces[0].shape[0] - 7 * size
    total = jnp.zeros((spare, chans), F32)
    column = lax.broadcasted_iota(jnp.int32, (128, chans), 1)
    row = lax.broadcasted_iota(jnp.int32, (128, chans), 0)
    for b, piece in enumerate(pieces):
        d = me[0] ^ b
        for k in range(5):
            proj[k, d] = piece[k * size : (k + 1) * size, :]
        for k in range(2):
            w_out[k, d] = piece[(5 + k) * size : (6 + k) * size, :]
        here = jnp.logical_and(column == d * size + row, row < size)
        total += nn(piece[7 * size :, 0:128], here.astype(F32).astype(BF16))
    return total[0:kinds] + total[kinds : 2 * kinds] + total[2 * kinds : 3 * kinds]


def project_body(steps, chans, count, kinds, per_dev, me, layer, tokens, gain, *refs):
    given, refs = refs[: max(count, 2)], refs[max(count, 2) :]
    normed, pre, pre_out, local, decays, prefix, totals, tables, lags, *made, carry = refs
    chunk = per_dev // CHUNKS

    @pl.when(first_step())
    def _():
        rows = gathered_weights(chans, kinds, me, given, *made) if count else given[1][...]
        make_tables(rows, layer[0], chunk, per_dev, tables, lags)

    w = made[0][...].reshape(5 * chans, made[0].shape[-1]) if count else given[0][...]
    t = pl.program_id(1)

    @pl.when(t == 0)
    def _():
        carry[0:2] = jnp.zeros((2,) + carry.shape[1:], F32)
        carry[2] = jnp.ones(carry.shape[1:], F32)

    values = tokens[...].astype(F32)
    unit = (values * rms_rows(values) * gain[...]).astype(BF16)
    normed[...] = unit
    low = tables[BOUND : BOUND + 1, :]
    scan = nt(unit, w[2 * chans : 5 * chans])
    pre[...] = scan.astype(BF16)
    decay = low + (1.0 - low) * sigmoid(scan[:, 2 * chans :])
    decays[...] = decay
    in_re, in_im = scan[:, 0:chans], scan[:, chans : 2 * chans]
    local[:, 0:chans] = (1.0 - decay) * (in_re * sigmoid(in_re))
    local[:, chans:] = (1.0 - decay) * (in_im * sigmoid(in_im))
    pre_out[...] = nt(unit, w[0 : 2 * chans]).astype(BF16)
    cos_one, sin_one = tables[ONE : ONE + 1, :], tables[ONE + 1 : ONE + 2, :]

    def step(j, state):
        state_re, state_im, prod = state
        rows = step_rows(j)
        decay = decays[rows, :]
        turned_re, turned_im = turn(cos_one, sin_one, state_re, state_im)
        state_re = decay * turned_re + local[rows, 0:chans]
        state_im = decay * turned_im + local[rows, chans:]
        local[rows, 0:chans] = state_re
        local[rows, chans:] = state_im
        return state_re, state_im, prod * decay

    end_re, end_im, prod = lax.fori_loop(
        0, steps, step, (carry[0], carry[1], carry[2]), unroll=8
    )
    carry[0], carry[1], carry[2] = end_re, end_im, prod

    @pl.when(t == pl.num_programs(1) - 1)
    def _():
        chain_chunks(range(CHUNKS), turn, tables, prod, end_re, end_im, prefix, totals)


def project(me, layer, tokens, gain, pieces, kinds, w_proj, rows_all, groups, chans):
    rows, width = tokens.shape
    per = rows // groups
    tile = min(TILE, per)
    tiles = per // tile
    rowed = functools.partial(ahead, tiles, tile)
    made = [(5, 8, chans // 8, width), (2, 8, chans // 8, width)] if pieces else []
    given = pieces if pieces else [w_proj, rows_all]
    lags = (per // CHUNKS + 8, 2 * chans)
    return kernel_call(
        functools.partial(project_body, tile // CHUNKS, chans, len(pieces), kinds, per),
        (groups, tiles),
        [
            SMEM_SPEC,
            SMEM_SPEC,
            rowed(width),
            whole((1, width)),
            *(whole(value.shape) for value in given),
        ],
        [
            rowed(width),
            rowed(3 * chans),
            rowed(2 * chans),
            rowed(2 * chans),
            rowed(chans),
            per_group((1, 3, CHUNKS, chans)),
            per_group((1, CHUNKS, chans)),
            kept((16, chans)),
            kept(lags),
            *map(kept, made),
        ],
        [
            shaped((rows, width), BF16),
            shaped((rows, 3 * chans), BF16),
            shaped((rows, 2 * chans), BF16),
            Near(shaped((rows, 2 * chans))),
            shaped((rows, chans)),
            shaped((groups, 3, CHUNKS, chans)),
            shaped((groups, CHUNKS, chans)),
            shaped((16, chans)),
            shaped(lags),
            *(shaped(shape, BF16) for shape in made),
        ],
        [pltpu.VMEM((3, CHUNKS, chans), F32)],
        vmem=36,
        free=range(4, 4 + len(pieces)),
    )(me, layer, tokens, gain, *given)


def mix_body(
    steps,
    chans,
    blocks,
    me,
    keep,
    gathered,
    local,
    decays,
    prefix,
    angles,
    table,
    pre_out,
    tokens,
    w_out,
    out_gain,
    ffn_gain,
    states,
    entering,
    gated,
    mid,
    ffn_normed,
    full,
    carry,
):
    g, t = pl.program_id(0), pl.program_id(1)

    @pl.when(t == 0)
    def _():
        cos_dev, sin_dev = angles[DEVICE : DEVICE + 1, :], angles[DEVICE + 1 : DEVICE + 2, :]
        state_re = jnp.zeros((1, chans), F32)
        state_im = jnp.zeros((1, chans), F32)
        for d in range(blocks):
            kept_one = keep[g, d]
            turned_re, turned_im = turn(cos_dev, sin_dev, kept_one * state_re, kept_one * state_im)
            decay = gathered[d, 0, 0:1, :]
            earlier = d < me[0]
            state_re = jnp.where(earlier, decay * turned_re + gathered[d, 0, 1:2, :], state_re)
            state_im = jnp.where(earlier, decay * turned_im + gathered[d, 0, 2:3, :], state_im)
        kept_one = keep[g, me[0]]
        state_re, state_im = kept_one * state_re, kept_one * state_im
        cos_chunk, sin_chunk = angles[CHUNK : CHUNK + 1, :], angles[CHUNK + 1 : CHUNK + 2, :]
        for s in range(CHUNKS):
            run = prefix[0, 0, s : s + 1, :]
            entering[0, 0, s : s + 1, :] = run * state_re + prefix[0, 1, s : s + 1, :]
            entering[0, 1, s : s + 1, :] = run * state_im + prefix[0, 2, s : s + 1, :]
            state_re, state_im = turn(cos_chunk, sin_chunk, state_re, state_im)
        carry[...] = jnp.ones_like(carry)

    enter_re, enter_im = entering[0, 0], entering[0, 1]

    def step(j, prod):
        rows = step_rows(j)
        prod = prod * decays[rows, :]
        lag = pl.ds(t * steps + j + 1, 1)
        turned_re, turned_im = turn(table[lag, 0:chans], table[lag, chans:], enter_re, enter_im)
        full[rows, 0:chans] = local[rows, 0:chans] + prod * turned_re
        full[rows, chans:] = local[rows, chans:] + prod * turned_im
        return prod

    carry[...] = lax.fori_loop(0, steps, step, carry[...], unroll=8)
    state = full[...]
    states[...] = state.astype(BF16)
    inv_rms = rms_rows(state)
    gate = pre_out[...].astype(F32)
    gate_in = (state * out_gain[...] * (gate * sigmoid(gate))).astype(BF16)
    gated[...] = gate_in
    stream = tokens[...].astype(F32) + inv_rms * nn(gate_in, w_out[...])
    mid[...] = stream
    ffn_normed[...] = (stream * rms_rows(stream) * ffn_gain[...]).astype(BF16)


def mix(
    me, keep, gathered, local, decays, prefix, angles, table, pre_out, tokens, w, out_gain, ffn_gain, groups, chans
):
    rows, width = tokens.shape
    per = rows // groups
    tile = min(TILE, per)
    tiles = per // tile
    blocks = gathered.shape[0]
    rowed = functools.partial(ahead, tiles, tile)
    return kernel_call(
        functools.partial(mix_body, tile // CHUNKS, chans, blocks),
        (groups, tiles),
        [
            SMEM_SPEC,
            SMEM_SPEC,
            pl.BlockSpec((blocks, 1, CHUNKS, chans), lambda g, t: (0, g, 0, 0)),
            rowed(2 * chans),
            rowed(chans),
            per_group((1, 3, CHUNKS, chans)),
            whole(angles.shape),
            whole(table.shape),
            rowed(2 * chans),
            rowed(width),
            whole((2 * chans, width)),
            whole((1, 2 * chans)),
            whole((1, width)),
        ],
        [
            rowed(2 * chans),
            per_group((1, 2, CHUNKS, chans)),
            rowed(2 * chans),
            rowed(width),
            rowed(width),
        ],
        [
            shaped((rows, 2 * chans), BF16),
            shaped((groups, 2, CHUNKS, chans)),
            shaped((rows, 2 * chans), BF16),
            shaped((rows, width)),
            shaped((rows, width), BF16),
        ],
        [pltpu.VMEM((tile, 2 * chans), F32), pltpu.VMEM((CHUNKS, chans), F32)],
    )(me, keep, gathered, Near(local), decays, prefix, angles, table, pre_out, tokens, w, out_gain, ffn_gain)


def split_by_core(first, grads, span, unit, same, other):
    for chip in range(span // (2 * unit)):
        for k, part in enumerate(grads):
            even = part[2 * chip * unit : (2 * chip + 1) * unit]
            odd = part[(2 * chip + 1) * unit : (2 * chip + 2) * unit]
            rows = slice(k * unit, (k + 1) * unit)
            same[chip, rows, :] = jnp.where(first, even, odd)
            other[chip, rows, :] = jnp.where(first, odd, even)


def swiglu_body(unit, tile, x, up, w, act, d_pre, grads, w_out):
    devices = w.shape[0]

    def every(part):
        return jnp.concatenate([w[dev, part] for dev in range(devices)], axis=0)

    span = devices * unit
    w_pre = jnp.concatenate([every(0), every(1)], axis=0)
    w_down = every(2)
    w_out[...] = w_pre
    for start in range(0, x.shape[0], tile):
        rows = slice(start, start + tile)
        pre = nt(x[rows, :], w_pre)
        d_hidden = nt(up[rows, :], w_down)
        gate, lift = pre[:, :span], pre[:, span:]
        sigma = sigmoid(gate)
        silu = gate * sigma
        act[rows, :] = (silu * lift).astype(BF16)
        d_pre[rows, :span] = (d_hidden * lift * (sigma + silu * (1.0 - sigma))).astype(BF16)
        d_pre[rows, span:] = (d_hidden * silu).astype(BF16)
    g_pre = tn(d_pre[...], x[...]).astype(BF16)
    g_down = tn(act[...], up[...]).astype(BF16)
    for dev in range(devices):
        own = slice(dev * unit, (dev + 1) * unit)
        grads[dev, 0:unit, :] = g_pre[own]
        grads[dev, unit : 2 * unit, :] = g_pre[span + dev * unit : span + (dev + 1) * unit]
        grads[dev, 2 * unit : 3 * unit, :] = g_down[own]


def units_at_once(blocks, unit):
    devices = 2
    while devices < blocks and (devices * unit % 128 or devices * unit < 384):
        devices *= 2
    return devices


def swiglu(x, up, w):
    rows, width = x.shape
    blocks, _, unit, _ = w.shape
    devices = units_at_once(blocks, unit)
    span = devices * unit
    return kernel_call(
        functools.partial(swiglu_body, unit, min(rows, 512)),
        (blocks // devices,),
        [
            whole((rows, width)),
            whole((rows, width)),
            pl.BlockSpec((devices, 3, unit, width), lambda q: (q, 0, 0, 0)),
        ],
        [
            pl.BlockSpec((rows, span), lambda q: (0, q)),
            pl.BlockSpec((rows, 2 * span), lambda q: (0, q)),
            pl.BlockSpec((devices, 3 * unit, width), lambda q: (q, 0, 0)),
            pl.BlockSpec((2 * span, width), lambda q: (q, 0)),
        ],
        [
            shaped((rows, blocks * unit), BF16),
            shaped((rows, 2 * blocks * unit), BF16),
            shaped((blocks, 3 * unit, width), BF16),
            shaped((2 * blocks * unit, width), BF16),
        ],
    )(x, up, w)


def finish_grads(core, grads, kinds, chans, unit, same, other):
    grads = [grad.astype(BF16) for grad in grads]
    if unit % 16:
        same[...] = jnp.concatenate(grads, axis=0)
        other[...] = jnp.zeros_like(other)
        return
    each = [grad[at : at + chans] for grad in grads for at in range(0, grad.shape[0], chans)]
    split_by_core(core[0] == 0, each, chans, unit, same, other)


def grads_shapes(kinds, chans, unit, width):
    if unit % 16:
        return [(kinds * chans, width), (16, width)]
    return [(chans // (2 * unit), kinds * unit, width)] * 2


def first_step():
    return jnp.logical_and(pl.program_id(0) == 0, pl.program_id(1) == 0)


def last_step():
    return jnp.logical_and(
        pl.program_id(0) == pl.num_programs(0) - 1, pl.program_id(1) == pl.num_programs(1) - 1
    )


def mix_back_body(
    steps,
    chans,
    unit_chans,
    core,
    d_pre,
    w_pre,
    mid,
    upstream,
    tokens,
    states,
    pre_out,
    gated,
    normed,
    decays,
    w_out,
    out_gain,
    ffn_gain,
    angles,
    d_mid,
    d_outgate,
    local,
    suffix,
    totals,
    same,
    other,
    sums,
    d_mixes,
    d_gates,
    carry,
    gated_here,
    normed_here,
    arrivals,
):
    rows_here = steps * CHUNKS
    at = pl.program_id(0) * pl.num_programs(1) + pl.num_programs(1) - 1 - pl.program_id(1)
    here = pl.ds(pl.multiple_of(at * rows_here, rows_here), rows_here)

    fetches = [
        pltpu.make_async_copy(gated, gated_here, arrivals.at[0]),
        pltpu.make_async_copy(normed, normed_here, arrivals.at[1]),
    ]

    @pl.when(first_step())
    def _():
        sums[...] = jnp.zeros_like(sums)
        for fetch in fetches:
            fetch.start()

    @pl.when(pl.program_id(1) == 0)
    def _():
        carry[0:2] = jnp.zeros((2,) + carry.shape[1:], F32)
        carry[2] = jnp.ones(carry.shape[1:], F32)

    d_norm = nn(d_pre[...], w_pre[...])
    stream = mid[...]
    inv_mid = rms_rows(stream)
    unit_mid = stream * inv_mid
    sums[0:1, :] += jnp.sum(d_norm * unit_mid, axis=0, keepdims=True)
    d_stream = upstream[...].astype(F32) + rms_pull(unit_mid, inv_mid, ffn_gain[...], d_norm)
    d_mid[...] = d_stream.astype(BF16)
    state = states[...].astype(F32)
    inv_rms = rms_rows(state)
    d_mix = (inv_rms * d_stream).astype(BF16)
    mixed = stream - tokens[...].astype(F32)
    d_square = (-0.5 / chans) * inv_rms * inv_rms * jnp.sum(d_stream * mixed, axis=-1, keepdims=True)
    d_gated = nt(d_mix, w_out[...])
    gate = pre_out[...].astype(F32)
    sigma = sigmoid(gate)
    silu = gate * sigma
    gain = out_gain[...]
    local[...] = d_gated * gain * silu + d_square * state
    d_state_gate = d_gated * state
    sums[1:2, :] += jnp.sum(d_state_gate * silu, axis=0, keepdims=True)
    d_gate = (d_state_gate * gain * (sigma + silu * (1.0 - sigma))).astype(BF16)
    d_outgate[...] = d_gate
    d_mixes[here, :] = d_mix
    d_gates[here, :] = d_gate
    cos_one, sin_one = angles[ONE : ONE + 1, :], angles[ONE + 1 : ONE + 2, :]

    def step(i, flow):
        flow_re, flow_im, prod = flow
        rows = step_rows(steps - 1 - i)
        grad_re = local[rows, 0:chans] + flow_re
        grad_im = local[rows, chans:] + flow_im
        local[rows, 0:chans] = grad_re
        local[rows, chans:] = grad_im
        decay = decays[rows, :]
        turned_re, turned_im = back_turn(cos_one, sin_one, grad_re, grad_im)
        return decay * turned_re, decay * turned_im, prod * decay

    end_re, end_im, prod = lax.fori_loop(
        0, steps, step, (carry[0], carry[1], carry[2]), unroll=8
    )
    carry[0], carry[1], carry[2] = end_re, end_im, prod

    @pl.when(pl.program_id(1) == pl.num_programs(1) - 1)
    def _():
        chain_chunks(reversed(range(CHUNKS)), back_turn, angles, prod, end_re, end_im, suffix, totals)

    @pl.when(last_step())
    def _():
        for fetch in fetches:
            fetch.wait()
        grads = [tn(gated_here[...], d_mixes[...]), tn(d_gates[...], normed_here[...])]
        finish_grads(core, grads, 4, chans, unit_chans, same, other)


def mix_back(
    core,
    unit_chans,
    d_pre,
    w_pre,
    mid,
    upstream,
    tokens,
    states,
    pre_out,
    gated,
    normed,
    decays,
    w,
    out_gain,
    ffn_gain,
    angles,
    groups,
    chans,
):
    rows, width = mid.shape
    per = rows // groups
    tile = min(TILE, per)
    tiles = per // tile
    rowed = functools.partial(behind, tiles, tile)
    return kernel_call(
        functools.partial(mix_back_body, tile // CHUNKS, chans, unit_chans),
        (groups, tiles),
        [
            SMEM_SPEC,
            rowed(d_pre.shape[1]),
            whole(w_pre.shape),
            rowed(width),
            rowed(width),
            rowed(width),
            rowed(2 * chans),
            rowed(2 * chans),
            pl.BlockSpec(memory_space=pl.ANY),
            pl.BlockSpec(memory_space=pl.ANY),
            rowed(chans),
            whole((2 * chans, width)),
            whole((1, 2 * chans)),
            whole((1, width)),
            whole(angles.shape),
        ],
        [
            rowed(width),
            rowed(2 * chans),
            rowed(2 * chans),
            per_group((1, 3, CHUNKS, chans)),
            per_group((1, CHUNKS, chans)),
            *map(kept, grads_shapes(4, chans, unit_chans, width)),
            kept((8, width)),
        ],
        [
            shaped((rows, width), BF16),
            shaped((rows, 2 * chans), BF16),
            Near(shaped((rows, 2 * chans))),
            shaped((groups, 3, CHUNKS, chans)),
            shaped((groups, CHUNKS, chans)),
            *(shaped(shape, BF16) for shape in grads_shapes(4, chans, unit_chans, width)),
            shaped((8, width)),
        ],
        [
            pltpu.VMEM((rows, width), BF16),
            pltpu.VMEM((rows, 2 * chans), BF16),
            pltpu.VMEM((3, CHUNKS, chans), F32),
            pltpu.VMEM((rows, 2 * chans), BF16),
            pltpu.VMEM((rows, width), BF16),
            pltpu.SemaphoreType.DMA((2,)),
        ],
        vmem=40,
    )(
        core,
        d_pre,
        w_pre,
        mid,
        upstream,
        tokens,
        states,
        pre_out,
        gated,
        normed,
        decays,
        w,
        out_gain,
        ffn_gain,
        angles,
    )


def silu_slope(values, sigma):
    return sigma * (1.0 + values * (1.0 - sigma))


def adjoint_finish_body(
    steps,
    chans,
    blocks,
    unit_chans,
    me,
    core,
    keep,
    gathered,
    local,
    decays,
    suffix,
    pre,
    states,
    before,
    entering,
    angles,
    table,
    normed,
    d_pre,
    sums,
    same,
    other,
    leaving,
    full,
    d_pres,
    carry,
):
    g, t = pl.program_id(0), pl.program_id(1)
    tiles = pl.num_programs(1)
    rows_here = steps * CHUNKS
    here = pl.ds(pl.multiple_of((g * tiles + tiles - 1 - t) * rows_here, rows_here), rows_here)

    @pl.when(t == 0)
    def _():
        cos_chunk, sin_chunk = angles[CHUNK : CHUNK + 1, :], angles[CHUNK + 1 : CHUNK + 2, :]
        cos_dev, sin_dev = angles[DEVICE : DEVICE + 1, :], angles[DEVICE + 1 : DEVICE + 2, :]
        flow_re = jnp.zeros((1, chans), F32)
        flow_im = jnp.zeros((1, chans), F32)
        for d in reversed(range(blocks)):
            kept_one = keep[g, d]
            turned_re, turned_im = back_turn(cos_dev, sin_dev, flow_re, flow_im)
            decay = gathered[d, 0, 0:1, :]
            later = d > me[0]
            flow_re = jnp.where(
                later, kept_one * (decay * turned_re + gathered[d, 0, 1:2, :]), flow_re
            )
            flow_im = jnp.where(
                later, kept_one * (decay * turned_im + gathered[d, 0, 2:3, :]), flow_im
            )
        for s in reversed(range(CHUNKS)):
            run = suffix[0, 0, s : s + 1, :]
            leaving[0, s : s + 1, :] = run * flow_re + suffix[0, 1, s : s + 1, :]
            leaving[1, s : s + 1, :] = run * flow_im + suffix[0, 2, s : s + 1, :]
            flow_re, flow_im = back_turn(cos_chunk, sin_chunk, flow_re, flow_im)
        carry[...] = jnp.ones_like(carry)
        sums[...] = jnp.zeros_like(sums)

    low = angles[BOUND : BOUND + 1, :]
    cos_one, sin_one = angles[ONE : ONE + 1, :], angles[ONE + 1 : ONE + 2, :]
    leave_re, leave_im = leaving[0], leaving[1]

    def step(i, prod):
        rows = step_rows(steps - 1 - i)
        lag = pl.ds(t * steps + i, 1)
        turned_re, turned_im = back_turn(table[lag, 0:chans], table[lag, chans:], leave_re, leave_im)
        full[rows, 0:chans] = local[rows, 0:chans] + prod * turned_re
        full[rows, chans:] = local[rows, chans:] + prod * turned_im
        return prod * decays[rows, :]

    carry[...] = lax.fori_loop(0, steps, step, carry[...], unroll=8)
    first_tile = t == tiles - 1
    last = before[...].astype(F32)[CHUNKS:]
    last_re = jnp.where(first_tile, entering[0, 0], last[:, 0:chans])
    last_im = jnp.where(first_tile, entering[0, 1], last[:, chans:])
    state = states[...].astype(F32)[: (steps - 1) * CHUNKS]
    last_re = jnp.concatenate([last_re, state[:, 0:chans]], axis=0)
    last_im = jnp.concatenate([last_im, state[:, chans:]], axis=0)
    grad_re, grad_im = full[:, 0:chans], full[:, chans:]
    scan = pre[...].astype(F32)
    in_re, in_im = scan[:, 0:chans], scan[:, chans : 2 * chans]
    sigma_re, sigma_im = sigmoid(in_re), sigmoid(in_im)
    sigma = sigmoid(scan[:, 2 * chans :])
    decay = decays[...]
    cross_re = grad_re * last_re + grad_im * last_im
    cross_im = grad_im * last_re - grad_re * last_im
    along, across = back_turn(cos_one, sin_one, cross_re, cross_im)
    d_decay = along - (grad_re * in_re * sigma_re + grad_im * in_im * sigma_im)
    rest = 1.0 - decay
    d_low = d_decay * (1.0 - sigma)
    d_re = (grad_re * rest * silu_slope(in_re, sigma_re)).astype(BF16)
    d_im = (grad_im * rest * silu_slope(in_im, sigma_im)).astype(BF16)
    d_forget = (d_low * (1.0 - low) * sigma).astype(BF16)
    d_all = jnp.concatenate([d_re, d_im, d_forget], axis=1)
    d_pre[...] = d_all
    d_pres[here, :] = d_all
    sums[0, 0] += jnp.sum((decay * across).reshape(steps, CHUNKS, chans), axis=0)
    sums[0, 1] += jnp.sum(d_low.reshape(steps, CHUNKS, chans), axis=0)

    @pl.when(last_step())
    def _():
        finish_grads(core, [tn(d_pres[...], normed[...])], 3, chans, unit_chans, same, other)


def adjoint_finish(
    unit_chans,
    me,
    core,
    keep,
    gathered,
    local,
    decays,
    suffix,
    pre,
    states,
    entering,
    angles,
    table,
    normed,
    groups,
    chans,
):
    rows, width = normed.shape
    per = rows // groups
    tile = min(TILE, per)
    tiles = per // tile
    steps = tile // CHUNKS
    blocks = gathered.shape[0]
    rowed = functools.partial(behind, tiles, tile)

    def one_before(g, t):
        return (jnp.maximum((g * tiles + tiles - 1 - t) * (steps // 2) - 1, 0), 0)

    return kernel_call(
        functools.partial(adjoint_finish_body, steps, chans, blocks, unit_chans),
        (groups, tiles),
        [
            SMEM_SPEC,
            SMEM_SPEC,
            SMEM_SPEC,
            pl.BlockSpec((blocks, 1, CHUNKS, chans), lambda g, t: (0, g, 0, 0)),
            rowed(2 * chans),
            rowed(chans),
            per_group((1, 3, CHUNKS, chans)),
            rowed(3 * chans),
            rowed(2 * chans),
            pl.BlockSpec((2 * CHUNKS, 2 * chans), one_before),
            per_group((1, 2, CHUNKS, chans)),
            whole(angles.shape),
            whole(table.shape),
            whole((rows, width)),
        ],
        [
            rowed(3 * chans),
            per_group((1, 2, CHUNKS, chans)),
            *map(kept, grads_shapes(3, chans, unit_chans, width)),
        ],
        [
            shaped((rows, 3 * chans), BF16),
            shaped((groups, 2, CHUNKS, chans)),
            *(shaped(shape, BF16) for shape in grads_shapes(3, chans, unit_chans, width)),
        ],
        [
            pltpu.VMEM((2, CHUNKS, chans), F32),
            pltpu.VMEM((tile, 2 * chans), F32),
            pltpu.VMEM((rows, 3 * chans), BF16),
            pltpu.VMEM((CHUNKS, chans), F32),
        ],
    )(
        me,
        core,
        keep,
        gathered,
        Near(local),
        decays,
        suffix,
        pre,
        states,
        states,
        entering,
        angles,
        table,
        normed,
    )


def tokens_back_body(chans, d_scan, d_outgate, w, tokens, d_mid, gain, early, scan, grad_tokens, sums):
    @pl.when(first_step())
    def _():
        sums[...] = jnp.zeros_like(sums)
        sums[1:3, :] = early[0:2, :]
        sums[3:4, 0:chans] = jnp.sum(scan[:, 0], axis=(0, 1))[None]
        sums[3:4, chans : 2 * chans] = jnp.sum(scan[:, 1], axis=(0, 1))[None]

    d_normed = nn(d_scan[...], w[2 * chans : 5 * chans, :])
    d_normed += nn(d_outgate[...], w[0 : 2 * chans, :])
    values = tokens[...].astype(F32)
    inv = rms_rows(values)
    unit = values * inv
    sums[0:1, :] += jnp.sum(d_normed * unit, axis=0, keepdims=True)
    grad_tokens[...] = (d_mid[...].astype(F32) + rms_pull(unit, inv, gain[...], d_normed)).astype(BF16)


def tokens_back(d_scan, d_outgate, w, tokens, d_mid, gain, early, scan, groups, chans):
    rows, width = tokens.shape
    per = rows // groups
    tile = min(TILE, per)
    tiles = per // tile
    rowed = functools.partial(ahead, tiles, tile)
    return kernel_call(
        functools.partial(tokens_back_body, chans),
        (groups, tiles),
        [
            rowed(3 * chans),
            rowed(2 * chans),
            whole(w.shape),
            rowed(width),
            rowed(width),
            whole((1, width)),
            whole(early.shape),
            whole(scan.shape),
        ],
        [rowed(width), kept((8, width))],
        [Near(shaped((rows, width), BF16)), shaped((8, width))],
        vmem=20,
    )(d_scan, d_outgate, w, tokens, d_mid, gain, early, scan)


def result_body(act, w_down, mid, result):
    blocks = w_down.shape[0]
    down = jnp.concatenate([w_down[dev, 0] for dev in range(blocks)], axis=0)
    result[...] = (mid[...] + nn(act[...], down)).astype(BF16)


def block_result(act, w_ffn, mid):
    rows, width = mid.shape
    blocks, _, units, _ = w_ffn.shape
    tile = min(TILE, rows)

    def rowed(wide):
        return pl.BlockSpec((tile, wide), lambda i: (i, 0))

    return kernel_call(
        result_body,
        (rows // tile,),
        [rowed(act.shape[1]), whole((blocks, 1, units, width), (0, 2, 0, 0)), rowed(width)],
        rowed(width),
        Near(shaped((rows, width), BF16)),
        vmem=20,
    )(act, w_ffn, mid)


def swap(values, axis, bit, size):
    return lax.ppermute(values, axis, [(i, i ^ bit) for i in range(size)])


def joined(*parts):
    return sum(part.astype(F32) for part in parts)


def pick(values, index, axis):
    return lax.dynamic_index_in_dim(values, index, axis, keepdims=False)


def gather_pieces(shard, size, *others):
    half = shard.shape[0] // 32 * 16
    near_x = swap(shard, "mp", 2, size)
    near_y = swap(shard, "mp", 4, size)
    core = swap(shard, "mp", 1, size)
    near_x, near_y, *others = tied(near_x, near_y, *others)
    far_one = swap(near_x[:half], "mp", 4, size)
    far_two = swap(near_y[half:], "mp", 2, size)
    core_x = swap(near_x, "mp", 1, size)
    core_y = swap(near_y, "mp", 1, size)
    far = jnp.concatenate([far_one, far_two], axis=0)
    core_far = swap(far, "mp", 1, size)
    return [shard, core, near_x, core_x, near_y, core_y, far, core_far], *others


def reduce_mp(grads):
    return lax.psum_scatter(grads, "mp", scatter_dimension=0, tiled=False)


def sends_body(chip, same, got, out_x, out_y, out_far):
    for b, out in ((1, out_x), (2, out_y), (3, out_far)):
        at = chip[0] ^ b
        out[...] = (same[at].astype(F32) + got[at].astype(F32)).astype(BF16)


def sends(chip, same, got):
    return pl.pallas_call(
        sends_body,
        in_specs=[SMEM_SPEC, VMEM_SPEC, VMEM_SPEC],
        out_specs=[VMEM_SPEC] * 3,
        out_shape=[jax.ShapeDtypeStruct(same.shape[1:], BF16)] * 3,
        cost_estimate=pl.CostEstimate(flops=1, bytes_accessed=1, transcendentals=0),
        compiler_params=pltpu.CompilerParams(vmem_limit_bytes=16 * MIB),
    )(chip, same, got)


def last_sums(finish, order, size, layers, flat, chip, same, got, early, early_got):
    last = Reduction(same, None, chip, size, layers)
    last.flying = [got]
    flat = flat + swap(flat, "mp", 2 * order[0], size)
    flat = last.to_chips(flat)
    early, flat = tied(both(early, early_got), flat)
    early_got = along_layers(2, early)
    flat = flat + swap(flat, "mp", 2 * order[1], size)
    late, early, early_got, flat = tied(last.share_here(), early, early_got, flat)
    late_got = along_layers(1, late)
    early = both(early, early_got)
    early_got = along_layers(3, early)
    one, two, three = (swap(flat, "dp", bit, layers) for bit in (1, 2, 3))
    flat = (flat + one) + (two + three)
    for number in (2, 3):
        late = both(late, late_got)
        late_got = along_layers(number, late)
    return finish(flat, settled(late, late_got), settled(early, early_got))


class Reduction:
    def __init__(self, same, other, chip, size, layers):
        self.same, self.chip, self.size, self.layers = same, chip, size, layers
        self.flying = [] if other is None else [swap(other, "mp", 1, size)]

    def arrived(self, *others):
        count = len(self.flying)
        both = tied(*self.flying, *others)
        self.flying = both[:count]
        return both[count:] if len(others) > 1 else both[-1]

    def to_chips(self, other):
        self.got = self.flying[0]
        *parts, other = tied(*sends(self.chip, self.same, self.got), other)
        self.flying = [swap(part, "mp", 2 * b, self.size) for b, part in zip((1, 2, 3), parts)]
        return other

    def share_here(self):
        at = self.chip[0]
        mine = pick(self.same, at, 0), pick(self.got, at, 0)
        return joined(*mine, *self.flying).astype(BF16)


def along_layers(number, share):
    pairs = {1: [(0, 1), (3, 2)], 2: [(1, 2), (2, 1)], 3: [(1, 0), (2, 3)]}[number]
    return lax.ppermute(share, "dp", pairs)


def both(share, got):
    return joined(share, got).astype(BF16)


def settled(share, got):
    z = lax.axis_index("dp")
    inner = jnp.logical_or(z == 1, z == 2)
    return jnp.where(inner, share, got).astype(F32)


def split_three(values):
    one = lax.reduce_precision(values, 8, 7)
    two = lax.reduce_precision(values - one, 8, 7)
    three = values - one - two
    return jnp.stack([one, two, three], axis=0).astype(BF16)


def tied(*values):
    return lax.optimization_barrier(values)


def shards(
    tokens,
    upstream,
    pieces,
    layer_index,
    mix_gain,
    w_input,
    w_forget,
    w_outgate,
    phase_angle,
    lower_logits,
    out_gain,
    w_output,
    ffn_gain,
    w_gate,
    w_up,
    w_down,
):
    rows_dev, groups, width = tokens.shape
    blocks = lax.axis_size("mp")
    me = lax.axis_index("mp")
    layers_z = lax.axis_size("dp")
    seq_len = rows_dev * blocks
    chans_dev = w_input.shape[2]
    chans = chans_dev * blocks
    units_dev = w_gate.shape[1]
    units = units_dev * blocks
    steps = rows_dev // CHUNKS
    rows = rows_dev * groups

    def to_rows(values):
        return jnp.transpose(
            values.reshape(CHUNKS, steps, groups, width), (2, 1, 0, 3)
        ).reshape(rows, width)

    def from_rows(values):
        return jnp.transpose(
            values.reshape(groups, steps, CHUNKS, width), (2, 1, 0, 3)
        ).reshape(rows_dev, groups, width)

    me_one = me[None].astype(jnp.int32)
    rows_own = channel_rows(lower_logits, phase_angle, out_gain)
    kinds = rows_own.shape[0]
    by_hand = blocks == 8 and layers_z == 4 and chans_dev % 16 == 0
    mix_shard = jnp.concatenate(
        [
            jnp.transpose(w_outgate, (1, 2, 0)),
            jnp.transpose(w_input, (1, 2, 0)),
            jnp.transpose(w_forget)[None],
            w_output,
        ],
        axis=0,
    )
    ffn_parts = jnp.transpose(w_gate), jnp.transpose(w_up), w_down
    tok, up_rows = to_rows(tokens), to_rows(upstream)
    pieces_w, w_proj, rows_all = [], None, None
    if by_hand:
        terms = split_three(rows_own).reshape(3 * kinds, chans_dev)
        spare = (3 * kinds + 15) // 16 * 16
        terms = jnp.pad(terms, ((0, spare - 3 * kinds), (0, width - chans_dev)))
        own = jnp.concatenate([mix_shard.reshape(7 * chans_dev, width), terms], axis=0)
        own, *ffn_parts = tied(own, *ffn_parts)
        pieces_w, tok, up_rows = gather_pieces(own, blocks, tok, up_rows)
    else:
        w_mix = lax.all_gather(mix_shard, "mp", axis=0)
        w_mix = jnp.transpose(w_mix, (1, 0, 2, 3)).reshape(7 * chans, width)
        w_proj, w_out = w_mix[: 5 * chans], w_mix[5 * chans :]
        rows_all = lax.all_gather(rows_own, "mp", axis=0)
        rows_all = jnp.transpose(rows_all, (1, 0, 2)).reshape(kinds, chans)
    w_ffn = lax.all_gather(jnp.concatenate(ffn_parts, axis=0), "mp", axis=0)
    starts = jnp.arange(blocks, dtype=jnp.int32) * rows_dev
    keep = (starts[None, :] % (seq_len // pieces)[:, None] != 0).astype(F32)

    mix_row, ffn_row = mix_gain[None], ffn_gain[None]
    normed, pre, pre_out, local, decays, prefix, totals, angles, lags, *made = project(
        me_one, layer_index, tok, mix_row, pieces_w, kinds, w_proj, rows_all, groups, chans
    )
    if by_hand:
        w_proj, w_out = made[0].reshape(5 * chans, width), made[1].reshape(2 * chans, width)
    gain_row = angles[GAIN : GAIN + 2].reshape(1, 2 * chans)
    ends = lax.all_gather(totals, "mp", axis=0)
    states, entering, gated, mid, ffn_normed = mix(
        me_one,
        keep,
        ends,
        local,
        decays,
        prefix,
        angles,
        lags,
        pre_out,
        tok,
        w_out,
        gain_row,
        ffn_row,
        groups,
        chans,
    )
    core = (me & 1) if by_hand else jnp.zeros_like(me)
    core_one = core[None].astype(jnp.int32)
    chip_one = (me >> 1)[None].astype(jnp.int32)
    w_ffn = w_ffn.reshape(blocks, 3, units_dev, width)

    def reduction(same, other):
        return Reduction(same, other, chip_one, blocks, layers_z)

    act, d_pre, grad_ffn, w_pre = swiglu(ffn_normed, up_rows, w_ffn)
    grad_ffn = reduce_mp(grad_ffn)
    d_mid, d_outgate, back_local, suffix, back_totals, same, other, early_sums = mix_back(
        core_one,
        chans_dev,
        d_pre,
        w_pre,
        mid,
        up_rows,
        tok,
        states,
        pre_out,
        gated,
        normed,
        decays,
        w_out,
        gain_row,
        ffn_row,
        angles,
        groups,
        chans,
    )
    if by_hand:
        early = reduction(same, other)
    else:
        early = jnp.moveaxis(same.reshape(4, blocks, chans_dev, width), 1, 0)
    back_ends = lax.all_gather(back_totals, "mp", axis=0)
    if by_hand:
        back_ends = early.to_chips(early.arrived(back_ends))
        mid, back_ends = tied(mid, back_ends)
    out_result = from_rows(block_result(act, w_ffn, mid))
    if by_hand:
        back_ends, out_result = tied(back_ends, out_result)
    d_scan, sums, same, other = adjoint_finish(
        chans_dev,
        me_one,
        core_one,
        keep,
        back_ends,
        back_local,
        decays,
        suffix,
        pre,
        states,
        entering,
        angles,
        lags,
        normed,
        groups,
        chans,
    )
    if by_hand:
        other, d_scan = early.arrived(other, d_scan)
        late = reduction(same, other)
        early_share, d_scan = tied(early.share_here(), d_scan)
        early_got = along_layers(1, early_share)
    else:
        late = jnp.moveaxis(same.reshape(3, blocks, chans_dev, width), 1, 0)
    def finish(flat, late, early):
        early = early.reshape(4, chans_dev, width)
        late = late.reshape(3, chans_dev, width)
        own = me * chans_dev

        def own_part(row, offset):
            return lax.dynamic_slice(flat, (row, offset * chans + own), (1, chans_dev))[0]

        grad_gain = jnp.stack([own_part(2, 0), own_part(2, 1)], axis=0)
        below = jnp.arange(lower_logits.shape[0], dtype=jnp.int32) < layer_index[0]
        below = below.astype(F32)[:, None]
        soft = jax.nn.softmax(lower_logits, axis=0)
        bound_own = jnp.sum(soft * below, axis=0, keepdims=True)
        return (
            flat[0],
            jnp.transpose(late[0:2], (2, 0, 1)),
            jnp.transpose(late[2]),
            jnp.transpose(early[2:4], (2, 0, 1)),
            own_part(3, 0),
            soft * (below - bound_own) * own_part(3, 1)[None],
            grad_gain,
            early[0:2],
            flat[1],
        )

    grad_tokens, flat = tokens_back(
        d_scan, d_outgate, w_proj, tok, d_mid, mix_row, early_sums, sums, groups, chans
    )
    if by_hand:
        flat = flat + swap(flat, "mp", 1, blocks)
        out_tokens = from_rows(grad_tokens)
        early_got, flat = tied(early_got, flat)
        flat, out_tokens, grad_ffn = late.arrived(flat, out_tokens, grad_ffn)
        same, got = late.same, late.flying[0]
    else:
        early = lax.psum(reduce_mp(early.reshape(blocks, -1, width)), "dp").astype(F32)
        late = lax.psum(reduce_mp(late.reshape(blocks, -1, width)), "dp").astype(F32)
    if by_hand:
        finished = lax.cond(
            layer_index[0] > 0,
            functools.partial(last_sums, finish, (1, 2), blocks, layers_z),
            functools.partial(last_sums, finish, (2, 1), blocks, layers_z),
            flat,
            chip_one,
            same,
            got,
            early_share,
            early_got,
        )
    else:
        flat = lax.psum(flat, ("dp", "mp"))
        out_tokens = from_rows(grad_tokens)
    grad_ffn = lax.psum(grad_ffn, "dp")
    if by_hand:
        *finished, grad_ffn = tied(*finished, grad_ffn)
    else:
        finished = finish(flat, late, early)
    grad_ffn = grad_ffn.astype(F32).reshape(3, units_dev, width)
    return (
        out_result,
        out_tokens,
        *finished,
        jnp.transpose(grad_ffn[0]),
        jnp.transpose(grad_ffn[1]),
        grad_ffn[2],
    )


def solution(mesh):
    in_specs = (
        P("mp", "dp", None),
        P("mp", "dp", None),
        P("dp"),
        P(),
        P(),
        P(None, None, "mp"),
        P(None, "mp"),
        P(None, None, "mp"),
        P("mp"),
        P(None, "mp"),
        P(None, "mp"),
        P(None, "mp", None),
        P(),
        P(None, "mp"),
        P(None, "mp"),
        P("mp", None),
    )
    out_specs = (
        P("mp", "dp", None),
        P("mp", "dp", None),
        P(),
        P(None, None, "mp"),
        P(None, "mp"),
        P(None, None, "mp"),
        P("mp"),
        P(None, "mp"),
        P(None, "mp"),
        P(None, "mp", None),
        P(),
        P(None, "mp"),
        P(None, "mp"),
        P("mp", None),
    )
    return jax.shard_map(shards, mesh=mesh, in_specs=in_specs, out_specs=out_specs, check_vma=False)
```

```python
import functools

import jax
import jax.numpy as jnp
from jax import lax
from jax.experimental import pallas as pl
from jax.experimental.pallas import tpu as pltpu
from jax.sharding import PartitionSpec as P

EPSILON = 1e-06
CHUNKS = 8
TILE = 256
MIB = 1024 * 1024
F32 = jnp.float32
BF16 = jnp.bfloat16


class Near:
    def __init__(self, value):
        self.value = value


def kernel_call(body, grid, in_specs, out_specs, out_shape, scratch=(), vmem=32, free=()):
    def space(shape):
        if isinstance(shape, Near):
            return pltpu.VMEM(shape.value.shape, shape.value.dtype)
        return pltpu.HBM(shape.shape, shape.dtype) if shape.size >= 65536 else shape

    def placed(value):
        if isinstance(value, Near):
            return pltpu.with_memory_space_constraint(value.value, pltpu.VMEM)
        if value.size < 65536:
            return value
        return pltpu.with_memory_space_constraint(value, pltpu.HBM)

    single = not isinstance(out_shape, (list, tuple))
    call = pl.pallas_call(
        body,
        grid=grid,
        in_specs=in_specs,
        out_specs=out_specs,
        out_shape=space(out_shape) if single else [space(shape) for shape in out_shape],
        scratch_shapes=scratch,
        cost_estimate=pl.CostEstimate(flops=1, bytes_accessed=1, transcendentals=0),
        compiler_params=pltpu.CompilerParams(vmem_limit_bytes=vmem * MIB),
    )
    return lambda *args: call(
        *(arg if at in free else placed(arg) for at, arg in enumerate(args))
    )


def shaped(shape, dtype=F32):
    return jax.ShapeDtypeStruct(shape, dtype)


def whole(shape, start=None):
    start = start or (0,) * len(shape)
    return pl.BlockSpec(shape, lambda *_: start, pipeline_mode=pl.Buffered(1))


def kept(shape):
    zeros = (0,) * len(shape)
    return pl.BlockSpec(shape, lambda *_: zeros)


def per_group(shape):
    zeros = (0,) * (len(shape) - 1)
    return pl.BlockSpec(shape, lambda g, t: (g,) + zeros)


def ahead(tiles, rows, width):
    return pl.BlockSpec((rows, width), lambda g, t: (g * tiles + t, 0))


def behind(tiles, rows, width):
    return pl.BlockSpec((rows, width), lambda g, t: (g * tiles + tiles - 1 - t, 0))


SMEM_SPEC = pl.BlockSpec(memory_space=pltpu.SMEM)
VMEM_SPEC = pl.BlockSpec(memory_space=pltpu.VMEM)


def turn(cos, sin, re, im):
    return cos * re - sin * im, sin * re + cos * im


def back_turn(cos, sin, re, im):
    return cos * re + sin * im, cos * im - sin * re


def sigmoid(values):
    return 0.5 * jnp.tanh(0.5 * values) + 0.5


def nt(left, right):
    return lax.dot_general(left, right, (((1,), (1,)), ((), ())), preferred_element_type=F32)


def nn(left, right):
    return lax.dot_general(left, right, (((1,), (0,)), ((), ())), preferred_element_type=F32)


def tn(left, right):
    return lax.dot_general(left, right, (((0,), (0,)), ((), ())), preferred_element_type=F32)


def rms_rows(values):
    return lax.rsqrt(jnp.mean(values * values, axis=-1, keepdims=True) + EPSILON)


def rms_pull(unit, inv, gain, d_out):
    scaled = d_out * gain
    return inv * (scaled - unit * jnp.mean(scaled * unit, axis=-1, keepdims=True))


def step_rows(j):
    return pl.ds(pl.multiple_of(j * CHUNKS, CHUNKS), CHUNKS)


def chain_chunks(order, turning, angles, prod, end_re, end_im, chain, totals):
    cos_chunk, sin_chunk = angles[CHUNK : CHUNK + 1, :], angles[CHUNK + 1 : CHUNK + 2, :]
    zero = jnp.zeros_like(prod[0:1])
    run, run_re, run_im = zero + 1.0, zero, zero
    for s in order:
        chain[0, 0, s : s + 1, :] = run
        chain[0, 1, s : s + 1, :] = run_re
        chain[0, 2, s : s + 1, :] = run_im
        turned_re, turned_im = turning(cos_chunk, sin_chunk, run_re, run_im)
        run_re = prod[s : s + 1] * turned_re + end_re[s : s + 1]
        run_im = prod[s : s + 1] * turned_im + end_im[s : s + 1]
        run = run * prod[s : s + 1]
    totals[0] = jnp.zeros_like(prod)
    totals[0, 0:1, :] = run
    totals[0, 1:2, :] = run_re
    totals[0, 2:3, :] = run_im


BOUND, PHASE, ONE, CHUNK, DEVICE, GAIN = 0, 1, 2, 4, 6, 8


def channel_rows(logits, phase, out_gain):
    return jnp.concatenate([logits, phase[None], out_gain], axis=0)


def make_tables(rows, layer, steps, rows_dev, tables, lags):
    layers = rows.shape[0] - 3
    logits = rows[:layers]
    phase = rows[layers : layers + 1]
    grown = jnp.exp(logits - jnp.max(logits, axis=0, keepdims=True))
    below = lax.broadcasted_iota(jnp.int32, grown.shape, 0) < layer
    bound = jnp.sum(jnp.where(below, grown, 0.0), axis=0, keepdims=True)
    tables[BOUND : BOUND + 1, :] = bound / jnp.sum(grown, axis=0, keepdims=True)
    tables[PHASE : PHASE + 1, :] = phase
    for at, span in ((ONE, 1), (CHUNK, steps), (DEVICE, rows_dev)):
        tables[at : at + 1, :] = jnp.cos(phase * span)
        tables[at + 1 : at + 2, :] = jnp.sin(phase * span)
    tables[GAIN : GAIN + 2, :] = rows[layers + 1 :]
    count, chans = lags.shape[0], phase.shape[1]
    turns = phase * lax.broadcasted_iota(jnp.int32, (count, chans), 0).astype(F32)
    lags[:, 0:chans] = jnp.cos(turns)
    lags[:, chans:] = jnp.sin(turns)


def gathered_weights(chans, kinds, me, pieces, proj, w_out):
    size = chans // len(pieces)
    spare = pieces[0].shape[0] - 7 * size
    total = jnp.zeros((spare, chans), F32)
    column = lax.broadcasted_iota(jnp.int32, (128, chans), 1)
    row = lax.broadcasted_iota(jnp.int32, (128, chans), 0)
    for b, piece in enumerate(pieces):
        d = me[0] ^ b
        for k in range(5):
            proj[k, d] = piece[k * size : (k + 1) * size, :]
        for k in range(2):
            w_out[k, d] = piece[(5 + k) * size : (6 + k) * size, :]
        here = jnp.logical_and(column == d * size + row, row < size)
        total += nn(piece[7 * size :, 0:128], here.astype(F32).astype(BF16))
    return total[0:kinds] + total[kinds : 2 * kinds] + total[2 * kinds : 3 * kinds]


def project_body(steps, chans, count, kinds, per_dev, me, layer, tokens, gain, *refs):
    given, refs = refs[: max(count, 2)], refs[max(count, 2) :]
    normed, pre, pre_out, local, decays, prefix, totals, tables, lags, *made, carry = refs
    chunk = per_dev // CHUNKS

    @pl.when(first_step())
    def _():
        rows = gathered_weights(chans, kinds, me, given, *made) if count else given[1][...]
        make_tables(rows, layer[0], chunk, per_dev, tables, lags)

    w = made[0][...].reshape(5 * chans, made[0].shape[-1]) if count else given[0][...]
    t = pl.program_id(1)

    @pl.when(t == 0)
    def _():
        carry[0:2] = jnp.zeros((2,) + carry.shape[1:], F32)
        carry[2] = jnp.ones(carry.shape[1:], F32)

    values = tokens[...].astype(F32)
    unit = (values * rms_rows(values) * gain[...]).astype(BF16)
    normed[...] = unit
    low = tables[BOUND : BOUND + 1, :]
    scan = nt(unit, w[2 * chans : 5 * chans])
    pre[...] = scan.astype(BF16)
    decay = low + (1.0 - low) * sigmoid(scan[:, 2 * chans :])
    decays[...] = decay
    in_re, in_im = scan[:, 0:chans], scan[:, chans : 2 * chans]
    local[:, 0:chans] = (1.0 - decay) * (in_re * sigmoid(in_re))
    local[:, chans:] = (1.0 - decay) * (in_im * sigmoid(in_im))
    pre_out[...] = nt(unit, w[0 : 2 * chans]).astype(BF16)
    cos_one, sin_one = tables[ONE : ONE + 1, :], tables[ONE + 1 : ONE + 2, :]

    def step(j, state):
        state_re, state_im, prod = state
        rows = step_rows(j)
        decay = decays[rows, :]
        turned_re, turned_im = turn(cos_one, sin_one, state_re, state_im)
        state_re = decay * turned_re + local[rows, 0:chans]
        state_im = decay * turned_im + local[rows, chans:]
        local[rows, 0:chans] = state_re
        local[rows, chans:] = state_im
        return state_re, state_im, prod * decay

    end_re, end_im, prod = lax.fori_loop(
        0, steps, step, (carry[0], carry[1], carry[2]), unroll=8
    )
    carry[0], carry[1], carry[2] = end_re, end_im, prod

    @pl.when(t == pl.num_programs(1) - 1)
    def _():
        chain_chunks(range(CHUNKS), turn, tables, prod, end_re, end_im, prefix, totals)


def project(me, layer, tokens, gain, pieces, kinds, w_proj, rows_all, groups, chans):
    rows, width = tokens.shape
    per = rows // groups
    tile = min(TILE, per)
    tiles = per // tile
    rowed = functools.partial(ahead, tiles, tile)
    made = [(5, 8, chans // 8, width), (2, 8, chans // 8, width)] if pieces else []
    given = pieces if pieces else [w_proj, rows_all]
    lags = (per // CHUNKS + 8, 2 * chans)
    return kernel_call(
        functools.partial(project_body, tile // CHUNKS, chans, len(pieces), kinds, per),
        (groups, tiles),
        [
            SMEM_SPEC,
            SMEM_SPEC,
            rowed(width),
            whole((1, width)),
            *(whole(value.shape) for value in given),
        ],
        [
            rowed(width),
            rowed(3 * chans),
            rowed(2 * chans),
            rowed(2 * chans),
            rowed(chans),
            per_group((1, 3, CHUNKS, chans)),
            per_group((1, CHUNKS, chans)),
            kept((16, chans)),
            kept(lags),
            *map(kept, made),
        ],
        [
            shaped((rows, width), BF16),
            shaped((rows, 3 * chans), BF16),
            shaped((rows, 2 * chans), BF16),
            Near(shaped((rows, 2 * chans))),
            shaped((rows, chans)),
            shaped((groups, 3, CHUNKS, chans)),
            shaped((groups, CHUNKS, chans)),
            shaped((16, chans)),
            shaped(lags),
            *(shaped(shape, BF16) for shape in made),
        ],
        [pltpu.VMEM((3, CHUNKS, chans), F32)],
        vmem=36,
        free=range(4, 4 + len(pieces)),
    )(me, layer, tokens, gain, *given)


def mix_body(
    steps,
    chans,
    blocks,
    me,
    keep,
    gathered,
    local,
    decays,
    prefix,
    angles,
    table,
    pre_out,
    tokens,
    w_out,
    out_gain,
    ffn_gain,
    states,
    entering,
    gated,
    mid,
    ffn_normed,
    full,
    carry,
):
    g, t = pl.program_id(0), pl.program_id(1)

    @pl.when(t == 0)
    def _():
        cos_dev, sin_dev = angles[DEVICE : DEVICE + 1, :], angles[DEVICE + 1 : DEVICE + 2, :]
        state_re = jnp.zeros((1, chans), F32)
        state_im = jnp.zeros((1, chans), F32)
        for d in range(blocks):
            kept_one = keep[g, d]
            turned_re, turned_im = turn(cos_dev, sin_dev, kept_one * state_re, kept_one * state_im)
            decay = gathered[d, 0, 0:1, :]
            earlier = d < me[0]
            state_re = jnp.where(earlier, decay * turned_re + gathered[d, 0, 1:2, :], state_re)
            state_im = jnp.where(earlier, decay * turned_im + gathered[d, 0, 2:3, :], state_im)
        kept_one = keep[g, me[0]]
        state_re, state_im = kept_one * state_re, kept_one * state_im
        cos_chunk, sin_chunk = angles[CHUNK : CHUNK + 1, :], angles[CHUNK + 1 : CHUNK + 2, :]
        for s in range(CHUNKS):
            run = prefix[0, 0, s : s + 1, :]
            entering[0, 0, s : s + 1, :] = run * state_re + prefix[0, 1, s : s + 1, :]
            entering[0, 1, s : s + 1, :] = run * state_im + prefix[0, 2, s : s + 1, :]
            state_re, state_im = turn(cos_chunk, sin_chunk, state_re, state_im)
        carry[...] = jnp.ones_like(carry)

    enter_re, enter_im = entering[0, 0], entering[0, 1]

    def step(j, prod):
        rows = step_rows(j)
        prod = prod * decays[rows, :]
        lag = pl.ds(t * steps + j + 1, 1)
        turned_re, turned_im = turn(table[lag, 0:chans], table[lag, chans:], enter_re, enter_im)
        full[rows, 0:chans] = local[rows, 0:chans] + prod * turned_re
        full[rows, chans:] = local[rows, chans:] + prod * turned_im
        return prod

    carry[...] = lax.fori_loop(0, steps, step, carry[...], unroll=8)
    state = full[...]
    states[...] = state.astype(BF16)
    inv_rms = rms_rows(state)
    gate = pre_out[...].astype(F32)
    gate_in = (state * out_gain[...] * (gate * sigmoid(gate))).astype(BF16)
    gated[...] = gate_in
    stream = tokens[...].astype(F32) + inv_rms * nn(gate_in, w_out[...])
    mid[...] = stream
    ffn_normed[...] = (stream * rms_rows(stream) * ffn_gain[...]).astype(BF16)


def mix(
    me, keep, gathered, local, decays, prefix, angles, table, pre_out, tokens, w, out_gain, ffn_gain, groups, chans
):
    rows, width = tokens.shape
    per = rows // groups
    tile = min(TILE, per)
    tiles = per // tile
    blocks = gathered.shape[0]
    rowed = functools.partial(ahead, tiles, tile)
    return kernel_call(
        functools.partial(mix_body, tile // CHUNKS, chans, blocks),
        (groups, tiles),
        [
            SMEM_SPEC,
            SMEM_SPEC,
            pl.BlockSpec((blocks, 1, CHUNKS, chans), lambda g, t: (0, g, 0, 0)),
            rowed(2 * chans),
            rowed(chans),
            per_group((1, 3, CHUNKS, chans)),
            whole(angles.shape),
            whole(table.shape),
            rowed(2 * chans),
            rowed(width),
            whole((2 * chans, width)),
            whole((1, 2 * chans)),
            whole((1, width)),
        ],
        [
            rowed(2 * chans),
            per_group((1, 2, CHUNKS, chans)),
            rowed(2 * chans),
            rowed(width),
            rowed(width),
        ],
        [
            shaped((rows, 2 * chans), BF16),
            shaped((groups, 2, CHUNKS, chans)),
            shaped((rows, 2 * chans), BF16),
            shaped((rows, width)),
            shaped((rows, width), BF16),
        ],
        [pltpu.VMEM((tile, 2 * chans), F32), pltpu.VMEM((CHUNKS, chans), F32)],
    )(me, keep, gathered, Near(local), decays, prefix, angles, table, pre_out, tokens, w, out_gain, ffn_gain)


def split_by_core(first, grads, span, unit, same, other):
    for chip in range(span // (2 * unit)):
        for k, part in enumerate(grads):
            even = part[2 * chip * unit : (2 * chip + 1) * unit]
            odd = part[(2 * chip + 1) * unit : (2 * chip + 2) * unit]
            rows = slice(k * unit, (k + 1) * unit)
            same[chip, rows, :] = jnp.where(first, even, odd)
            other[chip, rows, :] = jnp.where(first, odd, even)


def swiglu_body(unit, tile, x, up, w, act, d_pre, grads, w_out):
    devices = w.shape[0]

    def every(part):
        return jnp.concatenate([w[dev, part] for dev in range(devices)], axis=0)

    span = devices * unit
    w_pre = jnp.concatenate([every(0), every(1)], axis=0)
    w_down = every(2)
    w_out[...] = w_pre
    for start in range(0, x.shape[0], tile):
        rows = slice(start, start + tile)
        pre = nt(x[rows, :], w_pre)
        d_hidden = nt(up[rows, :], w_down)
        gate, lift = pre[:, :span], pre[:, span:]
        sigma = sigmoid(gate)
        silu = gate * sigma
        act[rows, :] = (silu * lift).astype(BF16)
        d_pre[rows, :span] = (d_hidden * lift * (sigma + silu * (1.0 - sigma))).astype(BF16)
        d_pre[rows, span:] = (d_hidden * silu).astype(BF16)
    g_pre = tn(d_pre[...], x[...]).astype(BF16)
    g_down = tn(act[...], up[...]).astype(BF16)
    for dev in range(devices):
        own = slice(dev * unit, (dev + 1) * unit)
        grads[dev, 0:unit, :] = g_pre[own]
        grads[dev, unit : 2 * unit, :] = g_pre[span + dev * unit : span + (dev + 1) * unit]
        grads[dev, 2 * unit : 3 * unit, :] = g_down[own]


def units_at_once(blocks, unit):
    devices = 2
    while devices < blocks and (devices * unit % 128 or devices * unit < 384):
        devices *= 2
    return devices


def swiglu(x, up, w):
    rows, width = x.shape
    blocks, _, unit, _ = w.shape
    devices = units_at_once(blocks, unit)
    span = devices * unit
    return kernel_call(
        functools.partial(swiglu_body, unit, min(rows, 512)),
        (blocks // devices,),
        [
            whole((rows, width)),
            whole((rows, width)),
            pl.BlockSpec((devices, 3, unit, width), lambda q: (q, 0, 0, 0)),
        ],
        [
            pl.BlockSpec((rows, span), lambda q: (0, q)),
            pl.BlockSpec((rows, 2 * span), lambda q: (0, q)),
            pl.BlockSpec((devices, 3 * unit, width), lambda q: (q, 0, 0)),
            pl.BlockSpec((2 * span, width), lambda q: (q, 0)),
        ],
        [
            shaped((rows, blocks * unit), BF16),
            shaped((rows, 2 * blocks * unit), BF16),
            shaped((blocks, 3 * unit, width), BF16),
            shaped((2 * blocks * unit, width), BF16),
        ],
    )(x, up, w)


def finish_grads(core, grads, kinds, chans, unit, same, other):
    grads = [grad.astype(BF16) for grad in grads]
    if unit % 16:
        same[...] = jnp.concatenate(grads, axis=0)
        other[...] = jnp.zeros_like(other)
        return
    each = [grad[at : at + chans] for grad in grads for at in range(0, grad.shape[0], chans)]
    split_by_core(core[0] == 0, each, chans, unit, same, other)


def grads_shapes(kinds, chans, unit, width):
    if unit % 16:
        return [(kinds * chans, width), (16, width)]
    return [(chans // (2 * unit), kinds * unit, width)] * 2


def first_step():
    return jnp.logical_and(pl.program_id(0) == 0, pl.program_id(1) == 0)


def last_step():
    return jnp.logical_and(
        pl.program_id(0) == pl.num_programs(0) - 1, pl.program_id(1) == pl.num_programs(1) - 1
    )


def mix_back_body(
    steps,
    chans,
    unit_chans,
    core,
    d_pre,
    w_pre,
    mid,
    upstream,
    tokens,
    states,
    pre_out,
    gated,
    normed,
    decays,
    w_out,
    out_gain,
    ffn_gain,
    angles,
    d_mid,
    d_outgate,
    local,
    suffix,
    totals,
    same,
    other,
    sums,
    d_mixes,
    d_gates,
    carry,
    gated_here,
    normed_here,
    arrivals,
):
    rows_here = steps * CHUNKS
    at = pl.program_id(0) * pl.num_programs(1) + pl.num_programs(1) - 1 - pl.program_id(1)
    here = pl.ds(pl.multiple_of(at * rows_here, rows_here), rows_here)

    fetches = [
        pltpu.make_async_copy(gated, gated_here, arrivals.at[0]),
        pltpu.make_async_copy(normed, normed_here, arrivals.at[1]),
    ]

    @pl.when(first_step())
    def _():
        sums[...] = jnp.zeros_like(sums)
        for fetch in fetches:
            fetch.start()

    @pl.when(pl.program_id(1) == 0)
    def _():
        carry[0:2] = jnp.zeros((2,) + carry.shape[1:], F32)
        carry[2] = jnp.ones(carry.shape[1:], F32)

    d_norm = nn(d_pre[...], w_pre[...])
    stream = mid[...]
    inv_mid = rms_rows(stream)
    unit_mid = stream * inv_mid
    sums[0:1, :] += jnp.sum(d_norm * unit_mid, axis=0, keepdims=True)
    d_stream = upstream[...].astype(F32) + rms_pull(unit_mid, inv_mid, ffn_gain[...], d_norm)
    d_mid[...] = d_stream.astype(BF16)
    state = states[...].astype(F32)
    inv_rms = rms_rows(state)
    d_mix = (inv_rms * d_stream).astype(BF16)
    mixed = stream - tokens[...].astype(F32)
    d_square = (-0.5 / chans) * inv_rms * inv_rms * jnp.sum(d_stream * mixed, axis=-1, keepdims=True)
    d_gated = nt(d_mix, w_out[...])
    gate = pre_out[...].astype(F32)
    sigma = sigmoid(gate)
    silu = gate * sigma
    gain = out_gain[...]
    local[...] = d_gated * gain * silu + d_square * state
    d_state_gate = d_gated * state
    sums[1:2, :] += jnp.sum(d_state_gate * silu, axis=0, keepdims=True)
    d_gate = (d_state_gate * gain * (sigma + silu * (1.0 - sigma))).astype(BF16)
    d_outgate[...] = d_gate
    d_mixes[here, :] = d_mix
    d_gates[here, :] = d_gate
    cos_one, sin_one = angles[ONE : ONE + 1, :], angles[ONE + 1 : ONE + 2, :]

    def step(i, flow):
        flow_re, flow_im, prod = flow
        rows = step_rows(steps - 1 - i)
        grad_re = local[rows, 0:chans] + flow_re
        grad_im = local[rows, chans:] + flow_im
        local[rows, 0:chans] = grad_re
        local[rows, chans:] = grad_im
        decay = decays[rows, :]
        turned_re, turned_im = back_turn(cos_one, sin_one, grad_re, grad_im)
        return decay * turned_re, decay * turned_im, prod * decay

    end_re, end_im, prod = lax.fori_loop(
        0, steps, step, (carry[0], carry[1], carry[2]), unroll=8
    )
    carry[0], carry[1], carry[2] = end_re, end_im, prod

    @pl.when(pl.program_id(1) == pl.num_programs(1) - 1)
    def _():
        chain_chunks(reversed(range(CHUNKS)), back_turn, angles, prod, end_re, end_im, suffix, totals)

    @pl.when(last_step())
    def _():
        for fetch in fetches:
            fetch.wait()
        grads = [tn(gated_here[...], d_mixes[...]), tn(d_gates[...], normed_here[...])]
        finish_grads(core, grads, 4, chans, unit_chans, same, other)


def mix_back(
    core,
    unit_chans,
    d_pre,
    w_pre,
    mid,
    upstream,
    tokens,
    states,
    pre_out,
    gated,
    normed,
    decays,
    w,
    out_gain,
    ffn_gain,
    angles,
    groups,
    chans,
):
    rows, width = mid.shape
    per = rows // groups
    tile = min(TILE, per)
    tiles = per // tile
    rowed = functools.partial(behind, tiles, tile)
    return kernel_call(
        functools.partial(mix_back_body, tile // CHUNKS, chans, unit_chans),
        (groups, tiles),
        [
            SMEM_SPEC,
            rowed(d_pre.shape[1]),
            whole(w_pre.shape),
            rowed(width),
            rowed(width),
            rowed(width),
            rowed(2 * chans),
            rowed(2 * chans),
            pl.BlockSpec(memory_space=pl.ANY),
            pl.BlockSpec(memory_space=pl.ANY),
            rowed(chans),
            whole((2 * chans, width)),
            whole((1, 2 * chans)),
            whole((1, width)),
            whole(angles.shape),
        ],
        [
            rowed(width),
            rowed(2 * chans),
            rowed(2 * chans),
            per_group((1, 3, CHUNKS, chans)),
            per_group((1, CHUNKS, chans)),
            *map(kept, grads_shapes(4, chans, unit_chans, width)),
            kept((8, width)),
        ],
        [
            shaped((rows, width), BF16),
            shaped((rows, 2 * chans), BF16),
            Near(shaped((rows, 2 * chans))),
            shaped((groups, 3, CHUNKS, chans)),
            shaped((groups, CHUNKS, chans)),
            *(shaped(shape, BF16) for shape in grads_shapes(4, chans, unit_chans, width)),
            shaped((8, width)),
        ],
        [
            pltpu.VMEM((rows, width), BF16),
            pltpu.VMEM((rows, 2 * chans), BF16),
            pltpu.VMEM((3, CHUNKS, chans), F32),
            pltpu.VMEM((rows, 2 * chans), BF16),
            pltpu.VMEM((rows, width), BF16),
            pltpu.SemaphoreType.DMA((2,)),
        ],
        vmem=40,
    )(
        core,
        d_pre,
        w_pre,
        mid,
        upstream,
        tokens,
        states,
        pre_out,
        gated,
        normed,
        decays,
        w,
        out_gain,
        ffn_gain,
        angles,
    )


def silu_slope(values, sigma):
    return sigma * (1.0 + values * (1.0 - sigma))


def adjoint_finish_body(
    steps,
    chans,
    blocks,
    unit_chans,
    me,
    core,
    keep,
    gathered,
    local,
    decays,
    suffix,
    pre,
    states,
    before,
    entering,
    angles,
    table,
    normed,
    d_pre,
    sums,
    same,
    other,
    leaving,
    full,
    d_pres,
    carry,
):
    g, t = pl.program_id(0), pl.program_id(1)
    tiles = pl.num_programs(1)
    rows_here = steps * CHUNKS
    here = pl.ds(pl.multiple_of((g * tiles + tiles - 1 - t) * rows_here, rows_here), rows_here)

    @pl.when(t == 0)
    def _():
        cos_chunk, sin_chunk = angles[CHUNK : CHUNK + 1, :], angles[CHUNK + 1 : CHUNK + 2, :]
        cos_dev, sin_dev = angles[DEVICE : DEVICE + 1, :], angles[DEVICE + 1 : DEVICE + 2, :]
        flow_re = jnp.zeros((1, chans), F32)
        flow_im = jnp.zeros((1, chans), F32)
        for d in reversed(range(blocks)):
            kept_one = keep[g, d]
            turned_re, turned_im = back_turn(cos_dev, sin_dev, flow_re, flow_im)
            decay = gathered[d, 0, 0:1, :]
            later = d > me[0]
            flow_re = jnp.where(
                later, kept_one * (decay * turned_re + gathered[d, 0, 1:2, :]), flow_re
            )
            flow_im = jnp.where(
                later, kept_one * (decay * turned_im + gathered[d, 0, 2:3, :]), flow_im
            )
        for s in reversed(range(CHUNKS)):
            run = suffix[0, 0, s : s + 1, :]
            leaving[0, s : s + 1, :] = run * flow_re + suffix[0, 1, s : s + 1, :]
            leaving[1, s : s + 1, :] = run * flow_im + suffix[0, 2, s : s + 1, :]
            flow_re, flow_im = back_turn(cos_chunk, sin_chunk, flow_re, flow_im)
        carry[...] = jnp.ones_like(carry)
        sums[...] = jnp.zeros_like(sums)

    low = angles[BOUND : BOUND + 1, :]
    cos_one, sin_one = angles[ONE : ONE + 1, :], angles[ONE + 1 : ONE + 2, :]
    leave_re, leave_im = leaving[0], leaving[1]

    def step(i, prod):
        rows = step_rows(steps - 1 - i)
        lag = pl.ds(t * steps + i, 1)
        turned_re, turned_im = back_turn(table[lag, 0:chans], table[lag, chans:], leave_re, leave_im)
        full[rows, 0:chans] = local[rows, 0:chans] + prod * turned_re
        full[rows, chans:] = local[rows, chans:] + prod * turned_im
        return prod * decays[rows, :]

    carry[...] = lax.fori_loop(0, steps, step, carry[...], unroll=8)
    first_tile = t == tiles - 1
    last = before[...].astype(F32)[CHUNKS:]
    last_re = jnp.where(first_tile, entering[0, 0], last[:, 0:chans])
    last_im = jnp.where(first_tile, entering[0, 1], last[:, chans:])
    state = states[...].astype(F32)[: (steps - 1) * CHUNKS]
    last_re = jnp.concatenate([last_re, state[:, 0:chans]], axis=0)
    last_im = jnp.concatenate([last_im, state[:, chans:]], axis=0)
    grad_re, grad_im = full[:, 0:chans], full[:, chans:]
    scan = pre[...].astype(F32)
    in_re, in_im = scan[:, 0:chans], scan[:, chans : 2 * chans]
    sigma_re, sigma_im = sigmoid(in_re), sigmoid(in_im)
    sigma = sigmoid(scan[:, 2 * chans :])
    decay = decays[...]
    cross_re = grad_re * last_re + grad_im * last_im
    cross_im = grad_im * last_re - grad_re * last_im
    along, across = back_turn(cos_one, sin_one, cross_re, cross_im)
    d_decay = along - (grad_re * in_re * sigma_re + grad_im * in_im * sigma_im)
    rest = 1.0 - decay
    d_low = d_decay * (1.0 - sigma)
    d_re = (grad_re * rest * silu_slope(in_re, sigma_re)).astype(BF16)
    d_im = (grad_im * rest * silu_slope(in_im, sigma_im)).astype(BF16)
    d_forget = (d_low * (1.0 - low) * sigma).astype(BF16)
    d_all = jnp.concatenate([d_re, d_im, d_forget], axis=1)
    d_pre[...] = d_all
    d_pres[here, :] = d_all
    sums[0, 0] += jnp.sum((decay * across).reshape(steps, CHUNKS, chans), axis=0)
    sums[0, 1] += jnp.sum(d_low.reshape(steps, CHUNKS, chans), axis=0)

    @pl.when(last_step())
    def _():
        finish_grads(core, [tn(d_pres[...], normed[...])], 3, chans, unit_chans, same, other)


def adjoint_finish(
    unit_chans,
    me,
    core,
    keep,
    gathered,
    local,
    decays,
    suffix,
    pre,
    states,
    entering,
    angles,
    table,
    normed,
    groups,
    chans,
):
    rows, width = normed.shape
    per = rows // groups
    tile = min(TILE, per)
    tiles = per // tile
    steps = tile // CHUNKS
    blocks = gathered.shape[0]
    rowed = functools.partial(behind, tiles, tile)

    def one_before(g, t):
        return (jnp.maximum((g * tiles + tiles - 1 - t) * (steps // 2) - 1, 0), 0)

    return kernel_call(
        functools.partial(adjoint_finish_body, steps, chans, blocks, unit_chans),
        (groups, tiles),
        [
            SMEM_SPEC,
            SMEM_SPEC,
            SMEM_SPEC,
            pl.BlockSpec((blocks, 1, CHUNKS, chans), lambda g, t: (0, g, 0, 0)),
            rowed(2 * chans),
            rowed(chans),
            per_group((1, 3, CHUNKS, chans)),
            rowed(3 * chans),
            rowed(2 * chans),
            pl.BlockSpec((2 * CHUNKS, 2 * chans), one_before),
            per_group((1, 2, CHUNKS, chans)),
            whole(angles.shape),
            whole(table.shape),
            whole((rows, width)),
        ],
        [
            rowed(3 * chans),
            per_group((1, 2, CHUNKS, chans)),
            *map(kept, grads_shapes(3, chans, unit_chans, width)),
        ],
        [
            shaped((rows, 3 * chans), BF16),
            shaped((groups, 2, CHUNKS, chans)),
            *(shaped(shape, BF16) for shape in grads_shapes(3, chans, unit_chans, width)),
        ],
        [
            pltpu.VMEM((2, CHUNKS, chans), F32),
            pltpu.VMEM((tile, 2 * chans), F32),
            pltpu.VMEM((rows, 3 * chans), BF16),
            pltpu.VMEM((CHUNKS, chans), F32),
        ],
    )(
        me,
        core,
        keep,
        gathered,
        Near(local),
        decays,
        suffix,
        pre,
        states,
        states,
        entering,
        angles,
        table,
        normed,
    )


def tokens_back_body(chans, d_scan, d_outgate, w, tokens, d_mid, gain, early, scan, grad_tokens, sums):
    @pl.when(first_step())
    def _():
        sums[...] = jnp.zeros_like(sums)
        sums[1:3, :] = early[0:2, :]
        sums[3:4, 0:chans] = jnp.sum(scan[:, 0], axis=(0, 1))[None]
        sums[3:4, chans : 2 * chans] = jnp.sum(scan[:, 1], axis=(0, 1))[None]

    d_normed = nn(d_scan[...], w[2 * chans : 5 * chans, :])
    d_normed += nn(d_outgate[...], w[0 : 2 * chans, :])
    values = tokens[...].astype(F32)
    inv = rms_rows(values)
    unit = values * inv
    sums[0:1, :] += jnp.sum(d_normed * unit, axis=0, keepdims=True)
    grad_tokens[...] = (d_mid[...].astype(F32) + rms_pull(unit, inv, gain[...], d_normed)).astype(BF16)


def tokens_back(d_scan, d_outgate, w, tokens, d_mid, gain, early, scan, groups, chans):
    rows, width = tokens.shape
    per = rows // groups
    tile = min(TILE, per)
    tiles = per // tile
    rowed = functools.partial(ahead, tiles, tile)
    return kernel_call(
        functools.partial(tokens_back_body, chans),
        (groups, tiles),
        [
            rowed(3 * chans),
            rowed(2 * chans),
            whole(w.shape),
            rowed(width),
            rowed(width),
            whole((1, width)),
            whole(early.shape),
            whole(scan.shape),
        ],
        [rowed(width), kept((8, width))],
        [Near(shaped((rows, width), BF16)), shaped((8, width))],
        vmem=20,
    )(d_scan, d_outgate, w, tokens, d_mid, gain, early, scan)


def result_body(act, w_down, mid, result):
    blocks = w_down.shape[0]
    down = jnp.concatenate([w_down[dev, 0] for dev in range(blocks)], axis=0)
    result[...] = (mid[...] + nn(act[...], down)).astype(BF16)


def block_result(act, w_ffn, mid):
    rows, width = mid.shape
    blocks, _, units, _ = w_ffn.shape
    tile = min(TILE, rows)

    def rowed(wide):
        return pl.BlockSpec((tile, wide), lambda i: (i, 0))

    return kernel_call(
        result_body,
        (rows // tile,),
        [rowed(act.shape[1]), whole((blocks, 1, units, width), (0, 2, 0, 0)), rowed(width)],
        rowed(width),
        Near(shaped((rows, width), BF16)),
        vmem=20,
    )(act, w_ffn, mid)


def unpack_body(ffn, gate, up, down):
    rows = gate.shape[0]
    for k, out in enumerate((gate, up, down)):
        out[...] = ffn[k * rows : (k + 1) * rows, :].astype(F32)


def unpack(ffn):
    rows, width = ffn.shape[0] // 3, ffn.shape[1]
    return kernel_call(
        unpack_body,
        (1,),
        [whole(ffn.shape)],
        [whole((rows, width))] * 3,
        [shaped((rows, width))] * 3,
        vmem=16,
    )(ffn)


def swap(values, axis, bit, size):
    return lax.ppermute(values, axis, [(i, i ^ bit) for i in range(size)])


def joined(*parts):
    return sum(part.astype(F32) for part in parts)


def pick(values, index, axis):
    return lax.dynamic_index_in_dim(values, index, axis, keepdims=False)


def gather_pieces(shard, size, *others):
    half = shard.shape[0] // 32 * 16
    near_x = swap(shard, "mp", 2, size)
    near_y = swap(shard, "mp", 4, size)
    core = swap(shard, "mp", 1, size)
    near_x, near_y, *others = tied(near_x, near_y, *others)
    far_one = swap(near_x[:half], "mp", 4, size)
    far_two = swap(near_y[half:], "mp", 2, size)
    core_x = swap(near_x, "mp", 1, size)
    core_y = swap(near_y, "mp", 1, size)
    far = jnp.concatenate([far_one, far_two], axis=0)
    core_far = swap(far, "mp", 1, size)
    return [shard, core, near_x, core_x, near_y, core_y, far, core_far], *others


def reduce_mp(grads):
    return lax.psum_scatter(grads, "mp", scatter_dimension=0, tiled=False)


def sends_body(chip, same, got, out_x, out_y, out_far):
    for b, out in ((1, out_x), (2, out_y), (3, out_far)):
        at = chip[0] ^ b
        out[...] = (same[at].astype(F32) + got[at].astype(F32)).astype(BF16)


def sends(chip, same, got):
    return pl.pallas_call(
        sends_body,
        in_specs=[SMEM_SPEC, VMEM_SPEC, VMEM_SPEC],
        out_specs=[VMEM_SPEC] * 3,
        out_shape=[jax.ShapeDtypeStruct(same.shape[1:], BF16)] * 3,
        cost_estimate=pl.CostEstimate(flops=1, bytes_accessed=1, transcendentals=0),
        compiler_params=pltpu.CompilerParams(vmem_limit_bytes=16 * MIB),
    )(chip, same, got)


def last_sums(finish, from_rows, order, size, layers, flat, chip, same, got, early, early_got, tokens):
    last = Reduction(same, None, chip, size, layers)
    last.flying = [got]
    early = both(early, early_got)
    early_got = along_layers(2, early)
    flat = flat + swap(flat, "mp", 2 * order[0], size)
    flat, tokens = tied(last.to_chips(flat), tokens)
    flat = flat + swap(flat, "mp", 2 * order[1], size)
    moved = from_rows(tokens)
    late, flat, moved, early_got = tied(last.share_here(), flat, moved, early_got)
    one, two, three = (swap(late, "dp", bit, layers) for bit in (1, 2, 3))
    early = both(early, early_got)
    early_got = along_layers(3, early)
    flat = flat + swap(flat, "mp", 1, size)
    late = joined(joined(late, one), joined(two, three))
    early = settled(early, early_got).reshape(2, 2, -1, early.shape[-1])
    return (*finish(flat, late), moved, early[0], early[1])


class Reduction:
    def __init__(self, same, other, chip, size, layers):
        self.same, self.chip, self.size, self.layers = same, chip, size, layers
        self.flying = [] if other is None else [swap(other, "mp", 1, size)]

    def arrived(self, *others):
        count = len(self.flying)
        both = tied(*self.flying, *others)
        self.flying = both[:count]
        return both[count:] if len(others) > 1 else both[-1]

    def to_chips(self, other):
        self.got = self.flying[0]
        *parts, other = tied(*sends(self.chip, self.same, self.got), other)
        self.flying = [swap(part, "mp", 2 * b, self.size) for b, part in zip((1, 2, 3), parts)]
        return other

    def share_here(self):
        at = self.chip[0]
        mine = pick(self.same, at, 0), pick(self.got, at, 0)
        return joined(*mine, *self.flying).astype(BF16)


def along_layers(number, share):
    pairs = {1: [(0, 1), (3, 2)], 2: [(1, 2), (2, 1)], 3: [(1, 0), (2, 3)]}[number]
    return lax.ppermute(share, "dp", pairs)


def both(share, got):
    return joined(share, got).astype(BF16)


def settled(share, got):
    z = lax.axis_index("dp")
    inner = jnp.logical_or(z == 1, z == 2)
    return jnp.where(inner, share, got).astype(F32)


def split_three(values):
    one = lax.reduce_precision(values, 8, 7)
    two = lax.reduce_precision(values - one, 8, 7)
    three = values - one - two
    return jnp.stack([one, two, three], axis=0).astype(BF16)


def tied(*values):
    return lax.optimization_barrier(values)


def shards(
    tokens,
    upstream,
    pieces,
    layer_index,
    mix_gain,
    w_input,
    w_forget,
    w_outgate,
    phase_angle,
    lower_logits,
    out_gain,
    w_output,
    ffn_gain,
    w_gate,
    w_up,
    w_down,
):
    rows_dev, groups, width = tokens.shape
    blocks = lax.axis_size("mp")
    me = lax.axis_index("mp")
    layers_z = lax.axis_size("dp")
    seq_len = rows_dev * blocks
    chans_dev = w_input.shape[2]
    chans = chans_dev * blocks
    units_dev = w_gate.shape[1]
    units = units_dev * blocks
    steps = rows_dev // CHUNKS
    rows = rows_dev * groups

    def to_rows(values):
        return jnp.transpose(
            values.reshape(CHUNKS, steps, groups, width), (2, 1, 0, 3)
        ).reshape(rows, width)

    def from_rows(values):
        return jnp.transpose(
            values.reshape(groups, steps, CHUNKS, width), (2, 1, 0, 3)
        ).reshape(rows_dev, groups, width)

    me_one = me[None].astype(jnp.int32)
    rows_own = channel_rows(lower_logits, phase_angle, out_gain)
    kinds = rows_own.shape[0]
    by_hand = blocks == 8 and layers_z == 4 and chans_dev % 16 == 0
    mix_shard = jnp.concatenate(
        [
            jnp.transpose(w_outgate, (1, 2, 0)),
            jnp.transpose(w_input, (1, 2, 0)),
            jnp.transpose(w_forget)[None],
            w_output,
        ],
        axis=0,
    )
    ffn_parts = jnp.transpose(w_gate), jnp.transpose(w_up), w_down
    tok, up_rows = to_rows(tokens), to_rows(upstream)
    pieces_w, w_proj, rows_all = [], None, None
    if by_hand:
        terms = split_three(rows_own).reshape(3 * kinds, chans_dev)
        spare = (3 * kinds + 15) // 16 * 16
        terms = jnp.pad(terms, ((0, spare - 3 * kinds), (0, width - chans_dev)))
        own = jnp.concatenate([mix_shard.reshape(7 * chans_dev, width), terms], axis=0)
        own, *ffn_parts = tied(own, *ffn_parts)
        pieces_w, tok, up_rows = gather_pieces(own, blocks, tok, up_rows)
    else:
        w_mix = lax.all_gather(mix_shard, "mp", axis=0)
        w_mix = jnp.transpose(w_mix, (1, 0, 2, 3)).reshape(7 * chans, width)
        w_proj, w_out = w_mix[: 5 * chans], w_mix[5 * chans :]
        rows_all = lax.all_gather(rows_own, "mp", axis=0)
        rows_all = jnp.transpose(rows_all, (1, 0, 2)).reshape(kinds, chans)
    w_ffn = lax.all_gather(jnp.concatenate(ffn_parts, axis=0), "mp", axis=0)
    starts = jnp.arange(blocks, dtype=jnp.int32) * rows_dev
    keep = (starts[None, :] % (seq_len // pieces)[:, None] != 0).astype(F32)

    mix_row, ffn_row = mix_gain[None], ffn_gain[None]
    normed, pre, pre_out, local, decays, prefix, totals, angles, lags, *made = project(
        me_one, layer_index, tok, mix_row, pieces_w, kinds, w_proj, rows_all, groups, chans
    )
    if by_hand:
        w_proj, w_out = made[0].reshape(5 * chans, width), made[1].reshape(2 * chans, width)
    gain_row = angles[GAIN : GAIN + 2].reshape(1, 2 * chans)
    ends = lax.all_gather(totals, "mp", axis=0)
    states, entering, gated, mid, ffn_normed = mix(
        me_one,
        keep,
        ends,
        local,
        decays,
        prefix,
        angles,
        lags,
        pre_out,
        tok,
        w_out,
        gain_row,
        ffn_row,
        groups,
        chans,
    )
    core = (me & 1) if by_hand else jnp.zeros_like(me)
    core_one = core[None].astype(jnp.int32)
    chip_one = (me >> 1)[None].astype(jnp.int32)
    w_ffn = w_ffn.reshape(blocks, 3, units_dev, width)

    def reduction(same, other):
        return Reduction(same, other, chip_one, blocks, layers_z)

    act, d_pre, grad_ffn, w_pre = swiglu(ffn_normed, up_rows, w_ffn)
    grad_ffn = reduce_mp(grad_ffn)
    d_mid, d_outgate, back_local, suffix, back_totals, same, other, early_sums = mix_back(
        core_one,
        chans_dev,
        d_pre,
        w_pre,
        mid,
        up_rows,
        tok,
        states,
        pre_out,
        gated,
        normed,
        decays,
        w_out,
        gain_row,
        ffn_row,
        angles,
        groups,
        chans,
    )
    if by_hand:
        early = reduction(same, other)
    else:
        early = jnp.moveaxis(same.reshape(4, blocks, chans_dev, width), 1, 0)
    back_ends = lax.all_gather(back_totals, "mp", axis=0)
    if by_hand:
        back_ends = early.to_chips(early.arrived(back_ends))
        mid, back_ends = tied(mid, back_ends)
    out_result = from_rows(block_result(act, w_ffn, mid))
    if by_hand:
        back_ends, out_result = tied(back_ends, out_result)
    d_scan, sums, same, other = adjoint_finish(
        chans_dev,
        me_one,
        core_one,
        keep,
        back_ends,
        back_local,
        decays,
        suffix,
        pre,
        states,
        entering,
        angles,
        lags,
        normed,
        groups,
        chans,
    )
    if by_hand:
        other, d_scan = early.arrived(other, d_scan)
        late = reduction(same, other)
        early_share, d_scan = tied(early.share_here(), d_scan)
        early_got = along_layers(1, early_share)
    else:
        late = jnp.moveaxis(same.reshape(3, blocks, chans_dev, width), 1, 0)
    def finish(flat, late):
        late = late.reshape(3, chans_dev, width)
        own = me * chans_dev

        def own_part(row, offset):
            return lax.dynamic_slice(flat, (row, offset * chans + own), (1, chans_dev))[0]

        grad_gain = jnp.stack([own_part(2, 0), own_part(2, 1)], axis=0)
        below = jnp.arange(lower_logits.shape[0], dtype=jnp.int32) < layer_index[0]
        below = below.astype(F32)[:, None]
        soft = jax.nn.softmax(lower_logits, axis=0)
        bound_own = jnp.sum(soft * below, axis=0, keepdims=True)
        return (
            flat[0],
            jnp.transpose(late[0:2], (2, 0, 1)),
            jnp.transpose(late[2]),
            own_part(3, 0),
            soft * (below - bound_own) * own_part(3, 1)[None],
            grad_gain,
            flat[1],
        )

    grad_tokens, flat = tokens_back(
        d_scan, d_outgate, w_proj, tok, d_mid, mix_row, early_sums, sums, groups, chans
    )
    if by_hand:
        one, two, three = (swap(flat, "dp", bit, layers_z) for bit in (1, 2, 3))
        flat, early_got = tied((flat + one) + (two + three), early_got)
        flat, grad_tokens, grad_ffn = late.arrived(flat, grad_tokens, grad_ffn)
        same, got = late.same, late.flying[0]
        finished = lax.cond(
            layer_index[0] > 0,
            functools.partial(last_sums, finish, from_rows, (1, 2), blocks, layers_z),
            functools.partial(last_sums, finish, from_rows, (2, 1), blocks, layers_z),
            flat,
            chip_one,
            same,
            got,
            early_share,
            early_got,
            grad_tokens,
        )
    else:
        early = lax.psum(reduce_mp(early.reshape(blocks, -1, width)), "dp").astype(F32)
        late = lax.psum(reduce_mp(late.reshape(blocks, -1, width)), "dp").astype(F32)
        flat = lax.psum(flat, ("dp", "mp"))
    grad_ffn = lax.psum(grad_ffn.reshape(3 * units_dev, width), "dp")
    if by_hand:
        *finished, grad_ffn = tied(*finished, grad_ffn)
        *finished, g_output, g_outgate = finished
        g_gate, g_up, g_down = unpack(grad_ffn)
    else:
        finished = finish(flat, late)
        g_gate, g_up, g_down = grad_ffn.astype(F32).reshape(3, units_dev, width)
        g_output, g_outgate = early.reshape(2, 2, chans_dev, width)
    gain_mix, g_input, g_forget, g_phase, g_lower, g_gain, gain_ffn, *moved = finished
    out_tokens = moved[0] if moved else from_rows(grad_tokens)
    return (
        out_result,
        out_tokens,
        gain_mix,
        g_input,
        g_forget,
        jnp.transpose(g_outgate, (2, 0, 1)),
        g_phase,
        g_lower,
        g_gain,
        g_output,
        gain_ffn,
        jnp.transpose(g_gate),
        jnp.transpose(g_up),
        g_down,
    )


def solution(mesh):
    in_specs = (
        P("mp", "dp", None),
        P("mp", "dp", None),
        P("dp"),
        P(),
        P(),
        P(None, None, "mp"),
        P(None, "mp"),
        P(None, None, "mp"),
        P("mp"),
        P(None, "mp"),
        P(None, "mp"),
        P(None, "mp", None),
        P(),
        P(None, "mp"),
        P(None, "mp"),
        P("mp", None),
    )
    out_specs = (
        P("mp", "dp", None),
        P("mp", "dp", None),
        P(),
        P(None, None, "mp"),
        P(None, "mp"),
        P(None, None, "mp"),
        P("mp"),
        P(None, "mp"),
        P(None, "mp"),
        P(None, "mp", None),
        P(),
        P(None, "mp"),
        P(None, "mp"),
        P("mp", None),
    )
    return jax.shard_map(shards, mesh=mesh, in_specs=in_specs, out_specs=out_specs, check_vma=False)
```

```python
import functools

import jax
import jax.numpy as jnp
from jax import lax
from jax.experimental import pallas as pl
from jax.experimental.pallas import tpu as pltpu
from jax.sharding import PartitionSpec as P

EPSILON = 1e-06
CHUNKS = 8
TILE = 256
MIB = 1024 * 1024
F32 = jnp.float32
BF16 = jnp.bfloat16


class Near:
    def __init__(self, value):
        self.value = value


def kernel_call(body, grid, in_specs, out_specs, out_shape, scratch=(), vmem=32, free=()):
    def space(shape):
        if isinstance(shape, Near):
            return pltpu.VMEM(shape.value.shape, shape.value.dtype)
        return pltpu.HBM(shape.shape, shape.dtype) if shape.size >= 65536 else shape

    def placed(value):
        if isinstance(value, Near):
            return pltpu.with_memory_space_constraint(value.value, pltpu.VMEM)
        if value.size < 65536:
            return value
        return pltpu.with_memory_space_constraint(value, pltpu.HBM)

    single = not isinstance(out_shape, (list, tuple))
    call = pl.pallas_call(
        body,
        grid=grid,
        in_specs=in_specs,
        out_specs=out_specs,
        out_shape=space(out_shape) if single else [space(shape) for shape in out_shape],
        scratch_shapes=scratch,
        cost_estimate=pl.CostEstimate(flops=1, bytes_accessed=1, transcendentals=0),
        compiler_params=pltpu.CompilerParams(vmem_limit_bytes=vmem * MIB),
    )
    return lambda *args: call(
        *(arg if at in free else placed(arg) for at, arg in enumerate(args))
    )


def shaped(shape, dtype=F32):
    return jax.ShapeDtypeStruct(shape, dtype)


def whole(shape, start=None):
    start = start or (0,) * len(shape)
    return pl.BlockSpec(shape, lambda *_: start, pipeline_mode=pl.Buffered(1))


def kept(shape):
    zeros = (0,) * len(shape)
    return pl.BlockSpec(shape, lambda *_: zeros)


def per_group(shape):
    zeros = (0,) * (len(shape) - 1)
    return pl.BlockSpec(shape, lambda g, t: (g,) + zeros)


def ahead(tiles, rows, width):
    return pl.BlockSpec((rows, width), lambda g, t: (g * tiles + t, 0))


def behind(tiles, rows, width):
    return pl.BlockSpec((rows, width), lambda g, t: (g * tiles + tiles - 1 - t, 0))


SMEM_SPEC = pl.BlockSpec(memory_space=pltpu.SMEM)
VMEM_SPEC = pl.BlockSpec(memory_space=pltpu.VMEM)


def turn(cos, sin, re, im):
    return cos * re - sin * im, sin * re + cos * im


def back_turn(cos, sin, re, im):
    return cos * re + sin * im, cos * im - sin * re


def sigmoid(values):
    return 0.5 * jnp.tanh(0.5 * values) + 0.5


def nt(left, right):
    return lax.dot_general(left, right, (((1,), (1,)), ((), ())), preferred_element_type=F32)


def nn(left, right):
    return lax.dot_general(left, right, (((1,), (0,)), ((), ())), preferred_element_type=F32)


def tn(left, right):
    return lax.dot_general(left, right, (((0,), (0,)), ((), ())), preferred_element_type=F32)


def rms_rows(values):
    return lax.rsqrt(jnp.mean(values * values, axis=-1, keepdims=True) + EPSILON)


def rms_pull(unit, inv, gain, d_out):
    scaled = d_out * gain
    return inv * (scaled - unit * jnp.mean(scaled * unit, axis=-1, keepdims=True))


def step_rows(j):
    return pl.ds(pl.multiple_of(j * CHUNKS, CHUNKS), CHUNKS)


def chain_chunks(order, turning, angles, prod, end_re, end_im, chain, totals):
    cos_chunk, sin_chunk = angles[CHUNK : CHUNK + 1, :], angles[CHUNK + 1 : CHUNK + 2, :]
    zero = jnp.zeros_like(prod[0:1])
    run, run_re, run_im = zero + 1.0, zero, zero
    for s in order:
        chain[0, 0, s : s + 1, :] = run
        chain[0, 1, s : s + 1, :] = run_re
        chain[0, 2, s : s + 1, :] = run_im
        turned_re, turned_im = turning(cos_chunk, sin_chunk, run_re, run_im)
        run_re = prod[s : s + 1] * turned_re + end_re[s : s + 1]
        run_im = prod[s : s + 1] * turned_im + end_im[s : s + 1]
        run = run * prod[s : s + 1]
    totals[0] = jnp.zeros_like(prod)
    totals[0, 0:1, :] = run
    totals[0, 1:2, :] = run_re
    totals[0, 2:3, :] = run_im


BOUND, PHASE, ONE, CHUNK, DEVICE, GAIN = 0, 1, 2, 4, 6, 8


def channel_rows(logits, phase, out_gain):
    return jnp.concatenate([logits, phase[None], out_gain], axis=0)


def make_tables(rows, layer, steps, rows_dev, tables, lags):
    layers = rows.shape[0] - 3
    logits = rows[:layers]
    phase = rows[layers : layers + 1]
    grown = jnp.exp(logits - jnp.max(logits, axis=0, keepdims=True))
    below = lax.broadcasted_iota(jnp.int32, grown.shape, 0) < layer
    bound = jnp.sum(jnp.where(below, grown, 0.0), axis=0, keepdims=True)
    tables[BOUND : BOUND + 1, :] = bound / jnp.sum(grown, axis=0, keepdims=True)
    tables[PHASE : PHASE + 1, :] = phase
    for at, span in ((ONE, 1), (CHUNK, steps), (DEVICE, rows_dev)):
        tables[at : at + 1, :] = jnp.cos(phase * span)
        tables[at + 1 : at + 2, :] = jnp.sin(phase * span)
    tables[GAIN : GAIN + 2, :] = rows[layers + 1 :]
    count, chans = lags.shape[0], phase.shape[1]
    turns = phase * lax.broadcasted_iota(jnp.int32, (count, chans), 0).astype(F32)
    lags[:, 0:chans] = jnp.cos(turns)
    lags[:, chans:] = jnp.sin(turns)


def gathered_weights(chans, kinds, me, pieces, proj, w_out):
    size = chans // len(pieces)
    spare = pieces[0].shape[0] - 7 * size
    total = jnp.zeros((spare, chans), F32)
    column = lax.broadcasted_iota(jnp.int32, (128, chans), 1)
    row = lax.broadcasted_iota(jnp.int32, (128, chans), 0)
    for b, piece in enumerate(pieces):
        d = me[0] ^ b
        for k in range(5):
            proj[k, d] = piece[k * size : (k + 1) * size, :]
        for k in range(2):
            w_out[k, d] = piece[(5 + k) * size : (6 + k) * size, :]
        here = jnp.logical_and(column == d * size + row, row < size)
        total += nn(piece[7 * size :, 0:128], here.astype(F32).astype(BF16))
    return total[0:kinds] + total[kinds : 2 * kinds] + total[2 * kinds : 3 * kinds]


def project_body(steps, chans, count, kinds, per_dev, me, layer, tokens, gain, *refs):
    given, refs = refs[: max(count, 2)], refs[max(count, 2) :]
    normed, pre, pre_out, local, decays, prefix, totals, tables, lags, *made, carry = refs
    chunk = per_dev // CHUNKS

    @pl.when(first_step())
    def _():
        rows = gathered_weights(chans, kinds, me, given, *made) if count else given[1][...]
        make_tables(rows, layer[0], chunk, per_dev, tables, lags)

    w = made[0][...].reshape(5 * chans, made[0].shape[-1]) if count else given[0][...]
    t = pl.program_id(1)

    @pl.when(t == 0)
    def _():
        carry[0:2] = jnp.zeros((2,) + carry.shape[1:], F32)
        carry[2] = jnp.ones(carry.shape[1:], F32)

    values = tokens[...].astype(F32)
    unit = (values * rms_rows(values) * gain[...]).astype(BF16)
    normed[...] = unit
    low = tables[BOUND : BOUND + 1, :]
    scan = nt(unit, w[2 * chans : 5 * chans])
    pre[...] = scan.astype(BF16)
    decay = low + (1.0 - low) * sigmoid(scan[:, 2 * chans :])
    decays[...] = decay
    in_re, in_im = scan[:, 0:chans], scan[:, chans : 2 * chans]
    local[:, 0:chans] = (1.0 - decay) * (in_re * sigmoid(in_re))
    local[:, chans:] = (1.0 - decay) * (in_im * sigmoid(in_im))
    pre_out[...] = nt(unit, w[0 : 2 * chans]).astype(BF16)
    cos_one, sin_one = tables[ONE : ONE + 1, :], tables[ONE + 1 : ONE + 2, :]

    def step(j, state):
        state_re, state_im, prod = state
        rows = step_rows(j)
        decay = decays[rows, :]
        turned_re, turned_im = turn(cos_one, sin_one, state_re, state_im)
        state_re = decay * turned_re + local[rows, 0:chans]
        state_im = decay * turned_im + local[rows, chans:]
        local[rows, 0:chans] = state_re
        local[rows, chans:] = state_im
        return state_re, state_im, prod * decay

    end_re, end_im, prod = lax.fori_loop(
        0, steps, step, (carry[0], carry[1], carry[2]), unroll=8
    )
    carry[0], carry[1], carry[2] = end_re, end_im, prod

    @pl.when(t == pl.num_programs(1) - 1)
    def _():
        chain_chunks(range(CHUNKS), turn, tables, prod, end_re, end_im, prefix, totals)


def project(me, layer, tokens, gain, pieces, kinds, w_proj, rows_all, groups, chans):
    rows, width = tokens.shape
    per = rows // groups
    tile = min(2 * TILE, per)
    tiles = per // tile
    rowed = functools.partial(ahead, tiles, tile)
    made = [(5, 8, chans // 8, width), (2, 8, chans // 8, width)] if pieces else []
    given = pieces if pieces else [w_proj, rows_all]
    lags = (per // CHUNKS + 8, 2 * chans)
    return kernel_call(
        functools.partial(project_body, tile // CHUNKS, chans, len(pieces), kinds, per),
        (groups, tiles),
        [
            SMEM_SPEC,
            SMEM_SPEC,
            rowed(width),
            whole((1, width)),
            *(whole(value.shape) for value in given),
        ],
        [
            rowed(width),
            rowed(3 * chans),
            rowed(2 * chans),
            rowed(2 * chans),
            rowed(chans),
            per_group((1, 3, CHUNKS, chans)),
            per_group((1, CHUNKS, chans)),
            kept((16, chans)),
            kept(lags),
            *map(kept, made),
        ],
        [
            shaped((rows, width), BF16),
            shaped((rows, 3 * chans), BF16),
            shaped((rows, 2 * chans), BF16),
            Near(shaped((rows, 2 * chans))),
            shaped((rows, chans)),
            shaped((groups, 3, CHUNKS, chans)),
            shaped((groups, CHUNKS, chans)),
            shaped((16, chans)),
            shaped(lags),
            *(shaped(shape, BF16) for shape in made),
        ],
        [pltpu.VMEM((3, CHUNKS, chans), F32)],
        vmem=36,
    )(me, layer, tokens, gain, *given)


def mix_body(
    steps,
    chans,
    blocks,
    me,
    keep,
    gathered,
    local,
    decays,
    prefix,
    angles,
    table,
    pre_out,
    tokens,
    w_out,
    out_gain,
    ffn_gain,
    states,
    entering,
    gated,
    mid,
    ffn_normed,
    full,
    carry,
):
    g, t = pl.program_id(0), pl.program_id(1)

    @pl.when(t == 0)
    def _():
        cos_dev, sin_dev = angles[DEVICE : DEVICE + 1, :], angles[DEVICE + 1 : DEVICE + 2, :]
        state_re = jnp.zeros((1, chans), F32)
        state_im = jnp.zeros((1, chans), F32)
        for d in range(blocks):
            kept_one = keep[g, d]
            turned_re, turned_im = turn(cos_dev, sin_dev, kept_one * state_re, kept_one * state_im)
            decay = gathered[d, 0, 0:1, :]
            earlier = d < me[0]
            state_re = jnp.where(earlier, decay * turned_re + gathered[d, 0, 1:2, :], state_re)
            state_im = jnp.where(earlier, decay * turned_im + gathered[d, 0, 2:3, :], state_im)
        kept_one = keep[g, me[0]]
        state_re, state_im = kept_one * state_re, kept_one * state_im
        cos_chunk, sin_chunk = angles[CHUNK : CHUNK + 1, :], angles[CHUNK + 1 : CHUNK + 2, :]
        for s in range(CHUNKS):
            run = prefix[0, 0, s : s + 1, :]
            entering[0, 0, s : s + 1, :] = run * state_re + prefix[0, 1, s : s + 1, :]
            entering[0, 1, s : s + 1, :] = run * state_im + prefix[0, 2, s : s + 1, :]
            state_re, state_im = turn(cos_chunk, sin_chunk, state_re, state_im)
        carry[...] = jnp.ones_like(carry)

    enter_re, enter_im = entering[0, 0], entering[0, 1]

    def step(j, prod):
        rows = step_rows(j)
        prod = prod * decays[rows, :]
        lag = pl.ds(t * steps + j + 1, 1)
        turned_re, turned_im = turn(table[lag, 0:chans], table[lag, chans:], enter_re, enter_im)
        full[rows, 0:chans] = local[rows, 0:chans] + prod * turned_re
        full[rows, chans:] = local[rows, chans:] + prod * turned_im
        return prod

    carry[...] = lax.fori_loop(0, steps, step, carry[...], unroll=8)
    state = full[...]
    states[...] = state.astype(BF16)
    inv_rms = rms_rows(state)
    gate = pre_out[...].astype(F32)
    gate_in = (state * out_gain[...] * (gate * sigmoid(gate))).astype(BF16)
    gated[...] = gate_in
    stream = tokens[...].astype(F32) + inv_rms * nn(gate_in, w_out[...])
    mid[...] = stream
    ffn_normed[...] = (stream * rms_rows(stream) * ffn_gain[...]).astype(BF16)


def mix(
    me, keep, gathered, local, decays, prefix, angles, table, pre_out, tokens, w, out_gain, ffn_gain, groups, chans
):
    rows, width = tokens.shape
    per = rows // groups
    tile = min(TILE, per)
    tiles = per // tile
    blocks = gathered.shape[0]
    rowed = functools.partial(ahead, tiles, tile)
    return kernel_call(
        functools.partial(mix_body, tile // CHUNKS, chans, blocks),
        (groups, tiles),
        [
            SMEM_SPEC,
            SMEM_SPEC,
            pl.BlockSpec((blocks, 1, CHUNKS, chans), lambda g, t: (0, g, 0, 0)),
            rowed(2 * chans),
            rowed(chans),
            per_group((1, 3, CHUNKS, chans)),
            whole(angles.shape),
            whole(table.shape),
            rowed(2 * chans),
            rowed(width),
            whole((2 * chans, width)),
            whole((1, 2 * chans)),
            whole((1, width)),
        ],
        [
            rowed(2 * chans),
            per_group((1, 2, CHUNKS, chans)),
            rowed(2 * chans),
            rowed(width),
            rowed(width),
        ],
        [
            shaped((rows, 2 * chans), BF16),
            shaped((groups, 2, CHUNKS, chans)),
            shaped((rows, 2 * chans), BF16),
            shaped((rows, width)),
            shaped((rows, width), BF16),
        ],
        [pltpu.VMEM((tile, 2 * chans), F32), pltpu.VMEM((CHUNKS, chans), F32)],
    )(me, keep, gathered, Near(local), decays, prefix, angles, table, pre_out, tokens, w, out_gain, ffn_gain)


def split_by_core(first, grads, span, unit, same, other):
    for chip in range(span // (2 * unit)):
        for k, part in enumerate(grads):
            even = part[2 * chip * unit : (2 * chip + 1) * unit]
            odd = part[(2 * chip + 1) * unit : (2 * chip + 2) * unit]
            rows = slice(k * unit, (k + 1) * unit)
            same[chip, rows, :] = jnp.where(first, even, odd)
            other[chip, rows, :] = jnp.where(first, odd, even)


def swiglu_body(unit, tile, x, up, w, act, d_pre, grads, w_out):
    devices = w.shape[0]

    def every(part):
        return jnp.concatenate([w[dev, part] for dev in range(devices)], axis=0)

    span = devices * unit
    w_pre = jnp.concatenate([every(0), every(1)], axis=0)
    w_down = every(2)
    w_out[...] = w_pre
    for start in range(0, x.shape[0], tile):
        rows = slice(start, start + tile)
        pre = nt(x[rows, :], w_pre)
        d_hidden = nt(up[rows, :], w_down)
        gate, lift = pre[:, :span], pre[:, span:]
        sigma = sigmoid(gate)
        silu = gate * sigma
        act[rows, :] = (silu * lift).astype(BF16)
        d_pre[rows, :span] = (d_hidden * lift * (sigma + silu * (1.0 - sigma))).astype(BF16)
        d_pre[rows, span:] = (d_hidden * silu).astype(BF16)
    g_pre = tn(d_pre[...], x[...]).astype(BF16)
    g_down = tn(act[...], up[...]).astype(BF16)
    for dev in range(devices):
        own = slice(dev * unit, (dev + 1) * unit)
        grads[dev, 0:unit, :] = g_pre[own]
        grads[dev, unit : 2 * unit, :] = g_pre[span + dev * unit : span + (dev + 1) * unit]
        grads[dev, 2 * unit : 3 * unit, :] = g_down[own]


def units_at_once(blocks, unit):
    devices = 2
    while devices < blocks and (devices * unit % 128 or devices * unit < 384):
        devices *= 2
    return devices


def swiglu(x, up, w):
    rows, width = x.shape
    blocks, _, unit, _ = w.shape
    devices = units_at_once(blocks, unit)
    span = devices * unit
    return kernel_call(
        functools.partial(swiglu_body, unit, min(rows, 512)),
        (blocks // devices,),
        [
            whole((rows, width)),
            whole((rows, width)),
            pl.BlockSpec((devices, 3, unit, width), lambda q: (q, 0, 0, 0)),
        ],
        [
            pl.BlockSpec((rows, span), lambda q: (0, q)),
            pl.BlockSpec((rows, 2 * span), lambda q: (0, q)),
            pl.BlockSpec((devices, 3 * unit, width), lambda q: (q, 0, 0)),
            pl.BlockSpec((2 * span, width), lambda q: (q, 0)),
        ],
        [
            shaped((rows, blocks * unit), BF16),
            shaped((rows, 2 * blocks * unit), BF16),
            shaped((blocks, 3 * unit, width), BF16),
            shaped((2 * blocks * unit, width), BF16),
        ],
    )(x, up, w)


def finish_grads(core, grads, kinds, chans, unit, same, other):
    grads = [grad.astype(BF16) for grad in grads]
    if unit % 16:
        same[...] = jnp.concatenate(grads, axis=0)
        other[...] = jnp.zeros_like(other)
        return
    each = [grad[at : at + chans] for grad in grads for at in range(0, grad.shape[0], chans)]
    split_by_core(core[0] == 0, each, chans, unit, same, other)


def grads_shapes(kinds, chans, unit, width):
    if unit % 16:
        return [(kinds * chans, width), (16, width)]
    return [(chans // (2 * unit), kinds * unit, width)] * 2


def first_step():
    return jnp.logical_and(pl.program_id(0) == 0, pl.program_id(1) == 0)


def last_step():
    return jnp.logical_and(
        pl.program_id(0) == pl.num_programs(0) - 1, pl.program_id(1) == pl.num_programs(1) - 1
    )


def gain_share(grads, w, gain):
    return jnp.sum(grads * w[...].astype(F32), axis=0, keepdims=True) / gain[...]


def mix_back_body(
    steps,
    chans,
    unit_chans,
    core,
    d_pre,
    w_pre,
    mid,
    upstream,
    tokens,
    states,
    pre_out,
    gated,
    normed,
    decays,
    w_out,
    w_proj,
    mix_gain,
    out_gain,
    ffn_gain,
    angles,
    d_mid,
    d_outgate,
    local,
    suffix,
    totals,
    same,
    other,
    sums,
    d_mixes,
    d_gates,
    carry,
    gated_here,
    normed_here,
    w_here,
    arrivals,
):
    rows_here = steps * CHUNKS
    at = pl.program_id(0) * pl.num_programs(1) + pl.num_programs(1) - 1 - pl.program_id(1)
    here = pl.ds(pl.multiple_of(at * rows_here, rows_here), rows_here)

    fetches = [
        pltpu.make_async_copy(gated, gated_here, arrivals.at[0]),
        pltpu.make_async_copy(normed, normed_here, arrivals.at[1]),
        pltpu.make_async_copy(w_proj.at[pl.ds(0, 2 * chans)], w_here, arrivals.at[2]),
    ]

    @pl.when(first_step())
    def _():
        sums[...] = jnp.zeros_like(sums)
        for fetch in fetches:
            fetch.start()

    @pl.when(pl.program_id(1) == 0)
    def _():
        carry[0:2] = jnp.zeros((2,) + carry.shape[1:], F32)
        carry[2] = jnp.ones(carry.shape[1:], F32)

    d_norm = nn(d_pre[...], w_pre[...])
    stream = mid[...]
    inv_mid = rms_rows(stream)
    unit_mid = stream * inv_mid
    sums[0:1, :] += jnp.sum(d_norm * unit_mid, axis=0, keepdims=True)
    d_stream = upstream[...].astype(F32) + rms_pull(unit_mid, inv_mid, ffn_gain[...], d_norm)
    d_mid[...] = d_stream.astype(BF16)
    state = states[...].astype(F32)
    inv_rms = rms_rows(state)
    d_mix = (inv_rms * d_stream).astype(BF16)
    mixed = stream - tokens[...].astype(F32)
    d_square = (-0.5 / chans) * inv_rms * inv_rms * jnp.sum(d_stream * mixed, axis=-1, keepdims=True)
    d_gated = nt(d_mix, w_out[...])
    gate = pre_out[...].astype(F32)
    sigma = sigmoid(gate)
    silu = gate * sigma
    gain = out_gain[...]
    local[...] = d_gated * gain * silu + d_square * state
    d_state_gate = d_gated * state
    sums[1:2, :] += jnp.sum(d_state_gate * silu, axis=0, keepdims=True)
    d_gate = (d_state_gate * gain * (sigma + silu * (1.0 - sigma))).astype(BF16)
    d_outgate[...] = d_gate
    d_mixes[here, :] = d_mix
    d_gates[here, :] = d_gate
    cos_one, sin_one = angles[ONE : ONE + 1, :], angles[ONE + 1 : ONE + 2, :]

    def step(i, flow):
        flow_re, flow_im, prod = flow
        rows = step_rows(steps - 1 - i)
        grad_re = local[rows, 0:chans] + flow_re
        grad_im = local[rows, chans:] + flow_im
        local[rows, 0:chans] = grad_re
        local[rows, chans:] = grad_im
        decay = decays[rows, :]
        turned_re, turned_im = back_turn(cos_one, sin_one, grad_re, grad_im)
        return decay * turned_re, decay * turned_im, prod * decay

    end_re, end_im, prod = lax.fori_loop(
        0, steps, step, (carry[0], carry[1], carry[2]), unroll=8
    )
    carry[0], carry[1], carry[2] = end_re, end_im, prod

    @pl.when(pl.program_id(1) == pl.num_programs(1) - 1)
    def _():
        chain_chunks(reversed(range(CHUNKS)), back_turn, angles, prod, end_re, end_im, suffix, totals)

    @pl.when(last_step())
    def _():
        for fetch in fetches:
            fetch.wait()
        grads = [tn(gated_here[...], d_mixes[...]), tn(d_gates[...], normed_here[...])]
        sums[2:3, :] = gain_share(grads[1], w_here, mix_gain)
        finish_grads(core, grads, 4, chans, unit_chans, same, other)


def mix_back(
    core,
    unit_chans,
    d_pre,
    w_pre,
    mid,
    upstream,
    tokens,
    states,
    pre_out,
    gated,
    normed,
    decays,
    w,
    w_proj,
    mix_gain,
    out_gain,
    ffn_gain,
    angles,
    groups,
    chans,
):
    rows, width = mid.shape
    per = rows // groups
    tile = min(TILE, per)
    tiles = per // tile
    rowed = functools.partial(behind, tiles, tile)
    return kernel_call(
        functools.partial(mix_back_body, tile // CHUNKS, chans, unit_chans),
        (groups, tiles),
        [
            SMEM_SPEC,
            rowed(d_pre.shape[1]),
            whole(w_pre.shape),
            rowed(width),
            rowed(width),
            rowed(width),
            rowed(2 * chans),
            rowed(2 * chans),
            pl.BlockSpec(memory_space=pl.ANY),
            pl.BlockSpec(memory_space=pl.ANY),
            rowed(chans),
            whole((2 * chans, width)),
            pl.BlockSpec(memory_space=pl.ANY),
            whole((1, width)),
            whole((1, 2 * chans)),
            whole((1, width)),
            whole(angles.shape),
        ],
        [
            rowed(width),
            rowed(2 * chans),
            rowed(2 * chans),
            per_group((1, 3, CHUNKS, chans)),
            per_group((1, CHUNKS, chans)),
            *map(kept, grads_shapes(4, chans, unit_chans, width)),
            kept((8, width)),
        ],
        [
            shaped((rows, width), BF16),
            shaped((rows, 2 * chans), BF16),
            Near(shaped((rows, 2 * chans))),
            shaped((groups, 3, CHUNKS, chans)),
            shaped((groups, CHUNKS, chans)),
            *(shaped(shape, BF16) for shape in grads_shapes(4, chans, unit_chans, width)),
            shaped((8, width)),
        ],
        [
            pltpu.VMEM((rows, width), BF16),
            pltpu.VMEM((rows, 2 * chans), BF16),
            pltpu.VMEM((3, CHUNKS, chans), F32),
            pltpu.VMEM((rows, 2 * chans), BF16),
            pltpu.VMEM((rows, width), BF16),
            pltpu.VMEM((2 * chans, width), BF16),
            pltpu.SemaphoreType.DMA((3,)),
        ],
        vmem=42,
    )(
        core,
        d_pre,
        w_pre,
        mid,
        upstream,
        tokens,
        states,
        pre_out,
        gated,
        normed,
        decays,
        w,
        w_proj,
        mix_gain,
        out_gain,
        ffn_gain,
        angles,
    )


def silu_slope(values, sigma):
    return sigma * (1.0 + values * (1.0 - sigma))


def adjoint_finish_body(
    steps,
    chans,
    blocks,
    unit_chans,
    me,
    core,
    keep,
    gathered,
    local,
    decays,
    suffix,
    pre,
    states,
    before,
    entering,
    angles,
    table,
    normed,
    w_proj,
    mix_gain,
    early,
    d_pre,
    flat,
    same,
    other,
    leaving,
    full,
    d_pres,
    carry,
    sums,
    normed_here,
    w_here,
    arrivals,
):
    g, t = pl.program_id(0), pl.program_id(1)
    tiles = pl.num_programs(1)
    rows_here = steps * CHUNKS
    here = pl.ds(pl.multiple_of((g * tiles + tiles - 1 - t) * rows_here, rows_here), rows_here)
    fetches = [
        pltpu.make_async_copy(normed, normed_here, arrivals.at[0]),
        pltpu.make_async_copy(w_proj.at[pl.ds(2 * chans, 3 * chans)], w_here, arrivals.at[1]),
    ]

    @pl.when(first_step())
    def _():
        sums[...] = jnp.zeros_like(sums)
        for fetch in fetches:
            fetch.start()

    @pl.when(t == 0)
    def _():
        cos_chunk, sin_chunk = angles[CHUNK : CHUNK + 1, :], angles[CHUNK + 1 : CHUNK + 2, :]
        cos_dev, sin_dev = angles[DEVICE : DEVICE + 1, :], angles[DEVICE + 1 : DEVICE + 2, :]
        flow_re = jnp.zeros((1, chans), F32)
        flow_im = jnp.zeros((1, chans), F32)
        for d in reversed(range(blocks)):
            kept_one = keep[g, d]
            turned_re, turned_im = back_turn(cos_dev, sin_dev, flow_re, flow_im)
            decay = gathered[d, 0, 0:1, :]
            later = d > me[0]
            flow_re = jnp.where(
                later, kept_one * (decay * turned_re + gathered[d, 0, 1:2, :]), flow_re
            )
            flow_im = jnp.where(
                later, kept_one * (decay * turned_im + gathered[d, 0, 2:3, :]), flow_im
            )
        for s in reversed(range(CHUNKS)):
            run = suffix[0, 0, s : s + 1, :]
            leaving[0, s : s + 1, :] = run * flow_re + suffix[0, 1, s : s + 1, :]
            leaving[1, s : s + 1, :] = run * flow_im + suffix[0, 2, s : s + 1, :]
            flow_re, flow_im = back_turn(cos_chunk, sin_chunk, flow_re, flow_im)
        carry[...] = jnp.ones_like(carry)

    low = angles[BOUND : BOUND + 1, :]
    cos_one, sin_one = angles[ONE : ONE + 1, :], angles[ONE + 1 : ONE + 2, :]
    leave_re, leave_im = leaving[0], leaving[1]

    def step(i, prod):
        rows = step_rows(steps - 1 - i)
        lag = pl.ds(t * steps + i, 1)
        turned_re, turned_im = back_turn(table[lag, 0:chans], table[lag, chans:], leave_re, leave_im)
        full[rows, 0:chans] = local[rows, 0:chans] + prod * turned_re
        full[rows, chans:] = local[rows, chans:] + prod * turned_im
        return prod * decays[rows, :]

    carry[...] = lax.fori_loop(0, steps, step, carry[...], unroll=8)
    first_tile = t == tiles - 1
    last = before[...].astype(F32)[CHUNKS:]
    last_re = jnp.where(first_tile, entering[0, 0], last[:, 0:chans])
    last_im = jnp.where(first_tile, entering[0, 1], last[:, chans:])
    state = states[...].astype(F32)[: (steps - 1) * CHUNKS]
    last_re = jnp.concatenate([last_re, state[:, 0:chans]], axis=0)
    last_im = jnp.concatenate([last_im, state[:, chans:]], axis=0)
    grad_re, grad_im = full[:, 0:chans], full[:, chans:]
    scan = pre[...].astype(F32)
    in_re, in_im = scan[:, 0:chans], scan[:, chans : 2 * chans]
    sigma_re, sigma_im = sigmoid(in_re), sigmoid(in_im)
    sigma = sigmoid(scan[:, 2 * chans :])
    decay = decays[...]
    cross_re = grad_re * last_re + grad_im * last_im
    cross_im = grad_im * last_re - grad_re * last_im
    along, across = back_turn(cos_one, sin_one, cross_re, cross_im)
    d_decay = along - (grad_re * in_re * sigma_re + grad_im * in_im * sigma_im)
    rest = 1.0 - decay
    d_low = d_decay * (1.0 - sigma)
    d_re = (grad_re * rest * silu_slope(in_re, sigma_re)).astype(BF16)
    d_im = (grad_im * rest * silu_slope(in_im, sigma_im)).astype(BF16)
    d_forget = (d_low * (1.0 - low) * sigma).astype(BF16)
    d_all = jnp.concatenate([d_re, d_im, d_forget], axis=1)
    d_pre[...] = d_all
    d_pres[here, :] = d_all
    sums[0] += jnp.sum((decay * across).reshape(steps, CHUNKS, chans), axis=0)
    sums[1] += jnp.sum(d_low.reshape(steps, CHUNKS, chans), axis=0)

    @pl.when(last_step())
    def _():
        for fetch in fetches:
            fetch.wait()
        grads = tn(d_pres[...], normed_here[...])
        finish_grads(core, [grads], 3, chans, unit_chans, same, other)
        flat[...] = jnp.zeros_like(flat)
        flat[0:1, :] = early[2:3, :] + gain_share(grads, w_here, mix_gain)
        flat[1:3, :] = early[0:2, :]
        flat[3:4, 0:chans] = jnp.sum(sums[0], axis=0, keepdims=True)
        flat[3:4, chans:] = jnp.sum(sums[1], axis=0, keepdims=True)


def adjoint_finish(
    unit_chans,
    me,
    core,
    keep,
    gathered,
    local,
    decays,
    suffix,
    pre,
    states,
    entering,
    angles,
    table,
    normed,
    w_proj,
    mix_gain,
    early,
    groups,
    chans,
):
    rows, width = normed.shape
    per = rows // groups
    tile = min(TILE, per)
    tiles = per // tile
    steps = tile // CHUNKS
    blocks = gathered.shape[0]
    rowed = functools.partial(behind, tiles, tile)

    def one_before(g, t):
        return (jnp.maximum((g * tiles + tiles - 1 - t) * (steps // 2) - 1, 0), 0)

    return kernel_call(
        functools.partial(adjoint_finish_body, steps, chans, blocks, unit_chans),
        (groups, tiles),
        [
            SMEM_SPEC,
            SMEM_SPEC,
            SMEM_SPEC,
            pl.BlockSpec((blocks, 1, CHUNKS, chans), lambda g, t: (0, g, 0, 0)),
            rowed(2 * chans),
            rowed(chans),
            per_group((1, 3, CHUNKS, chans)),
            rowed(3 * chans),
            rowed(2 * chans),
            pl.BlockSpec((2 * CHUNKS, 2 * chans), one_before),
            per_group((1, 2, CHUNKS, chans)),
            whole(angles.shape),
            whole(table.shape),
            pl.BlockSpec(memory_space=pl.ANY),
            pl.BlockSpec(memory_space=pl.ANY),
            whole((1, width)),
            whole(early.shape),
        ],
        [
            rowed(3 * chans),
            kept((8, width)),
            *map(kept, grads_shapes(3, chans, unit_chans, width)),
        ],
        [
            shaped((rows, 3 * chans), BF16),
            shaped((8, width)),
            *(shaped(shape, BF16) for shape in grads_shapes(3, chans, unit_chans, width)),
        ],
        [
            pltpu.VMEM((2, CHUNKS, chans), F32),
            pltpu.VMEM((tile, 2 * chans), F32),
            pltpu.VMEM((rows, 3 * chans), BF16),
            pltpu.VMEM((CHUNKS, chans), F32),
            pltpu.VMEM((2, CHUNKS, chans), F32),
            pltpu.VMEM((rows, width), BF16),
            pltpu.VMEM((3 * chans, width), BF16),
            pltpu.SemaphoreType.DMA((2,)),
        ],
    )(
        me,
        core,
        keep,
        gathered,
        Near(local),
        decays,
        suffix,
        pre,
        states,
        states,
        entering,
        angles,
        table,
        normed,
        w_proj,
        mix_gain,
        early,
    )


def tokens_back_body(chans, d_scan, d_outgate, w, tokens, d_mid, gain, grad_tokens):
    d_normed = nn(d_scan[...], w[2 * chans : 5 * chans, :])
    d_normed += nn(d_outgate[...], w[0 : 2 * chans, :])
    values = tokens[...].astype(F32)
    inv = rms_rows(values)
    grad_tokens[...] = (
        d_mid[...].astype(F32) + rms_pull(values * inv, inv, gain[...], d_normed)
    ).astype(BF16)


def tokens_back(d_scan, d_outgate, w, tokens, d_mid, gain, groups, chans):
    rows, width = tokens.shape
    per = rows // groups
    tile = min(TILE, per)
    tiles = per // tile
    rowed = functools.partial(ahead, tiles, tile)
    return kernel_call(
        functools.partial(tokens_back_body, chans),
        (groups, tiles),
        [
            rowed(3 * chans),
            rowed(2 * chans),
            whole(w.shape),
            rowed(width),
            rowed(width),
            whole((1, width)),
        ],
        rowed(width),
        Near(shaped((rows, width), BF16)),
        vmem=20,
    )(d_scan, d_outgate, w, tokens, d_mid, gain)


def result_body(act, w_down, mid, result):
    blocks = w_down.shape[0]
    down = jnp.concatenate([w_down[dev, 0] for dev in range(blocks)], axis=0)
    result[...] = (mid[...] + nn(act[...], down)).astype(BF16)


def block_result(act, w_ffn, mid):
    rows, width = mid.shape
    blocks, _, units, _ = w_ffn.shape
    tile = min(TILE, rows)

    def rowed(wide):
        return pl.BlockSpec((tile, wide), lambda i: (i, 0))

    return kernel_call(
        result_body,
        (rows // tile,),
        [rowed(act.shape[1]), whole((blocks, 1, units, width), (0, 2, 0, 0)), rowed(width)],
        rowed(width),
        Near(shaped((rows, width), BF16)),
        vmem=20,
    )(act, w_ffn, mid)


def unpack_body(ffn, gate, up, down):
    rows = gate.shape[0]
    for k, out in enumerate((gate, up, down)):
        out[...] = ffn[k * rows : (k + 1) * rows, :].astype(F32)


def unpack(ffn):
    rows, width = ffn.shape[0] // 3, ffn.shape[1]
    return kernel_call(
        unpack_body,
        (1,),
        [whole(ffn.shape)],
        [whole((rows, width))] * 3,
        [shaped((rows, width))] * 3,
        vmem=16,
    )(ffn)


def swap(values, axis, bit, size):
    return lax.ppermute(values, axis, [(i, i ^ bit) for i in range(size)])


def joined(*parts):
    return sum(part.astype(F32) for part in parts)


def pick(values, index, axis):
    return lax.dynamic_index_in_dim(values, index, axis, keepdims=False)


def gather_pieces(shard, size, *others):
    half = shard.shape[0] // 32 * 16
    near_x = swap(shard, "mp", 2, size)
    near_y = swap(shard, "mp", 4, size)
    core = swap(shard, "mp", 1, size)
    near_x, near_y, *others = tied(near_x, near_y, *others)
    far_one = swap(near_x[:half], "mp", 4, size)
    far_two = swap(near_y[half:], "mp", 2, size)
    core_x = swap(near_x, "mp", 1, size)
    core_y = swap(near_y, "mp", 1, size)
    far = jnp.concatenate([far_one, far_two], axis=0)
    core_far = swap(far, "mp", 1, size)
    return [shard, core, near_x, core_x, near_y, core_y, far, core_far], *others


def reduce_mp(grads):
    return lax.psum_scatter(grads, "mp", scatter_dimension=0, tiled=False)


def sends_body(chip, same, got, out_x, out_y, out_far):
    for b, out in ((1, out_x), (2, out_y), (3, out_far)):
        at = chip[0] ^ b
        out[...] = (same[at].astype(F32) + got[at].astype(F32)).astype(BF16)


def sends(chip, same, got):
    return pl.pallas_call(
        sends_body,
        in_specs=[SMEM_SPEC, VMEM_SPEC, VMEM_SPEC],
        out_specs=[VMEM_SPEC] * 3,
        out_shape=[jax.ShapeDtypeStruct(same.shape[1:], BF16)] * 3,
        cost_estimate=pl.CostEstimate(flops=1, bytes_accessed=1, transcendentals=0),
        compiler_params=pltpu.CompilerParams(vmem_limit_bytes=16 * MIB),
    )(chip, same, got)


def last_sums(finish, from_rows, order, size, layers, flat, chip, same, got, early, early_got, tokens):
    last = Reduction(same, None, chip, size, layers)
    last.flying = [got]
    early = both(early, early_got)
    early_got = along_layers(2, early)
    flat = flat + swap(flat, "mp", 2 * order[0], size)
    flat, tokens = tied(last.to_chips(flat), tokens)
    flat = flat + swap(flat, "mp", 2 * order[1], size)
    moved = from_rows(tokens)
    late, flat, moved, early_got = tied(last.share_here(), flat, moved, early_got)
    one, two, three = (swap(late, "dp", bit, layers) for bit in (1, 2, 3))
    early = both(early, early_got)
    early_got = along_layers(3, early)
    flat = flat + swap(flat, "mp", 1, size)
    late = joined(joined(late, one), joined(two, three))
    early = settled(early, early_got).reshape(2, 2, -1, early.shape[-1])
    return (*finish(flat, late), moved, early[0], early[1])


class Reduction:
    def __init__(self, same, other, chip, size, layers):
        self.same, self.chip, self.size, self.layers = same, chip, size, layers
        self.flying = [] if other is None else [swap(other, "mp", 1, size)]

    def arrived(self, *others):
        count = len(self.flying)
        both = tied(*self.flying, *others)
        self.flying = both[:count]
        return both[count:] if len(others) > 1 else both[-1]

    def to_chips(self, other):
        self.got = self.flying[0]
        *parts, other = tied(*sends(self.chip, self.same, self.got), other)
        self.flying = [swap(part, "mp", 2 * b, self.size) for b, part in zip((1, 2, 3), parts)]
        return other

    def share_here(self):
        at = self.chip[0]
        mine = pick(self.same, at, 0), pick(self.got, at, 0)
        return joined(*mine, *self.flying).astype(BF16)


def along_layers(number, share):
    pairs = {1: [(0, 1), (3, 2)], 2: [(1, 2), (2, 1)], 3: [(1, 0), (2, 3)]}[number]
    return lax.ppermute(share, "dp", pairs)


def both(share, got):
    return joined(share, got).astype(BF16)


def settled(share, got):
    z = lax.axis_index("dp")
    inner = jnp.logical_or(z == 1, z == 2)
    return jnp.where(inner, share, got).astype(F32)


def split_three(values):
    one = lax.reduce_precision(values, 8, 7)
    two = lax.reduce_precision(values - one, 8, 7)
    three = values - one - two
    return jnp.stack([one, two, three], axis=0).astype(BF16)


def tied(*values):
    return lax.optimization_barrier(values)


def shards(
    tokens,
    upstream,
    pieces,
    layer_index,
    mix_gain,
    w_input,
    w_forget,
    w_outgate,
    phase_angle,
    lower_logits,
    out_gain,
    w_output,
    ffn_gain,
    w_gate,
    w_up,
    w_down,
):
    rows_dev, groups, width = tokens.shape
    blocks = lax.axis_size("mp")
    me = lax.axis_index("mp")
    layers_z = lax.axis_size("dp")
    seq_len = rows_dev * blocks
    chans_dev = w_input.shape[2]
    chans = chans_dev * blocks
    units_dev = w_gate.shape[1]
    units = units_dev * blocks
    steps = rows_dev // CHUNKS
    rows = rows_dev * groups

    def to_rows(values):
        return jnp.transpose(
            values.reshape(CHUNKS, steps, groups, width), (2, 1, 0, 3)
        ).reshape(rows, width)

    def from_rows(values):
        return jnp.transpose(
            values.reshape(groups, steps, CHUNKS, width), (2, 1, 0, 3)
        ).reshape(rows_dev, groups, width)

    me_one = me[None].astype(jnp.int32)
    rows_own = channel_rows(lower_logits, phase_angle, out_gain)
    kinds = rows_own.shape[0]
    by_hand = blocks == 8 and layers_z == 4 and chans_dev % 16 == 0
    mix_shard = jnp.concatenate(
        [
            jnp.transpose(w_outgate, (1, 2, 0)),
            jnp.transpose(w_input, (1, 2, 0)),
            jnp.transpose(w_forget)[None],
            w_output,
        ],
        axis=0,
    )
    ffn_parts = jnp.transpose(w_gate), jnp.transpose(w_up), w_down
    tok, up_rows = to_rows(tokens), to_rows(upstream)
    pieces_w, w_proj, rows_all = [], None, None
    if by_hand:
        terms = split_three(rows_own).reshape(3 * kinds, chans_dev)
        spare = (3 * kinds + 15) // 16 * 16
        terms = jnp.pad(terms, ((0, spare - 3 * kinds), (0, width - chans_dev)))
        own = jnp.concatenate([mix_shard.reshape(7 * chans_dev, width), terms], axis=0)
        own, *ffn_parts = tied(own, *ffn_parts)
        pieces_w, tok, up_rows = gather_pieces(own, blocks, tok, up_rows)
    else:
        w_mix = lax.all_gather(mix_shard, "mp", axis=0)
        w_mix = jnp.transpose(w_mix, (1, 0, 2, 3)).reshape(7 * chans, width)
        w_proj, w_out = w_mix[: 5 * chans], w_mix[5 * chans :]
        rows_all = lax.all_gather(rows_own, "mp", axis=0)
        rows_all = jnp.transpose(rows_all, (1, 0, 2)).reshape(kinds, chans)
    w_ffn = lax.all_gather(jnp.concatenate(ffn_parts, axis=0), "mp", axis=0)
    starts = jnp.arange(blocks, dtype=jnp.int32) * rows_dev
    keep = (starts[None, :] % (seq_len // pieces)[:, None] != 0).astype(F32)

    mix_row, ffn_row = mix_gain[None], ffn_gain[None]
    normed, pre, pre_out, local, decays, prefix, totals, angles, lags, *made = project(
        me_one, layer_index, tok, mix_row, pieces_w, kinds, w_proj, rows_all, groups, chans
    )
    if by_hand:
        w_proj, w_out = made[0].reshape(5 * chans, width), made[1].reshape(2 * chans, width)
    gain_row = angles[GAIN : GAIN + 2].reshape(1, 2 * chans)
    ends = lax.all_gather(totals, "mp", axis=0)
    states, entering, gated, mid, ffn_normed = mix(
        me_one,
        keep,
        ends,
        local,
        decays,
        prefix,
        angles,
        lags,
        pre_out,
        tok,
        w_out,
        gain_row,
        ffn_row,
        groups,
        chans,
    )
    core = (me & 1) if by_hand else jnp.zeros_like(me)
    core_one = core[None].astype(jnp.int32)
    chip_one = (me >> 1)[None].astype(jnp.int32)
    w_ffn = w_ffn.reshape(blocks, 3, units_dev, width)

    def reduction(same, other):
        return Reduction(same, other, chip_one, blocks, layers_z)

    act, d_pre, grad_ffn, w_pre = swiglu(ffn_normed, up_rows, w_ffn)
    grad_ffn = reduce_mp(grad_ffn)
    d_mid, d_outgate, back_local, suffix, back_totals, same, other, early_sums = mix_back(
        core_one,
        chans_dev,
        d_pre,
        w_pre,
        mid,
        up_rows,
        tok,
        states,
        pre_out,
        gated,
        normed,
        decays,
        w_out,
        w_proj,
        mix_row,
        gain_row,
        ffn_row,
        angles,
        groups,
        chans,
    )
    if by_hand:
        early = reduction(same, other)
    else:
        early = jnp.moveaxis(same.reshape(4, blocks, chans_dev, width), 1, 0)
    back_ends = lax.all_gather(back_totals, "mp", axis=0)
    if by_hand:
        back_ends = early.to_chips(early.arrived(back_ends))
        mid, back_ends = tied(mid, back_ends)
    out_result = from_rows(block_result(act, w_ffn, mid))
    if by_hand:
        back_ends, out_result = tied(back_ends, out_result)
    d_scan, flat, same, other = adjoint_finish(
        chans_dev,
        me_one,
        core_one,
        keep,
        back_ends,
        back_local,
        decays,
        suffix,
        pre,
        states,
        entering,
        angles,
        lags,
        normed,
        w_proj,
        mix_row,
        early_sums,
        groups,
        chans,
    )
    if by_hand:
        other, d_scan = early.arrived(other, d_scan)
        late = reduction(same, other)
        early_share, d_scan = tied(early.share_here(), d_scan)
        early_got = along_layers(1, early_share)
    else:
        late = jnp.moveaxis(same.reshape(3, blocks, chans_dev, width), 1, 0)
    def finish(flat, late):
        late = late.reshape(3, chans_dev, width)
        own = me * chans_dev

        def own_part(row, offset):
            return lax.dynamic_slice(flat, (row, offset * chans + own), (1, chans_dev))[0]

        grad_gain = jnp.stack([own_part(2, 0), own_part(2, 1)], axis=0)
        below = jnp.arange(lower_logits.shape[0], dtype=jnp.int32) < layer_index[0]
        below = below.astype(F32)[:, None]
        soft = jax.nn.softmax(lower_logits, axis=0)
        bound_own = jnp.sum(soft * below, axis=0, keepdims=True)
        return (
            flat[0],
            jnp.transpose(late[0:2], (2, 0, 1)),
            jnp.transpose(late[2]),
            own_part(3, 0),
            soft * (below - bound_own) * own_part(3, 1)[None],
            grad_gain,
            flat[1],
        )

    if by_hand:
        one, two, three = (swap(flat, "dp", bit, layers_z) for bit in (1, 2, 3))
    grad_tokens = tokens_back(d_scan, d_outgate, w_proj, tok, d_mid, mix_row, groups, chans)
    if by_hand:
        grad_tokens, one, two, three = tied(grad_tokens, one, two, three)
        flat, early_got = tied((flat + one) + (two + three), early_got)
        flat, grad_tokens, grad_ffn = late.arrived(flat, grad_tokens, grad_ffn)
        same, got = late.same, late.flying[0]
        finished = lax.cond(
            layer_index[0] > 0,
            functools.partial(last_sums, finish, from_rows, (1, 2), blocks, layers_z),
            functools.partial(last_sums, finish, from_rows, (2, 1), blocks, layers_z),
            flat,
            chip_one,
            same,
            got,
            early_share,
            early_got,
            grad_tokens,
        )
    else:
        early = lax.psum(reduce_mp(early.reshape(blocks, -1, width)), "dp").astype(F32)
        late = lax.psum(reduce_mp(late.reshape(blocks, -1, width)), "dp").astype(F32)
        flat = lax.psum(flat, ("dp", "mp"))
    grad_ffn = lax.psum(grad_ffn.reshape(3 * units_dev, width), "dp")
    if by_hand:
        *finished, grad_ffn = tied(*finished, grad_ffn)
        *finished, g_output, g_outgate = finished
        g_gate, g_up, g_down = unpack(grad_ffn)
    else:
        finished = finish(flat, late)
        g_gate, g_up, g_down = grad_ffn.astype(F32).reshape(3, units_dev, width)
        g_output, g_outgate = early.reshape(2, 2, chans_dev, width)
    gain_mix, g_input, g_forget, g_phase, g_lower, g_gain, gain_ffn, *moved = finished
    out_tokens = moved[0] if moved else from_rows(grad_tokens)
    return (
        out_result,
        out_tokens,
        gain_mix,
        g_input,
        g_forget,
        jnp.transpose(g_outgate, (2, 0, 1)),
        g_phase,
        g_lower,
        g_gain,
        g_output,
        gain_ffn,
        jnp.transpose(g_gate),
        jnp.transpose(g_up),
        g_down,
    )


def solution(mesh):
    in_specs = (
        P("mp", "dp", None),
        P("mp", "dp", None),
        P("dp"),
        P(),
        P(),
        P(None, None, "mp"),
        P(None, "mp"),
        P(None, None, "mp"),
        P("mp"),
        P(None, "mp"),
        P(None, "mp"),
        P(None, "mp", None),
        P(),
        P(None, "mp"),
        P(None, "mp"),
        P("mp", None),
    )
    out_specs = (
        P("mp", "dp", None),
        P("mp", "dp", None),
        P(),
        P(None, None, "mp"),
        P(None, "mp"),
        P(None, None, "mp"),
        P("mp"),
        P(None, "mp"),
        P(None, "mp"),
        P(None, "mp", None),
        P(),
        P(None, "mp"),
        P(None, "mp"),
        P("mp", None),
    )
    return jax.shard_map(shards, mesh=mesh, in_specs=in_specs, out_specs=out_specs, check_vma=False)
```

```python
import functools

import jax
import jax.numpy as jnp
from jax import lax
from jax.experimental import pallas as pl
from jax.experimental.pallas import tpu as pltpu
from jax.sharding import PartitionSpec as P

EPSILON = 1e-06
CHUNKS = 8
TILE = 256
MIB = 1024 * 1024
F32 = jnp.float32
BF16 = jnp.bfloat16


class Near:
    def __init__(self, value):
        self.value = value


def kernel_call(body, grid, in_specs, out_specs, out_shape, scratch=(), vmem=32, free=()):
    def space(shape):
        if isinstance(shape, Near):
            return pltpu.VMEM(shape.value.shape, shape.value.dtype)
        return pltpu.HBM(shape.shape, shape.dtype) if shape.size >= 65536 else shape

    def placed(value):
        if isinstance(value, Near):
            return pltpu.with_memory_space_constraint(value.value, pltpu.VMEM)
        if value.size < 65536:
            return value
        return pltpu.with_memory_space_constraint(value, pltpu.HBM)

    single = not isinstance(out_shape, (list, tuple))
    call = pl.pallas_call(
        body,
        grid=grid,
        in_specs=in_specs,
        out_specs=out_specs,
        out_shape=space(out_shape) if single else [space(shape) for shape in out_shape],
        scratch_shapes=scratch,
        cost_estimate=pl.CostEstimate(flops=1, bytes_accessed=1, transcendentals=0),
        compiler_params=pltpu.CompilerParams(vmem_limit_bytes=vmem * MIB),
    )
    return lambda *args: call(
        *(arg if at in free else placed(arg) for at, arg in enumerate(args))
    )


def shaped(shape, dtype=F32):
    return jax.ShapeDtypeStruct(shape, dtype)


def whole(shape, start=None):
    start = start or (0,) * len(shape)
    return pl.BlockSpec(shape, lambda *_: start, pipeline_mode=pl.Buffered(1))


def kept(shape):
    zeros = (0,) * len(shape)
    return pl.BlockSpec(shape, lambda *_: zeros)


def per_group(shape):
    zeros = (0,) * (len(shape) - 1)
    return pl.BlockSpec(shape, lambda g, t: (g,) + zeros)


def ahead(tiles, rows, width):
    return pl.BlockSpec((rows, width), lambda g, t: (g * tiles + t, 0))


def behind(tiles, rows, width):
    return pl.BlockSpec((rows, width), lambda g, t: (g * tiles + tiles - 1 - t, 0))


SMEM_SPEC = pl.BlockSpec(memory_space=pltpu.SMEM)
VMEM_SPEC = pl.BlockSpec(memory_space=pltpu.VMEM)


def turn(cos, sin, re, im):
    return cos * re - sin * im, sin * re + cos * im


def back_turn(cos, sin, re, im):
    return cos * re + sin * im, cos * im - sin * re


def sigmoid(values):
    return 0.5 * jnp.tanh(0.5 * values) + 0.5


def nt(left, right):
    return lax.dot_general(left, right, (((1,), (1,)), ((), ())), preferred_element_type=F32)


def nn(left, right):
    return lax.dot_general(left, right, (((1,), (0,)), ((), ())), preferred_element_type=F32)


def tn(left, right):
    return lax.dot_general(left, right, (((0,), (0,)), ((), ())), preferred_element_type=F32)


def rms_rows(values):
    return lax.rsqrt(jnp.mean(values * values, axis=-1, keepdims=True) + EPSILON)


def rms_pull(unit, inv, gain, d_out):
    scaled = d_out * gain
    return inv * (scaled - unit * jnp.mean(scaled * unit, axis=-1, keepdims=True))


def step_rows(j):
    return pl.ds(pl.multiple_of(j * CHUNKS, CHUNKS), CHUNKS)


def chain_chunks(order, turning, angles, prod, end_re, end_im, chain, totals):
    cos_chunk, sin_chunk = angles[CHUNK : CHUNK + 1, :], angles[CHUNK + 1 : CHUNK + 2, :]
    zero = jnp.zeros_like(prod[0:1])
    run, run_re, run_im = zero + 1.0, zero, zero
    for s in order:
        chain[0, 0, s : s + 1, :] = run
        chain[0, 1, s : s + 1, :] = run_re
        chain[0, 2, s : s + 1, :] = run_im
        turned_re, turned_im = turning(cos_chunk, sin_chunk, run_re, run_im)
        run_re = prod[s : s + 1] * turned_re + end_re[s : s + 1]
        run_im = prod[s : s + 1] * turned_im + end_im[s : s + 1]
        run = run * prod[s : s + 1]
    totals[0] = jnp.zeros_like(prod)
    totals[0, 0:1, :] = run
    totals[0, 1:2, :] = run_re
    totals[0, 2:3, :] = run_im


BOUND, PHASE, ONE, CHUNK, DEVICE, GAIN = 0, 1, 2, 4, 6, 8


def channel_rows(logits, phase, out_gain):
    return jnp.concatenate([logits, phase[None], out_gain], axis=0)


def make_tables(rows, layer, steps, rows_dev, tables, lags):
    layers = rows.shape[0] - 3
    logits = rows[:layers]
    phase = rows[layers : layers + 1]
    grown = jnp.exp(logits - jnp.max(logits, axis=0, keepdims=True))
    below = lax.broadcasted_iota(jnp.int32, grown.shape, 0) < layer
    bound = jnp.sum(jnp.where(below, grown, 0.0), axis=0, keepdims=True)
    tables[BOUND : BOUND + 1, :] = bound / jnp.sum(grown, axis=0, keepdims=True)
    tables[PHASE : PHASE + 1, :] = phase
    for at, span in ((ONE, 1), (CHUNK, steps), (DEVICE, rows_dev)):
        tables[at : at + 1, :] = jnp.cos(phase * span)
        tables[at + 1 : at + 2, :] = jnp.sin(phase * span)
    tables[GAIN : GAIN + 2, :] = rows[layers + 1 :]
    count, chans = lags.shape[0], phase.shape[1]
    turns = phase * lax.broadcasted_iota(jnp.int32, (count, chans), 0).astype(F32)
    lags[:, 0:chans] = jnp.cos(turns)
    lags[:, chans:] = jnp.sin(turns)


def gathered_weights(chans, kinds, me, pieces, proj, w_out):
    size = chans // len(pieces)
    spare = pieces[0].shape[0] - 7 * size
    total = jnp.zeros((spare, chans), F32)
    column = lax.broadcasted_iota(jnp.int32, (128, chans), 1)
    row = lax.broadcasted_iota(jnp.int32, (128, chans), 0)
    for b, piece in enumerate(pieces):
        d = me[0] ^ b
        for k in range(5):
            proj[k, d] = piece[k * size : (k + 1) * size, :]
        for k in range(2):
            w_out[k, d] = piece[(5 + k) * size : (6 + k) * size, :]
        here = jnp.logical_and(column == d * size + row, row < size)
        total += nn(piece[7 * size :, 0:128], here.astype(F32).astype(BF16))
    return total[0:kinds] + total[kinds : 2 * kinds] + total[2 * kinds : 3 * kinds]


def project_body(steps, chans, count, kinds, per_dev, me, layer, tokens, gain, *refs):
    given, refs = refs[: max(count, 2)], refs[max(count, 2) :]
    normed, pre, pre_out, local, decays, prefix, totals, tables, lags, *made, carry = refs
    chunk = per_dev // CHUNKS

    @pl.when(first_step())
    def _():
        rows = gathered_weights(chans, kinds, me, given, *made) if count else given[1][...]
        make_tables(rows, layer[0], chunk, per_dev, tables, lags)

    w = made[0][...].reshape(5 * chans, made[0].shape[-1]) if count else given[0][...]
    t = pl.program_id(1)

    @pl.when(t == 0)
    def _():
        carry[0:2] = jnp.zeros((2,) + carry.shape[1:], F32)
        carry[2] = jnp.ones(carry.shape[1:], F32)

    values = tokens[...].astype(F32)
    unit = (values * rms_rows(values) * gain[...]).astype(BF16)
    normed[...] = unit
    low = tables[BOUND : BOUND + 1, :]
    scan = nt(unit, w[2 * chans : 5 * chans])
    pre[...] = scan.astype(BF16)
    decay = low + (1.0 - low) * sigmoid(scan[:, 2 * chans :])
    decays[...] = decay
    in_re, in_im = scan[:, 0:chans], scan[:, chans : 2 * chans]
    local[:, 0:chans] = (1.0 - decay) * (in_re * sigmoid(in_re))
    local[:, chans:] = (1.0 - decay) * (in_im * sigmoid(in_im))
    pre_out[...] = nt(unit, w[0 : 2 * chans]).astype(BF16)
    cos_one, sin_one = tables[ONE : ONE + 1, :], tables[ONE + 1 : ONE + 2, :]

    def step(j, state):
        state_re, state_im, prod = state
        rows = step_rows(j)
        decay = decays[rows, :]
        turned_re, turned_im = turn(cos_one, sin_one, state_re, state_im)
        state_re = decay * turned_re + local[rows, 0:chans]
        state_im = decay * turned_im + local[rows, chans:]
        local[rows, 0:chans] = state_re
        local[rows, chans:] = state_im
        return state_re, state_im, prod * decay

    end_re, end_im, prod = lax.fori_loop(
        0, steps, step, (carry[0], carry[1], carry[2]), unroll=8
    )
    carry[0], carry[1], carry[2] = end_re, end_im, prod

    @pl.when(t == pl.num_programs(1) - 1)
    def _():
        chain_chunks(range(CHUNKS), turn, tables, prod, end_re, end_im, prefix, totals)


def project(me, layer, tokens, gain, pieces, kinds, w_proj, rows_all, groups, chans):
    rows, width = tokens.shape
    per = rows // groups
    tile = min(2 * TILE, per)
    tiles = per // tile
    rowed = functools.partial(ahead, tiles, tile)
    made = [(5, 8, chans // 8, width), (2, 8, chans // 8, width)] if pieces else []
    given = pieces if pieces else [w_proj, rows_all]
    lags = (per // CHUNKS + 8, 2 * chans)
    return kernel_call(
        functools.partial(project_body, tile // CHUNKS, chans, len(pieces), kinds, per),
        (groups, tiles),
        [
            SMEM_SPEC,
            SMEM_SPEC,
            rowed(width),
            whole((1, width)),
            *(whole(value.shape) for value in given),
        ],
        [
            rowed(width),
            rowed(3 * chans),
            rowed(2 * chans),
            rowed(2 * chans),
            rowed(chans),
            per_group((1, 3, CHUNKS, chans)),
            per_group((1, CHUNKS, chans)),
            kept((16, chans)),
            kept(lags),
            *map(kept, made),
        ],
        [
            shaped((rows, width), BF16),
            shaped((rows, 3 * chans), BF16),
            shaped((rows, 2 * chans), BF16),
            Near(shaped((rows, 2 * chans))),
            shaped((rows, chans)),
            shaped((groups, 3, CHUNKS, chans)),
            shaped((groups, CHUNKS, chans)),
            shaped((16, chans)),
            shaped(lags),
            *(shaped(shape, BF16) for shape in made),
        ],
        [pltpu.VMEM((3, CHUNKS, chans), F32)],
        vmem=36,
    )(me, layer, tokens, gain, *given)


def mix_body(
    steps,
    chans,
    blocks,
    me,
    keep,
    gathered,
    local,
    decays,
    prefix,
    angles,
    table,
    pre_out,
    tokens,
    w_out,
    out_gain,
    ffn_gain,
    states,
    entering,
    gated,
    mid,
    ffn_normed,
    full,
    carry,
):
    g, t = pl.program_id(0), pl.program_id(1)

    @pl.when(t == 0)
    def _():
        cos_dev, sin_dev = angles[DEVICE : DEVICE + 1, :], angles[DEVICE + 1 : DEVICE + 2, :]
        state_re = jnp.zeros((1, chans), F32)
        state_im = jnp.zeros((1, chans), F32)
        for d in range(blocks):
            kept_one = keep[g, d]
            turned_re, turned_im = turn(cos_dev, sin_dev, kept_one * state_re, kept_one * state_im)
            decay = gathered[d, 0, 0:1, :]
            earlier = d < me[0]
            state_re = jnp.where(earlier, decay * turned_re + gathered[d, 0, 1:2, :], state_re)
            state_im = jnp.where(earlier, decay * turned_im + gathered[d, 0, 2:3, :], state_im)
        kept_one = keep[g, me[0]]
        state_re, state_im = kept_one * state_re, kept_one * state_im
        cos_chunk, sin_chunk = angles[CHUNK : CHUNK + 1, :], angles[CHUNK + 1 : CHUNK + 2, :]
        for s in range(CHUNKS):
            run = prefix[0, 0, s : s + 1, :]
            entering[0, 0, s : s + 1, :] = run * state_re + prefix[0, 1, s : s + 1, :]
            entering[0, 1, s : s + 1, :] = run * state_im + prefix[0, 2, s : s + 1, :]
            state_re, state_im = turn(cos_chunk, sin_chunk, state_re, state_im)
        carry[...] = jnp.ones_like(carry)

    enter_re, enter_im = entering[0, 0], entering[0, 1]

    def step(j, prod):
        rows = step_rows(j)
        prod = prod * decays[rows, :]
        lag = pl.ds(t * steps + j + 1, 1)
        turned_re, turned_im = turn(table[lag, 0:chans], table[lag, chans:], enter_re, enter_im)
        full[rows, 0:chans] = local[rows, 0:chans] + prod * turned_re
        full[rows, chans:] = local[rows, chans:] + prod * turned_im
        return prod

    carry[...] = lax.fori_loop(0, steps, step, carry[...], unroll=8)
    state = full[...]
    states[...] = state.astype(BF16)
    inv_rms = rms_rows(state)
    gate = pre_out[...].astype(F32)
    gate_in = (state * out_gain[...] * (gate * sigmoid(gate))).astype(BF16)
    gated[...] = gate_in
    stream = tokens[...].astype(F32) + inv_rms * nn(gate_in, w_out[...])
    mid[...] = stream
    ffn_normed[...] = (stream * rms_rows(stream) * ffn_gain[...]).astype(BF16)


def mix(
    me, keep, gathered, local, decays, prefix, angles, table, pre_out, tokens, w, out_gain, ffn_gain, groups, chans
):
    rows, width = tokens.shape
    per = rows // groups
    tile = min(TILE, per)
    tiles = per // tile
    blocks = gathered.shape[0]
    rowed = functools.partial(ahead, tiles, tile)
    return kernel_call(
        functools.partial(mix_body, tile // CHUNKS, chans, blocks),
        (groups, tiles),
        [
            SMEM_SPEC,
            SMEM_SPEC,
            pl.BlockSpec((blocks, 1, CHUNKS, chans), lambda g, t: (0, g, 0, 0)),
            rowed(2 * chans),
            rowed(chans),
            per_group((1, 3, CHUNKS, chans)),
            whole(angles.shape),
            whole(table.shape),
            rowed(2 * chans),
            rowed(width),
            whole((2 * chans, width)),
            whole((1, 2 * chans)),
            whole((1, width)),
        ],
        [
            rowed(2 * chans),
            per_group((1, 2, CHUNKS, chans)),
            rowed(2 * chans),
            rowed(width),
            rowed(width),
        ],
        [
            shaped((rows, 2 * chans), BF16),
            shaped((groups, 2, CHUNKS, chans)),
            shaped((rows, 2 * chans), BF16),
            shaped((rows, width)),
            shaped((rows, width), BF16),
        ],
        [pltpu.VMEM((tile, 2 * chans), F32), pltpu.VMEM((CHUNKS, chans), F32)],
    )(me, keep, gathered, Near(local), decays, prefix, angles, table, pre_out, tokens, w, out_gain, ffn_gain)


def split_by_core(first, grads, span, unit, same, other):
    for chip in range(span // (2 * unit)):
        for k, part in enumerate(grads):
            even = part[2 * chip * unit : (2 * chip + 1) * unit]
            odd = part[(2 * chip + 1) * unit : (2 * chip + 2) * unit]
            rows = slice(k * unit, (k + 1) * unit)
            same[chip, rows, :] = jnp.where(first, even, odd)
            other[chip, rows, :] = jnp.where(first, odd, even)


def swiglu_body(unit, tile, x, up_all, w, act, d_pre, grads, w_out, up, arrival):
    devices = w.shape[0]
    fetch = pltpu.make_async_copy(up_all, up, arrival)

    @pl.when(pl.program_id(0) == 0)
    def _():
        fetch.start()

    def every(part):
        return jnp.concatenate([w[dev, part] for dev in range(devices)], axis=0)

    span = devices * unit
    w_pre = jnp.concatenate([every(0), every(1)], axis=0)
    w_down = every(2)
    w_out[...] = w_pre
    for start in range(0, x.shape[0], tile):
        rows = slice(start, start + tile)
        pre = nt(x[rows, :], w_pre)
        if start == 0:

            @pl.when(pl.program_id(0) == 0)
            def _():
                fetch.wait()

        d_hidden = nt(up[rows, :], w_down)
        gate, lift = pre[:, :span], pre[:, span:]
        sigma = sigmoid(gate)
        silu = gate * sigma
        act[rows, :] = (silu * lift).astype(BF16)
        d_pre[rows, :span] = (d_hidden * lift * (sigma + silu * (1.0 - sigma))).astype(BF16)
        d_pre[rows, span:] = (d_hidden * silu).astype(BF16)
    g_pre = tn(d_pre[...], x[...]).astype(BF16)
    g_down = tn(act[...], up[...]).astype(BF16)
    for dev in range(devices):
        own = slice(dev * unit, (dev + 1) * unit)
        grads[dev, 0:unit, :] = g_pre[own]
        grads[dev, unit : 2 * unit, :] = g_pre[span + dev * unit : span + (dev + 1) * unit]
        grads[dev, 2 * unit : 3 * unit, :] = g_down[own]


def units_at_once(blocks, unit):
    devices = 2
    while devices < blocks and (devices * unit % 128 or devices * unit < 384):
        devices *= 2
    return devices


def swiglu(x, up, w):
    rows, width = x.shape
    blocks, _, unit, _ = w.shape
    devices = units_at_once(blocks, unit)
    span = devices * unit
    return kernel_call(
        functools.partial(swiglu_body, unit, min(rows, 512)),
        (blocks // devices,),
        [
            whole((rows, width)),
            pl.BlockSpec(memory_space=pl.ANY),
            pl.BlockSpec((devices, 3, unit, width), lambda q: (q, 0, 0, 0)),
        ],
        [
            pl.BlockSpec((rows, span), lambda q: (0, q)),
            pl.BlockSpec((rows, 2 * span), lambda q: (0, q)),
            pl.BlockSpec((devices, 3 * unit, width), lambda q: (q, 0, 0)),
            pl.BlockSpec((2 * span, width), lambda q: (q, 0)),
        ],
        [
            shaped((rows, blocks * unit), BF16),
            shaped((rows, 2 * blocks * unit), BF16),
            shaped((blocks, 3 * unit, width), BF16),
            shaped((2 * blocks * unit, width), BF16),
        ],
        [pltpu.VMEM((rows, width), BF16), pltpu.SemaphoreType.DMA],
    )(x, up, w)


def finish_grads(core, grads, kinds, chans, unit, same, other):
    grads = [grad.astype(BF16) for grad in grads]
    if unit % 16:
        same[...] = jnp.concatenate(grads, axis=0)
        other[...] = jnp.zeros_like(other)
        return
    each = [grad[at : at + chans] for grad in grads for at in range(0, grad.shape[0], chans)]
    split_by_core(core[0] == 0, each, chans, unit, same, other)


def grads_shapes(kinds, chans, unit, width):
    if unit % 16:
        return [(kinds * chans, width), (16, width)]
    return [(chans // (2 * unit), kinds * unit, width)] * 2


def first_step():
    return jnp.logical_and(pl.program_id(0) == 0, pl.program_id(1) == 0)


def last_step():
    return jnp.logical_and(
        pl.program_id(0) == pl.num_programs(0) - 1, pl.program_id(1) == pl.num_programs(1) - 1
    )


def gain_share(grads, w, gain):
    return jnp.sum(grads * w[...].astype(F32), axis=0, keepdims=True) / gain[...]


def mix_back_body(
    steps,
    chans,
    unit_chans,
    core,
    d_pre,
    w_pre,
    mid,
    upstream,
    tokens,
    states,
    pre_out,
    gated,
    normed,
    decays,
    w_out,
    w_proj,
    mix_gain,
    out_gain,
    ffn_gain,
    angles,
    d_mid,
    d_outgate,
    local,
    suffix,
    totals,
    same,
    other,
    sums,
    d_mixes,
    d_gates,
    carry,
    gated_here,
    normed_here,
    w_here,
    arrivals,
):
    rows_here = steps * CHUNKS
    at = pl.program_id(0) * pl.num_programs(1) + pl.num_programs(1) - 1 - pl.program_id(1)
    here = pl.ds(pl.multiple_of(at * rows_here, rows_here), rows_here)

    fetches = [
        pltpu.make_async_copy(gated, gated_here, arrivals.at[0]),
        pltpu.make_async_copy(normed, normed_here, arrivals.at[1]),
        pltpu.make_async_copy(w_proj.at[pl.ds(0, 2 * chans)], w_here, arrivals.at[2]),
    ]

    @pl.when(first_step())
    def _():
        sums[...] = jnp.zeros_like(sums)
        for fetch in fetches:
            fetch.start()

    @pl.when(pl.program_id(1) == 0)
    def _():
        carry[0:2] = jnp.zeros((2,) + carry.shape[1:], F32)
        carry[2] = jnp.ones(carry.shape[1:], F32)

    d_norm = nn(d_pre[...], w_pre[...])
    stream = mid[...]
    inv_mid = rms_rows(stream)
    unit_mid = stream * inv_mid
    sums[0:1, :] += jnp.sum(d_norm * unit_mid, axis=0, keepdims=True)
    d_stream = upstream[...].astype(F32) + rms_pull(unit_mid, inv_mid, ffn_gain[...], d_norm)
    d_mid[...] = d_stream.astype(BF16)
    state = states[...].astype(F32)
    inv_rms = rms_rows(state)
    d_mix = (inv_rms * d_stream).astype(BF16)
    mixed = stream - tokens[...].astype(F32)
    d_square = (-0.5 / chans) * inv_rms * inv_rms * jnp.sum(d_stream * mixed, axis=-1, keepdims=True)
    d_gated = nt(d_mix, w_out[...])
    gate = pre_out[...].astype(F32)
    sigma = sigmoid(gate)
    silu = gate * sigma
    gain = out_gain[...]
    local[...] = d_gated * gain * silu + d_square * state
    d_state_gate = d_gated * state
    sums[1:2, :] += jnp.sum(d_state_gate * silu, axis=0, keepdims=True)
    d_gate = (d_state_gate * gain * (sigma + silu * (1.0 - sigma))).astype(BF16)
    d_outgate[...] = d_gate
    d_mixes[here, :] = d_mix
    d_gates[here, :] = d_gate
    cos_one, sin_one = angles[ONE : ONE + 1, :], angles[ONE + 1 : ONE + 2, :]

    def step(i, flow):
        flow_re, flow_im, prod = flow
        rows = step_rows(steps - 1 - i)
        grad_re = local[rows, 0:chans] + flow_re
        grad_im = local[rows, chans:] + flow_im
        local[rows, 0:chans] = grad_re
        local[rows, chans:] = grad_im
        decay = decays[rows, :]
        turned_re, turned_im = back_turn(cos_one, sin_one, grad_re, grad_im)
        return decay * turned_re, decay * turned_im, prod * decay

    end_re, end_im, prod = lax.fori_loop(
        0, steps, step, (carry[0], carry[1], carry[2]), unroll=8
    )
    carry[0], carry[1], carry[2] = end_re, end_im, prod

    @pl.when(pl.program_id(1) == pl.num_programs(1) - 1)
    def _():
        chain_chunks(reversed(range(CHUNKS)), back_turn, angles, prod, end_re, end_im, suffix, totals)

    @pl.when(last_step())
    def _():
        for fetch in fetches:
            fetch.wait()
        grads = [tn(gated_here[...], d_mixes[...]), tn(d_gates[...], normed_here[...])]
        sums[2:3, :] = gain_share(grads[1], w_here, mix_gain)
        finish_grads(core, grads, 4, chans, unit_chans, same, other)


def mix_back(
    core,
    unit_chans,
    d_pre,
    w_pre,
    mid,
    upstream,
    tokens,
    states,
    pre_out,
    gated,
    normed,
    decays,
    w,
    w_proj,
    mix_gain,
    out_gain,
    ffn_gain,
    angles,
    groups,
    chans,
):
    rows, width = mid.shape
    per = rows // groups
    tile = min(TILE, per)
    tiles = per // tile
    rowed = functools.partial(behind, tiles, tile)
    return kernel_call(
        functools.partial(mix_back_body, tile // CHUNKS, chans, unit_chans),
        (groups, tiles),
        [
            SMEM_SPEC,
            rowed(d_pre.shape[1]),
            whole(w_pre.shape),
            rowed(width),
            rowed(width),
            rowed(width),
            rowed(2 * chans),
            rowed(2 * chans),
            pl.BlockSpec(memory_space=pl.ANY),
            pl.BlockSpec(memory_space=pl.ANY),
            rowed(chans),
            whole((2 * chans, width)),
            pl.BlockSpec(memory_space=pl.ANY),
            whole((1, width)),
            whole((1, 2 * chans)),
            whole((1, width)),
            whole(angles.shape),
        ],
        [
            rowed(width),
            rowed(2 * chans),
            rowed(2 * chans),
            per_group((1, 3, CHUNKS, chans)),
            per_group((1, CHUNKS, chans)),
            *map(kept, grads_shapes(4, chans, unit_chans, width)),
            kept((8, width)),
        ],
        [
            shaped((rows, width), BF16),
            shaped((rows, 2 * chans), BF16),
            Near(shaped((rows, 2 * chans))),
            shaped((groups, 3, CHUNKS, chans)),
            shaped((groups, CHUNKS, chans)),
            *(shaped(shape, BF16) for shape in grads_shapes(4, chans, unit_chans, width)),
            shaped((8, width)),
        ],
        [
            pltpu.VMEM((rows, width), BF16),
            pltpu.VMEM((rows, 2 * chans), BF16),
            pltpu.VMEM((3, CHUNKS, chans), F32),
            pltpu.VMEM((rows, 2 * chans), BF16),
            pltpu.VMEM((rows, width), BF16),
            pltpu.VMEM((2 * chans, width), BF16),
            pltpu.SemaphoreType.DMA((3,)),
        ],
        vmem=42,
    )(
        core,
        d_pre,
        w_pre,
        mid,
        upstream,
        tokens,
        states,
        pre_out,
        gated,
        normed,
        decays,
        w,
        w_proj,
        mix_gain,
        out_gain,
        ffn_gain,
        angles,
    )


def silu_slope(values, sigma):
    return sigma * (1.0 + values * (1.0 - sigma))


def adjoint_finish_body(
    steps,
    chans,
    blocks,
    unit_chans,
    me,
    core,
    keep,
    gathered,
    local,
    decays,
    suffix,
    pre,
    states,
    before,
    entering,
    angles,
    table,
    normed,
    w_proj,
    mix_gain,
    early,
    d_pre,
    flat,
    same,
    other,
    leaving,
    full,
    d_pres,
    carry,
    sums,
    normed_here,
    w_here,
    arrivals,
):
    g, t = pl.program_id(0), pl.program_id(1)
    tiles = pl.num_programs(1)
    rows_here = steps * CHUNKS
    here = pl.ds(pl.multiple_of((g * tiles + tiles - 1 - t) * rows_here, rows_here), rows_here)
    fetches = [
        pltpu.make_async_copy(normed, normed_here, arrivals.at[0]),
        pltpu.make_async_copy(w_proj.at[pl.ds(2 * chans, 3 * chans)], w_here, arrivals.at[1]),
    ]

    @pl.when(first_step())
    def _():
        sums[...] = jnp.zeros_like(sums)
        for fetch in fetches:
            fetch.start()

    @pl.when(t == 0)
    def _():
        cos_chunk, sin_chunk = angles[CHUNK : CHUNK + 1, :], angles[CHUNK + 1 : CHUNK + 2, :]
        cos_dev, sin_dev = angles[DEVICE : DEVICE + 1, :], angles[DEVICE + 1 : DEVICE + 2, :]
        flow_re = jnp.zeros((1, chans), F32)
        flow_im = jnp.zeros((1, chans), F32)
        for d in reversed(range(blocks)):
            kept_one = keep[g, d]
            turned_re, turned_im = back_turn(cos_dev, sin_dev, flow_re, flow_im)
            decay = gathered[d, 0, 0:1, :]
            later = d > me[0]
            flow_re = jnp.where(
                later, kept_one * (decay * turned_re + gathered[d, 0, 1:2, :]), flow_re
            )
            flow_im = jnp.where(
                later, kept_one * (decay * turned_im + gathered[d, 0, 2:3, :]), flow_im
            )
        for s in reversed(range(CHUNKS)):
            run = suffix[0, 0, s : s + 1, :]
            leaving[0, s : s + 1, :] = run * flow_re + suffix[0, 1, s : s + 1, :]
            leaving[1, s : s + 1, :] = run * flow_im + suffix[0, 2, s : s + 1, :]
            flow_re, flow_im = back_turn(cos_chunk, sin_chunk, flow_re, flow_im)
        carry[...] = jnp.ones_like(carry)

    low = angles[BOUND : BOUND + 1, :]
    cos_one, sin_one = angles[ONE : ONE + 1, :], angles[ONE + 1 : ONE + 2, :]
    leave_re, leave_im = leaving[0], leaving[1]

    def step(i, prod):
        rows = step_rows(steps - 1 - i)
        lag = pl.ds(t * steps + i, 1)
        turned_re, turned_im = back_turn(table[lag, 0:chans], table[lag, chans:], leave_re, leave_im)
        full[rows, 0:chans] = local[rows, 0:chans] + prod * turned_re
        full[rows, chans:] = local[rows, chans:] + prod * turned_im
        return prod * decays[rows, :]

    carry[...] = lax.fori_loop(0, steps, step, carry[...], unroll=8)
    first_tile = t == tiles - 1
    last = before[...].astype(F32)[CHUNKS:]
    last_re = jnp.where(first_tile, entering[0, 0], last[:, 0:chans])
    last_im = jnp.where(first_tile, entering[0, 1], last[:, chans:])
    state = states[...].astype(F32)[: (steps - 1) * CHUNKS]
    last_re = jnp.concatenate([last_re, state[:, 0:chans]], axis=0)
    last_im = jnp.concatenate([last_im, state[:, chans:]], axis=0)
    grad_re, grad_im = full[:, 0:chans], full[:, chans:]
    scan = pre[...].astype(F32)
    in_re, in_im = scan[:, 0:chans], scan[:, chans : 2 * chans]
    sigma_re, sigma_im = sigmoid(in_re), sigmoid(in_im)
    sigma = sigmoid(scan[:, 2 * chans :])
    decay = decays[...]
    cross_re = grad_re * last_re + grad_im * last_im
    cross_im = grad_im * last_re - grad_re * last_im
    along, across = back_turn(cos_one, sin_one, cross_re, cross_im)
    d_decay = along - (grad_re * in_re * sigma_re + grad_im * in_im * sigma_im)
    rest = 1.0 - decay
    d_low = d_decay * (1.0 - sigma)
    d_re = (grad_re * rest * silu_slope(in_re, sigma_re)).astype(BF16)
    d_im = (grad_im * rest * silu_slope(in_im, sigma_im)).astype(BF16)
    d_forget = (d_low * (1.0 - low) * sigma).astype(BF16)
    d_all = jnp.concatenate([d_re, d_im, d_forget], axis=1)
    d_pre[...] = d_all
    d_pres[here, :] = d_all
    sums[0] += jnp.sum((decay * across).reshape(steps, CHUNKS, chans), axis=0)
    sums[1] += jnp.sum(d_low.reshape(steps, CHUNKS, chans), axis=0)

    @pl.when(last_step())
    def _():
        for fetch in fetches:
            fetch.wait()
        grads = tn(d_pres[...], normed_here[...])
        finish_grads(core, [grads], 3, chans, unit_chans, same, other)
        flat[...] = jnp.zeros_like(flat)
        flat[0:1, :] = early[2:3, :] + gain_share(grads, w_here, mix_gain)
        flat[1:3, :] = early[0:2, :]
        flat[3:4, 0:chans] = jnp.sum(sums[0], axis=0, keepdims=True)
        flat[3:4, chans:] = jnp.sum(sums[1], axis=0, keepdims=True)


def adjoint_finish(
    unit_chans,
    me,
    core,
    keep,
    gathered,
    local,
    decays,
    suffix,
    pre,
    states,
    entering,
    angles,
    table,
    normed,
    w_proj,
    mix_gain,
    early,
    groups,
    chans,
):
    rows, width = normed.shape
    per = rows // groups
    tile = min(TILE, per)
    tiles = per // tile
    steps = tile // CHUNKS
    blocks = gathered.shape[0]
    rowed = functools.partial(behind, tiles, tile)

    def one_before(g, t):
        return (jnp.maximum((g * tiles + tiles - 1 - t) * (steps // 2) - 1, 0), 0)

    return kernel_call(
        functools.partial(adjoint_finish_body, steps, chans, blocks, unit_chans),
        (groups, tiles),
        [
            SMEM_SPEC,
            SMEM_SPEC,
            SMEM_SPEC,
            pl.BlockSpec((blocks, 1, CHUNKS, chans), lambda g, t: (0, g, 0, 0)),
            rowed(2 * chans),
            rowed(chans),
            per_group((1, 3, CHUNKS, chans)),
            rowed(3 * chans),
            rowed(2 * chans),
            pl.BlockSpec((2 * CHUNKS, 2 * chans), one_before),
            per_group((1, 2, CHUNKS, chans)),
            whole(angles.shape),
            whole(table.shape),
            pl.BlockSpec(memory_space=pl.ANY),
            pl.BlockSpec(memory_space=pl.ANY),
            whole((1, width)),
            whole(early.shape),
        ],
        [
            rowed(3 * chans),
            kept((8, width)),
            *map(kept, grads_shapes(3, chans, unit_chans, width)),
        ],
        [
            shaped((rows, 3 * chans), BF16),
            shaped((8, width)),
            *(shaped(shape, BF16) for shape in grads_shapes(3, chans, unit_chans, width)),
        ],
        [
            pltpu.VMEM((2, CHUNKS, chans), F32),
            pltpu.VMEM((tile, 2 * chans), F32),
            pltpu.VMEM((rows, 3 * chans), BF16),
            pltpu.VMEM((CHUNKS, chans), F32),
            pltpu.VMEM((2, CHUNKS, chans), F32),
            pltpu.VMEM((rows, width), BF16),
            pltpu.VMEM((3 * chans, width), BF16),
            pltpu.SemaphoreType.DMA((2,)),
        ],
    )(
        me,
        core,
        keep,
        gathered,
        Near(local),
        decays,
        suffix,
        pre,
        states,
        states,
        entering,
        angles,
        table,
        normed,
        w_proj,
        mix_gain,
        early,
    )


def tokens_back_body(chans, d_scan, d_outgate, w, tokens, d_mid, gain, grad_tokens):
    d_normed = nn(d_scan[...], w[2 * chans : 5 * chans, :])
    d_normed += nn(d_outgate[...], w[0 : 2 * chans, :])
    values = tokens[...].astype(F32)
    inv = rms_rows(values)
    grad_tokens[...] = (
        d_mid[...].astype(F32) + rms_pull(values * inv, inv, gain[...], d_normed)
    ).astype(BF16)


def tokens_back(d_scan, d_outgate, w, tokens, d_mid, gain, groups, chans):
    rows, width = tokens.shape
    per = rows // groups
    tile = min(TILE, per)
    tiles = per // tile
    rowed = functools.partial(ahead, tiles, tile)
    return kernel_call(
        functools.partial(tokens_back_body, chans),
        (groups, tiles),
        [
            rowed(3 * chans),
            rowed(2 * chans),
            whole(w.shape),
            rowed(width),
            rowed(width),
            whole((1, width)),
        ],
        rowed(width),
        Near(shaped((rows, width), BF16)),
        vmem=20,
    )(d_scan, d_outgate, w, tokens, d_mid, gain)


def result_body(act, w_down, mid, result):
    blocks = w_down.shape[0]
    down = jnp.concatenate([w_down[dev, 0] for dev in range(blocks)], axis=0)
    result[...] = (mid[...] + nn(act[...], down)).astype(BF16)


def block_result(act, w_ffn, mid):
    rows, width = mid.shape
    blocks, _, units, _ = w_ffn.shape
    tile = min(TILE, rows)

    def rowed(wide):
        return pl.BlockSpec((tile, wide), lambda i: (i, 0))

    return kernel_call(
        result_body,
        (rows // tile,),
        [rowed(act.shape[1]), whole((blocks, 1, units, width), (0, 2, 0, 0)), rowed(width)],
        rowed(width),
        Near(shaped((rows, width), BF16)),
        vmem=20,
    )(act, w_ffn, mid)


def unpack_body(ffn, gate, up, down):
    rows = gate.shape[0]
    for k, out in enumerate((gate, up, down)):
        out[...] = ffn[k * rows : (k + 1) * rows, :].astype(F32)


def unpack(ffn):
    rows, width = ffn.shape[0] // 3, ffn.shape[1]
    return kernel_call(
        unpack_body,
        (1,),
        [whole(ffn.shape)],
        [whole((rows, width))] * 3,
        [shaped((rows, width))] * 3,
        vmem=16,
    )(ffn)


def swap(values, axis, bit, size):
    return lax.ppermute(values, axis, [(i, i ^ bit) for i in range(size)])


def joined(*parts):
    return sum(part.astype(F32) for part in parts)


def pick(values, index, axis):
    return lax.dynamic_index_in_dim(values, index, axis, keepdims=False)


def gather_pieces(shard, size, *others):
    half = shard.shape[0] // 32 * 16
    near_x = swap(shard, "mp", 2, size)
    near_y = swap(shard, "mp", 4, size)
    core = swap(shard, "mp", 1, size)
    near_x, near_y, *others = tied(near_x, near_y, *others)
    far_one = swap(near_x[:half], "mp", 4, size)
    far_two = swap(near_y[half:], "mp", 2, size)
    core_x = swap(near_x, "mp", 1, size)
    core_y = swap(near_y, "mp", 1, size)
    far = jnp.concatenate([far_one, far_two], axis=0)
    core_far = swap(far, "mp", 1, size)
    return [shard, core, near_x, core_x, near_y, core_y, far, core_far], *others


def reduce_mp(grads):
    return lax.psum_scatter(grads, "mp", scatter_dimension=0, tiled=False)


def sends_body(chip, same, got, out_x, out_y, out_far):
    for b, out in ((1, out_x), (2, out_y), (3, out_far)):
        at = chip[0] ^ b
        out[...] = (same[at].astype(F32) + got[at].astype(F32)).astype(BF16)


def sends(chip, same, got):
    return pl.pallas_call(
        sends_body,
        in_specs=[SMEM_SPEC, VMEM_SPEC, VMEM_SPEC],
        out_specs=[VMEM_SPEC] * 3,
        out_shape=[jax.ShapeDtypeStruct(same.shape[1:], BF16)] * 3,
        cost_estimate=pl.CostEstimate(flops=1, bytes_accessed=1, transcendentals=0),
        compiler_params=pltpu.CompilerParams(vmem_limit_bytes=16 * MIB),
    )(chip, same, got)


def last_sums(finish, from_rows, order, size, layers, flat, chip, same, got, early, early_got, tokens):
    last = Reduction(same, None, chip, size, layers)
    last.flying = [got]
    early = both(early, early_got)
    early_got = along_layers(2, early)
    flat = flat + swap(flat, "mp", 2 * order[0], size)
    flat, tokens = tied(last.to_chips(flat), tokens)
    flat = flat + swap(flat, "mp", 2 * order[1], size)
    moved = from_rows(tokens)
    late, flat, moved, early_got = tied(last.share_here(), flat, moved, early_got)
    one, two, three = (swap(late, "dp", bit, layers) for bit in (1, 2, 3))
    early = both(early, early_got)
    early_got = along_layers(3, early)
    flat = flat + swap(flat, "mp", 1, size)
    late = joined(joined(late, one), joined(two, three))
    early = settled(early, early_got).reshape(2, 2, -1, early.shape[-1])
    return (*finish(flat, late), moved, early[0], early[1])


class Reduction:
    def __init__(self, same, other, chip, size, layers):
        self.same, self.chip, self.size, self.layers = same, chip, size, layers
        self.flying = [] if other is None else [swap(other, "mp", 1, size)]

    def arrived(self, *others):
        count = len(self.flying)
        both = tied(*self.flying, *others)
        self.flying = both[:count]
        return both[count:] if len(others) > 1 else both[-1]

    def to_chips(self, other):
        self.got = self.flying[0]
        *parts, other = tied(*sends(self.chip, self.same, self.got), other)
        self.flying = [swap(part, "mp", 2 * b, self.size) for b, part in zip((1, 2, 3), parts)]
        return other

    def share_here(self):
        at = self.chip[0]
        mine = pick(self.same, at, 0), pick(self.got, at, 0)
        return joined(*mine, *self.flying).astype(BF16)


def along_layers(number, share):
    pairs = {1: [(0, 1), (3, 2)], 2: [(1, 2), (2, 1)], 3: [(1, 0), (2, 3)]}[number]
    return lax.ppermute(share, "dp", pairs)


def both(share, got):
    return joined(share, got).astype(BF16)


def settled(share, got):
    z = lax.axis_index("dp")
    inner = jnp.logical_or(z == 1, z == 2)
    return jnp.where(inner, share, got).astype(F32)


def split_three(values):
    one = lax.reduce_precision(values, 8, 7)
    two = lax.reduce_precision(values - one, 8, 7)
    three = values - one - two
    return jnp.stack([one, two, three], axis=0).astype(BF16)


def tied(*values):
    return lax.optimization_barrier(values)


def shards(
    tokens,
    upstream,
    pieces,
    layer_index,
    mix_gain,
    w_input,
    w_forget,
    w_outgate,
    phase_angle,
    lower_logits,
    out_gain,
    w_output,
    ffn_gain,
    w_gate,
    w_up,
    w_down,
):
    rows_dev, groups, width = tokens.shape
    blocks = lax.axis_size("mp")
    me = lax.axis_index("mp")
    layers_z = lax.axis_size("dp")
    seq_len = rows_dev * blocks
    chans_dev = w_input.shape[2]
    chans = chans_dev * blocks
    units_dev = w_gate.shape[1]
    units = units_dev * blocks
    steps = rows_dev // CHUNKS
    rows = rows_dev * groups

    def to_rows(values):
        return jnp.transpose(
            values.reshape(CHUNKS, steps, groups, width), (2, 1, 0, 3)
        ).reshape(rows, width)

    def from_rows(values):
        return jnp.transpose(
            values.reshape(groups, steps, CHUNKS, width), (2, 1, 0, 3)
        ).reshape(rows_dev, groups, width)

    me_one = me[None].astype(jnp.int32)
    rows_own = channel_rows(lower_logits, phase_angle, out_gain)
    kinds = rows_own.shape[0]
    by_hand = blocks == 8 and layers_z == 4 and chans_dev % 16 == 0
    mix_shard = jnp.concatenate(
        [
            jnp.transpose(w_outgate, (1, 2, 0)),
            jnp.transpose(w_input, (1, 2, 0)),
            jnp.transpose(w_forget)[None],
            w_output,
        ],
        axis=0,
    )
    ffn_parts = jnp.transpose(w_gate), jnp.transpose(w_up), w_down
    tok, up_rows = to_rows(tokens), to_rows(upstream)
    pieces_w, w_proj, rows_all = [], None, None
    if by_hand:
        terms = split_three(rows_own).reshape(3 * kinds, chans_dev)
        spare = (3 * kinds + 15) // 16 * 16
        terms = jnp.pad(terms, ((0, spare - 3 * kinds), (0, width - chans_dev)))
        own = jnp.concatenate([mix_shard.reshape(7 * chans_dev, width), terms], axis=0)
        own, *ffn_parts = tied(own, *ffn_parts)
        pieces_w, tok, up_rows = gather_pieces(own, blocks, tok, up_rows)
    else:
        w_mix = lax.all_gather(mix_shard, "mp", axis=0)
        w_mix = jnp.transpose(w_mix, (1, 0, 2, 3)).reshape(7 * chans, width)
        w_proj, w_out = w_mix[: 5 * chans], w_mix[5 * chans :]
        rows_all = lax.all_gather(rows_own, "mp", axis=0)
        rows_all = jnp.transpose(rows_all, (1, 0, 2)).reshape(kinds, chans)
    w_ffn = lax.all_gather(jnp.concatenate(ffn_parts, axis=0), "mp", axis=0)
    starts = jnp.arange(blocks, dtype=jnp.int32) * rows_dev
    keep = (starts[None, :] % (seq_len // pieces)[:, None] != 0).astype(F32)

    mix_row, ffn_row = mix_gain[None], ffn_gain[None]
    normed, pre, pre_out, local, decays, prefix, totals, angles, lags, *made = project(
        me_one, layer_index, tok, mix_row, pieces_w, kinds, w_proj, rows_all, groups, chans
    )
    if by_hand:
        w_proj, w_out = made[0].reshape(5 * chans, width), made[1].reshape(2 * chans, width)
    gain_row = angles[GAIN : GAIN + 2].reshape(1, 2 * chans)
    ends = lax.all_gather(totals, "mp", axis=0)
    states, entering, gated, mid, ffn_normed = mix(
        me_one,
        keep,
        ends,
        local,
        decays,
        prefix,
        angles,
        lags,
        pre_out,
        tok,
        w_out,
        gain_row,
        ffn_row,
        groups,
        chans,
    )
    core = (me & 1) if by_hand else jnp.zeros_like(me)
    core_one = core[None].astype(jnp.int32)
    chip_one = (me >> 1)[None].astype(jnp.int32)
    w_ffn = w_ffn.reshape(blocks, 3, units_dev, width)

    def reduction(same, other):
        return Reduction(same, other, chip_one, blocks, layers_z)

    act, d_pre, grad_ffn, w_pre = swiglu(ffn_normed, up_rows, w_ffn)
    grad_ffn = reduce_mp(grad_ffn)
    d_mid, d_outgate, back_local, suffix, back_totals, same, other, early_sums = mix_back(
        core_one,
        chans_dev,
        d_pre,
        w_pre,
        mid,
        up_rows,
        tok,
        states,
        pre_out,
        gated,
        normed,
        decays,
        w_out,
        w_proj,
        mix_row,
        gain_row,
        ffn_row,
        angles,
        groups,
        chans,
    )
    if by_hand:
        early = reduction(same, other)
    else:
        early = jnp.moveaxis(same.reshape(4, blocks, chans_dev, width), 1, 0)
    back_ends = lax.all_gather(back_totals, "mp", axis=0)
    if by_hand:
        back_ends = early.to_chips(early.arrived(back_ends))
        mid, back_ends = tied(mid, back_ends)
    out_result = from_rows(block_result(act, w_ffn, mid))
    if by_hand:
        back_ends, out_result = tied(back_ends, out_result)
    d_scan, flat, same, other = adjoint_finish(
        chans_dev,
        me_one,
        core_one,
        keep,
        back_ends,
        back_local,
        decays,
        suffix,
        pre,
        states,
        entering,
        angles,
        lags,
        normed,
        w_proj,
        mix_row,
        early_sums,
        groups,
        chans,
    )
    if by_hand:
        other, d_scan = early.arrived(other, d_scan)
        late = reduction(same, other)
        early_share, d_scan = tied(early.share_here(), d_scan)
        early_got = along_layers(1, early_share)
    else:
        late = jnp.moveaxis(same.reshape(3, blocks, chans_dev, width), 1, 0)
    def finish(flat, late):
        late = late.reshape(3, chans_dev, width)
        own = me * chans_dev

        def own_part(row, offset):
            return lax.dynamic_slice(flat, (row, offset * chans + own), (1, chans_dev))[0]

        grad_gain = jnp.stack([own_part(2, 0), own_part(2, 1)], axis=0)
        below = jnp.arange(lower_logits.shape[0], dtype=jnp.int32) < layer_index[0]
        below = below.astype(F32)[:, None]
        soft = jax.nn.softmax(lower_logits, axis=0)
        bound_own = jnp.sum(soft * below, axis=0, keepdims=True)
        return (
            flat[0],
            jnp.transpose(late[0:2], (2, 0, 1)),
            jnp.transpose(late[2]),
            own_part(3, 0),
            soft * (below - bound_own) * own_part(3, 1)[None],
            grad_gain,
            flat[1],
        )

    if by_hand:
        one, two, three = (swap(flat, "dp", bit, layers_z) for bit in (1, 2, 3))
    grad_tokens = tokens_back(d_scan, d_outgate, w_proj, tok, d_mid, mix_row, groups, chans)
    if by_hand:
        grad_tokens, one, two, three = tied(grad_tokens, one, two, three)
        flat, early_got = tied((flat + one) + (two + three), early_got)
        flat, grad_tokens, grad_ffn = late.arrived(flat, grad_tokens, grad_ffn)
        same, got = late.same, late.flying[0]
        finished = lax.cond(
            layer_index[0] > 0,
            functools.partial(last_sums, finish, from_rows, (1, 2), blocks, layers_z),
            functools.partial(last_sums, finish, from_rows, (2, 1), blocks, layers_z),
            flat,
            chip_one,
            same,
            got,
            early_share,
            early_got,
            grad_tokens,
        )
    else:
        early = lax.psum(reduce_mp(early.reshape(blocks, -1, width)), "dp").astype(F32)
        late = lax.psum(reduce_mp(late.reshape(blocks, -1, width)), "dp").astype(F32)
        flat = lax.psum(flat, ("dp", "mp"))
    grad_ffn = lax.psum(grad_ffn.reshape(3 * units_dev, width), "dp")
    if by_hand:
        *finished, grad_ffn = tied(*finished, grad_ffn)
        *finished, g_output, g_outgate = finished
        g_gate, g_up, g_down = unpack(grad_ffn)
    else:
        finished = finish(flat, late)
        g_gate, g_up, g_down = grad_ffn.astype(F32).reshape(3, units_dev, width)
        g_output, g_outgate = early.reshape(2, 2, chans_dev, width)
    gain_mix, g_input, g_forget, g_phase, g_lower, g_gain, gain_ffn, *moved = finished
    out_tokens = moved[0] if moved else from_rows(grad_tokens)
    return (
        out_result,
        out_tokens,
        gain_mix,
        g_input,
        g_forget,
        jnp.transpose(g_outgate, (2, 0, 1)),
        g_phase,
        g_lower,
        g_gain,
        g_output,
        gain_ffn,
        jnp.transpose(g_gate),
        jnp.transpose(g_up),
        g_down,
    )


def solution(mesh):
    in_specs = (
        P("mp", "dp", None),
        P("mp", "dp", None),
        P("dp"),
        P(),
        P(),
        P(None, None, "mp"),
        P(None, "mp"),
        P(None, None, "mp"),
        P("mp"),
        P(None, "mp"),
        P(None, "mp"),
        P(None, "mp", None),
        P(),
        P(None, "mp"),
        P(None, "mp"),
        P("mp", None),
    )
    out_specs = (
        P("mp", "dp", None),
        P("mp", "dp", None),
        P(),
        P(None, None, "mp"),
        P(None, "mp"),
        P(None, None, "mp"),
        P("mp"),
        P(None, "mp"),
        P(None, "mp"),
        P(None, "mp", None),
        P(),
        P(None, "mp"),
        P(None, "mp"),
        P("mp", None),
    )
    return jax.shard_map(shards, mesh=mesh, in_specs=in_specs, out_specs=out_specs, check_vma=False)
```
